768 devices in a mesh: sec: 4 (over x), tile: 24 (over z, core), lev: 8 (over y).
Axes of the slice: x: 4, y: 8, z: 12, core: 2. Of those that a mesh axis runs over, the one named last changes fastest.
Arguments:
- atmos_profile_state: bfloat16 [4, 72, 786432], P(None, None, ('sec', 'tile', 'lev')), may hold values from -6 to 6
- previous_surface_temp: float32 [786432], P(('sec', 'tile', 'lev')), may hold values from -4 to 4
- outbound_block_index: int32 [18432, 2], P(('sec', 'tile', 'lev')), may hold values from 0 to 7
- outbound_slot_counts: int32 [768, 24], P(('sec', 'tile', 'lev')), may hold values from 1 to 2, as said below
- pair_source_slot: int32 [6144, 4], P(('sec', 'tile', 'lev')), may hold values from 0 to 47, as said below
- overlay_weight: bfloat16 [6144, 4, 128, 128], P(('sec', 'tile', 'lev')), may hold values from 0 to 0.00390625
- ocean_tracer_state: float32 [2, 80, 768, 1024], P(None, None, ('sec', 'tile'), 'lev'), may hold values from -6 to 6
- ocean_cell_mask: int32 [768, 1024], P(('sec', 'tile'), 'lev'), may hold values 0 or 1
Outputs:
- ocean_output_tracers: float32 [2, 80, 768, 1024], P(None, None, ('sec', 'tile'), 'lev')
- surface_temp_columns: float32 [786432], P(('sec', 'tile', 'lev'))
The draws below stay inside these ranges and needn't reach their ends.
Inputs may be any that keep to these rules, and one draw needn't show every extreme that they name: `outbound_block_index`: entries j of a row at or beyond the row's live count in outbound_slot_counts are unused padding. outbound_slot_counts[d, p] is the number of live slots, the first ones, among the 2 slots from device d to the peer of tile index p; every device has some peer with all 2 slots live. `pair_source_slot`: an entry t * 2 + j names slot j from the device of tile index t in the receiver's sec and lev; j is below that sender's outbound_slot_counts entry for the receiver.
All inputs are finite; a program needn't handle non-finite values. No bound on the sum of `ocean_cell_mask` on one device may be relied on, other than what follows from the above.
Results may differ from the reference program's by a relative error of at most 0.0003.
Values sent between devices are 32-bit elements; how exact they have to be, the bound alone decides.
No kernel may reach another device: no remote copies, remote signals or barrier semaphores. Data moves between devices by JAX's collectives and lax.ppermute only.
A program may use at most 32 MiB of HBM per device.

```python
from functools import partial
import jax
import jax.numpy as jnp
from jax import lax

LEV_A = 72
LEV_O = 80
BLK = 128
K = 4
SLOT = 2
AB = 8
OB = 8
ATMOS_COLUMNS = 786432
OX = 768
OY = 1024
N_SEC = 4
N_TILE = 24
N_LEV = 8
DEVICES = 768


def count_table(key):
    device_count = N_SEC * N_TILE * N_LEV
    base_counts = jax.random.randint(jax.random.fold_in(key, 11), (device_count, N_TILE), 1, SLOT + 1)
    chosen = jax.random.randint(jax.random.fold_in(key, 12), (device_count, 1), 0, N_TILE)
    peer_index = jnp.arange(N_TILE, dtype=jnp.int32)[None, :]
    return jnp.where(peer_index == chosen, SLOT, base_counts).astype(jnp.int32)


def draw_outbound_slot_counts(key, part):
    return count_table(key)


def draw_pair_source_slot(key, part):
    counts = count_table(key)
    key = jax.random.fold_in(key, 3)
    device_count = N_SEC * N_TILE * N_LEV
    incoming = counts.reshape(N_SEC, N_TILE, N_LEV, N_TILE).transpose(0, 3, 2, 1).reshape(device_count, N_TILE)
    sender = jax.random.randint(jax.random.fold_in(key, 1), (device_count, OB * K), 0, N_TILE)
    live_here = jnp.take_along_axis(incoming, sender, axis=1)
    offset = jax.random.randint(jax.random.fold_in(key, 2), (device_count, OB * K), 0, 65536) % live_here
    return (sender * SLOT + offset).reshape(device_count * OB, K).astype(jnp.int32)


def touch_ends(values, rng, least, largest):
    spot = [jax.random.randint(jax.random.fold_in(rng, axis), (), 0, length) for axis, length in enumerate(values.shape)]
    main_axis = values.shape.index(max(values.shape))
    next_to = spot[:main_axis] + [(spot[main_axis] + 1) % values.shape[main_axis]] + spot[main_axis + 1:]
    return values.at[tuple(spot)].set(least).at[tuple(next_to)].set(largest)


def steps_of(stream_key, dims, cuts, smallest, largest):
    factor_of = 1.0
    for axis_at, shards_of in cuts:
        heights = jax.random.uniform(jax.random.fold_in(jax.random.fold_in(stream_key, 6), axis_at), (shards_of,), jnp.float32, smallest / len(cuts), largest / len(cuts))
        factor_of = factor_of * jnp.repeat(jnp.exp(heights), dims[axis_at] // shards_of).reshape((-1,) + (1,) * (len(dims) - 1 - axis_at))
    return factor_of


def centred(stream_key, shape, deviation, bound, shards=(), kind=jnp.bfloat16):
    values = jax.random.normal(stream_key, shape, jnp.float32) * deviation
    if len(shards) > 0:
        values = steps_of(stream_key, shape, shards, -0.22, 0.18) * values
    return jnp.clip(values, min=-bound, max=bound).astype(kind)


def setup_inputs(seed: int = 0) -> dict:
    arg_keys = jax.random.split(jax.random.key(seed), 9)
    return {
        "atmos_profile_state": centred(arg_keys[0], (4, LEV_A, ATMOS_COLUMNS), 1.0, 6.0, ((2, 768),)),
        "previous_surface_temp": centred(arg_keys[1], (ATMOS_COLUMNS,), 1.0, 4.0, ((0, 768),), jnp.float32),
        "outbound_block_index": touch_ends(jax.random.randint(arg_keys[2], (DEVICES * N_TILE, SLOT), 0, AB), jax.random.fold_in(arg_keys[2], 1), 0, AB - 1).astype(jnp.int32),
        "outbound_slot_counts": draw_outbound_slot_counts(jax.random.fold_in(arg_keys[8], 71), 0),
        "pair_source_slot": draw_pair_source_slot(jax.random.fold_in(arg_keys[8], 71), 0),
        "overlay_weight": jnp.clip(0.00390625 * jax.random.uniform(arg_keys[5], (DEVICES * OB, K, BLK, BLK), jnp.float32) ** steps_of(arg_keys[5], (DEVICES * OB, K, BLK, BLK), ((0, 768),), -0.2, 0.2), 0.0, 0.00390625).astype(jnp.bfloat16),
        "ocean_tracer_state": centred(arg_keys[6], (2, LEV_O, OX, OY), 1.0, 6.0, ((2, 96), (3, 8)), jnp.float32),
        "ocean_cell_mask": touch_ends((jax.random.randint(arg_keys[7], (OX, OY), 0, 4) < 3).astype(jnp.int32), jax.random.fold_in(arg_keys[7], 1), 0, 1),
    }


FULL_PRECISION = lax.Precision.HIGHEST
DIFFUSION_RATE = 0.15

def level_table(levels):
    level_index = jnp.arange(levels).astype(jnp.float32)
    bottom = jnp.exp(-level_index / 3.0)
    radiative = jnp.exp(-level_index / 24.0)
    return jnp.stack([bottom / jnp.sum(bottom), radiative / jnp.sum(radiative)], axis=1)

def compute_surface_flux(atmos_profile_state, previous_surface_temp):
    lookup_table = level_table(atmos_profile_state.shape[1])
    sums_by_level = jnp.einsum('oif,ia->oaf', atmos_profile_state.astype(jnp.float32), lookup_table, precision=FULL_PRECISION)
    wind_east = sums_by_level[2, 0]
    wind_north = sums_by_level[3, 0]
    wind_magnitude = jnp.sqrt(wind_east * wind_east + wind_north * wind_north + 1.0)
    sensible_heat = 0.3 * wind_magnitude * (sums_by_level[0, 0] - previous_surface_temp) + 0.5 * sums_by_level[0, 1]
    evaporative_loss = 0.3 * wind_magnitude * (jnp.exp(0.2 * previous_surface_temp) - 1.0 - sums_by_level[1, 0])
    stress_east = 0.1 * wind_magnitude * wind_east
    stress_north = 0.1 * wind_magnitude * wind_north
    return jnp.stack([sensible_heat, evaporative_loss, stress_east, stress_north])

def substep(tracers, wet_rim, forcing, levels):
    center = tracers[:, 1:-1, 1:-1]
    wet_centre = wet_rim[1:-1, 1:-1]
    laplace = wet_rim[2:, 1:-1] * (tracers[:, 2:, 1:-1] - center) + wet_rim[:-2, 1:-1] * (tracers[:, :-2, 1:-1] - center) + wet_rim[1:-1, 2:] * (tracers[:, 1:-1, 2:] - center) + wet_rim[1:-1, :-2] * (tracers[:, 1:-1, :-2] - center)
    stress = jnp.sqrt(forcing[2] * forcing[2] + forcing[3] * forcing[3])
    mixing = stress / (1.0 + stress)
    decay = jnp.exp(-jnp.arange(levels - 1).astype(jnp.float32) / 8.0)
    mix_rate = 0.05 + 0.15 * decay[:, None, None] * mixing[None]
    rows_here = center.shape[1]
    cells_here = center.shape[2]
    tracer = center.reshape(2, levels, rows_here, cells_here)
    vert_flow = mix_rate[None] * (tracer[:, 1:] - tracer[:, :-1])
    zero_rim = jnp.zeros((2, 1, rows_here, cells_here), tracer.dtype)
    vertical = jnp.concatenate([vert_flow, zero_rim], axis=1) - jnp.concatenate([zero_rim, vert_flow], axis=1)
    surface = jnp.concatenate([0.5 * forcing[:2][:, None], jnp.zeros((2, levels - 1, rows_here, cells_here), tracer.dtype)], axis=1)
    updated = tracer + wet_centre * (DIFFUSION_RATE * laplace.reshape(tracer.shape) + vertical + surface)
    return updated.reshape(center.shape)

def remap_inward(weight, picked):
    return jnp.einsum('okab,okfb->foa', weight.astype(jnp.float32), picked, precision=FULL_PRECISION)

def remap_outward(weight, sea_surface, pair_slots, total_slots):
    widened = weight.astype(jnp.float32)
    weighted = jnp.einsum('okab,oa->okb', widened, sea_surface, precision=FULL_PRECISION)
    coverage = lax.optimization_barrier(jnp.sum(widened, axis=2))
    terms = jnp.stack([weighted, coverage], axis=2).reshape(-1, 2 * widened.shape[3])
    selector = (pair_slots.reshape(-1)[:, None] == jnp.arange(total_slots)[None, :]).astype(jnp.float32)
    return jnp.dot(selector.T, terms, precision=FULL_PRECISION)

def collect_returns(returned, sender_ids, live_counts, atmos_column_blocks):
    slot_count = sender_ids.shape[1]
    live = jnp.arange(slot_count)[None, :] < live_counts[:, None]
    onehot = ((sender_ids[:, :, None] == jnp.arange(atmos_column_blocks)[None, None, :]) & live[:, :, None]).astype(jnp.float32)
    return jnp.dot(onehot.reshape(-1, atmos_column_blocks).T, returned, precision=FULL_PRECISION)

def pick_rows(source, index):
    return jnp.take(source, index, axis=0)

def section_inward(operands):
    return jax.vmap(remap_inward)(operands[0], operands[1])

def section_outward(operands):
    return jax.vmap(partial(remap_outward, total_slots=N_TILE * SLOT))(operands[0], operands[1], operands[2])

def two_substeps(operands):
    tracers, wet_cells, forcing = operands
    wet_rim = jnp.pad(wet_cells, 1)
    levels = tracers.shape[0] // 2
    for repeat in range(2):
        tracers = substep(jnp.pad(tracers, ((0, 0), (1, 1), (1, 1))), wet_rim, forcing, levels)
    return tracers

def reference(atmos_profile_state, previous_surface_temp, outbound_block_index, outbound_slot_counts, pair_source_slot, overlay_weight, ocean_tracer_state, ocean_cell_mask):
    device_count = N_SEC * N_TILE * N_LEV
    flux_terms = compute_surface_flux(atmos_profile_state, previous_surface_temp)
    blocks = flux_terms.reshape(4, device_count, AB, BLK).transpose(1, 2, 0, 3).reshape(device_count, AB, 4 * BLK)
    send_rows = outbound_block_index.reshape(device_count, N_TILE * SLOT)
    outgoing = jax.vmap(pick_rows)(blocks, send_rows)
    outgoing = outgoing.reshape(N_SEC, N_TILE, N_LEV, N_TILE, SLOT, 4 * BLK)
    arrived = outgoing.transpose(0, 3, 2, 1, 4, 5).reshape(device_count, N_TILE * SLOT, 4 * BLK)
    pair_slots = pair_source_slot.reshape(device_count, OB * K)
    picked = jax.vmap(pick_rows)(arrived, pair_slots).reshape(N_SEC, -1, OB, K, 4, BLK)
    weight = overlay_weight.reshape(N_SEC, -1, OB, K, BLK, BLK)
    forcing = lax.map(section_inward, (weight, picked))
    forcing = forcing.reshape(N_SEC, N_TILE, N_LEV, 4, OB, BLK).transpose(0, 3, 1, 4, 2, 5)
    forcing = forcing.reshape(N_SEC, 4, N_TILE * OB, N_LEV * BLK)
    tracers = ocean_tracer_state.reshape(2 * LEV_O, N_SEC, N_TILE * OB, N_LEV * BLK).transpose(1, 0, 2, 3)
    wet_cells = ocean_cell_mask.astype(jnp.float32).reshape(N_SEC, N_TILE * OB, N_LEV * BLK)
    updated = lax.map(two_substeps, (tracers, wet_cells, forcing))
    ocean_output_tracers = updated.transpose(1, 0, 2, 3).reshape(2, LEV_O, OX, OY)
    sea_surface = ocean_output_tracers[0, 0].reshape(N_SEC, N_TILE, OB, N_LEV, BLK).transpose(0, 1, 3, 2, 4)
    sea_surface = sea_surface.reshape(N_SEC, -1, OB, BLK)
    replies = lax.map(section_outward, (weight, sea_surface, pair_slots.reshape(N_SEC, -1, OB, K)))
    replies = replies.reshape(N_SEC, N_TILE, N_LEV, N_TILE, SLOT, 2 * BLK).transpose(0, 3, 2, 1, 4, 5)
    replies = replies.reshape(device_count, N_TILE * SLOT, 2 * BLK)
    accumulated = jax.vmap(partial(collect_returns, atmos_column_blocks=AB))(replies, outbound_block_index.reshape(device_count, N_TILE, SLOT), outbound_slot_counts)
    accumulated = accumulated.reshape(device_count, AB, 2, BLK)
    numerator = accumulated[:, :, 0].reshape(-1)
    denominator = accumulated[:, :, 1].reshape(-1)
    surface_temp_columns = (previous_surface_temp + numerator) / (1.0 + denominator)
    return (ocean_output_tracers, surface_temp_columns)
```

```python
import math

import jax
import jax.numpy as jnp
from jax import lax
from jax.experimental import pallas as pl
from jax.experimental.pallas import tpu as pltpu
from jax.sharding import PartitionSpec as P

F32 = jnp.float32
BF16 = jnp.bfloat16
DIFFUSION_RATE = 0.15
LANES = 128
ROWS = 8
LEVELS = 80
MASK_LANE = LEVELS
CELLS = 2 * LEVELS
BEFORE = CELLS
WET = 2 * CELLS
CORNER = WET + ROWS
MESSAGE = CORNER + ROWS
VMEM_LIMIT = 16 * 1024 * 1024

VM = pl.BlockSpec(memory_space=pltpu.VMEM)
SM = pl.BlockSpec(memory_space=pltpu.SMEM)
AN = pl.BlockSpec(memory_space=pl.ANY)


def vm(value):
    return pltpu.with_memory_space_constraint(value, pltpu.VMEM)


def hbm(value):
    return pltpu.with_memory_space_constraint(value, pltpu.HBM)


def call(kernel, out_shape, in_specs, scratch=(), name=None, aliases=None):
    outs = jax.tree.map(lambda _: VM, out_shape)
    return pl.pallas_call(
        kernel,
        out_shape=out_shape,
        in_specs=in_specs,
        out_specs=outs,
        scratch_shapes=list(scratch),
        name=name,
        input_output_aliases=aliases or {},
        compiler_params=pltpu.CompilerParams(vmem_limit_bytes=VMEM_LIMIT),
    )


def split3(value):
    high = value.astype(BF16).astype(F32)
    rest = value - high
    middle = rest.astype(BF16).astype(F32)
    return high, middle, rest - middle


def iota(axis):
    return lax.broadcasted_iota(jnp.int32, (ROWS, LANES), axis)


def roll(value, shift, axis):
    return pltpu.roll(value, shift, axis)


def flux_kernel(atmos_in, previous_in, index_in, packed, blocks, atmos, previous, index, arrivals):
    copies = [pltpu.make_async_copy(index_in, index, arrivals.at[0])]
    copies.append(pltpu.make_async_copy(previous_in, previous, arrivals.at[1]))
    for field in range(4):
        copies.append(
            pltpu.make_async_copy(atmos_in.at[field], atmos.at[field], arrivals.at[2 + field])
        )
    for copy in copies:
        copy.start()
    levels = atmos.shape[1]
    row = lax.broadcasted_iota(jnp.int32, (ROWS, levels), 0)
    level = lax.broadcasted_iota(jnp.int32, (ROWS, levels), 1).astype(F32)
    bottom_total = sum(math.exp(-l / 3.0) for l in range(levels))
    radiative_total = sum(math.exp(-l / 24.0) for l in range(levels))
    bottom = split3(jnp.exp(-level / 3.0) / bottom_total)
    radiative = split3(jnp.exp(-level / 24.0) / radiative_total)
    table = jnp.zeros((ROWS, levels), F32)
    for at, part in enumerate(bottom + radiative):
        table = jnp.where(row == at, part, table)
    table = table.astype(BF16)

    def sums(field):
        copies[2 + field].wait()
        return lax.dot_general(
            table, atmos[field], (((1,), (0,)), ((), ())), preferred_element_type=F32
        )

    def low(value):
        return value[0:1] + value[1:2] + value[2:3]

    copies[0].wait()
    copies[1].wait()
    temperature = sums(0)
    humidity = sums(1)
    radiation = temperature[3:4] + temperature[4:5] + temperature[5:6]
    east = low(sums(2))
    north = low(sums(3))
    speed = jnp.sqrt(east * east + north * north + 1.0)
    prior = previous[...]
    terms = (
        0.3 * speed * (low(temperature) - prior) + 0.5 * radiation,
        0.3 * speed * (jnp.exp(0.2 * prior) - 1.0 - low(humidity)),
        0.1 * speed * east,
        0.1 * speed * north,
    )
    for term, value in enumerate(terms):
        for block in range(blocks.shape[0]):
            blocks[block, term : term + 1, :] = value[:, block * LANES : (block + 1) * LANES]
    for slot in range(packed.shape[0]):
        packed[slot] = blocks[index[slot % 2, slot // 2]]


def tile(ref, at):
    return ref[pl.ds(pl.multiple_of(at * ROWS, ROWS), ROWS), :]


def to_first(value, level):
    return roll(value, lax.rem(LANES - level, LANES), 1)


def to_last(value, level):
    return roll(value, LANES - 1 - level, 1)


def first_kernel(
    arrived, slots, weight, tracers, mask,
    partial, north, south, west, east, coefficients, picked, forcing,
):
    pairs = weight.shape[1]
    for row in range(ROWS):
        for pair in range(pairs):
            picked[row // 2, 4 * (row % 2) : 4 * (row % 2) + 4, pair * LANES : (pair + 1) * LANES] = (
                arrived[slots[pair, row]]
            )
    for half in range(ROWS // 2):
        left = jnp.concatenate(split3(picked[half]), axis=0).astype(BF16)
        for parity in range(2):
            row = 2 * half + parity
            right = jnp.concatenate([weight[row, pair] for pair in range(pairs)], axis=1)
            product = lax.dot_general(
                left, right, (((1,), (1,)), ((), ())), preferred_element_type=F32
            )
            product = product[0:8] + product[8:16] + product[16:24]
            for term in range(4):
                at = 4 * parity + term
                forcing[term, row : row + 1, :] = product[at : at + 1]
    sub, lane = iota(0), iota(1)
    wet = mask[...].astype(F32)
    inner = (
        DIFFUSION_RATE * jnp.where(sub == 0, 0.0, wet * roll(wet, 1, 0)),
        DIFFUSION_RATE * jnp.where(sub == ROWS - 1, 0.0, wet * roll(wet, ROWS - 1, 0)),
        DIFFUSION_RATE * jnp.where(lane == 0, 0.0, wet * roll(wet, 1, 1)),
        DIFFUSION_RATE * jnp.where(lane == LANES - 1, 0.0, wet * roll(wet, LANES - 1, 1)),
    )
    total_weight = inner[0] + inner[1] + inner[2] + inner[3]
    stress_east, stress_north = forcing[2], forcing[3]
    stress = jnp.sqrt(stress_east * stress_east + stress_north * stress_north)
    constant = 0.05 * wet
    decaying = 0.15 * wet * (stress / (1.0 + stress))
    surface = [0.5 * wet * forcing[0], 0.5 * wet * forcing[1]]
    for at, value in enumerate(inner + (wet, constant, decaying, surface[0], surface[1])):
        coefficients[at] = value
    unroll = 8
    decay = [math.exp(-inner_level / 8.0) for inner_level in range(unroll + 1)]

    def step(group, carry):
        now, flow, depth, kept = list(carry[0]), list(carry[1]), carry[2], list(carry[3])
        for inner_level in range(unroll):
            level = group * unroll + inner_level
            later = jnp.minimum(level + 1, LEVELS - 1)
            rate = constant + depth * decay[inner_level]
            marked = lane == level
            for tracer in range(2):
                here = now[tracer]
                below = tile(tracers, tracer * LEVELS + later)
                fall = rate * (below - here)
                left_side = roll(here, 1, 1)
                total = here - total_weight * here + (fall - flow[tracer])
                total = total + inner[0] * roll(here, 1, 0)
                total = total + inner[1] * roll(here, ROWS - 1, 0)
                total = total + inner[2] * left_side
                total = total + inner[3] * roll(here, LANES - 1, 1)
                at = pl.multiple_of((tracer * LEVELS + level) * ROWS, ROWS)
                partial[pl.ds(at, ROWS), :] = total
                now[tracer] = below
                flow[tracer] = fall
                for place, value in ((0, total), (2, here)):
                    kept[place + tracer] = jnp.where(
                        marked, roll(value, level, 1), kept[place + tracer]
                    )
                    kept[4 + place + tracer] = jnp.where(
                        marked, roll(value, level + 1, 1), kept[4 + place + tracer]
                    )
        return tuple(now), tuple(flow), depth * decay[unroll], tuple(kept)

    zero = jnp.zeros((ROWS, LANES), F32)
    first = (
        (tile(tracers, 0), tile(tracers, LEVELS)),
        (-surface[0], -surface[1]),
        decaying,
        (zero,) * 8,
    )
    kept = list(lax.fori_loop(0, LEVELS // unroll, step, first)[3])
    kept[2] = jnp.where(lane == MASK_LANE, roll(wet, MASK_LANE, 1), kept[2])
    kept[6] = jnp.where(lane == MASK_LANE, roll(wet, MASK_LANE + 1, 1), kept[6])
    for at in range(4):
        west[at] = kept[at]
        east[at] = kept[4 + at]
    for group in range(CELLS // ROWS):
        start = group * ROWS * ROWS
        for base, source in ((0, partial), (BEFORE, tracers)):
            at = pl.ds(base + group * ROWS, ROWS)
            north[at, :] = source[pl.ds(start, ROWS, stride=ROWS), :]
            south[at, :] = source[pl.ds(start + ROWS - 1, ROWS, stride=ROWS), :]
    north[WET:CORNER, :] = jnp.broadcast_to(wet[0:1], (ROWS, LANES))
    south[WET:CORNER, :] = jnp.broadcast_to(wet[ROWS - 1 :], (ROWS, LANES))
    north[CORNER:MESSAGE, :] = zero
    south[CORNER:MESSAGE, :] = zero


def corner_kernel(west, east, _, __, north, south):
    for at, source in enumerate((west[2], west[3], east[2], east[3])):
        north[CORNER + at : CORNER + at + 1, :] = source[0:1]
        south[CORNER + at : CORNER + at + 1, :] = source[ROWS - 1 :]


class Rim:
    def __init__(self, partial, own, halo, coefficients):
        self.partial = partial
        self.own_north, self.own_south, own_west, own_east = own
        self.north, self.south, west, east = halo
        self.sub, self.lane = iota(0), iota(1)
        sub, lane = self.sub, self.lane
        wet = coefficients[4]
        self.inner = [coefficients[at] for at in range(4)]
        wet_north = self.north[WET : WET + 1, :]
        wet_south = self.south[WET : WET + 1, :]
        wet_west = to_first(west[2], MASK_LANE)
        wet_east = to_last(east[2], MASK_LANE)
        self.row_north = DIFFUSION_RATE * wet[0:1] * wet_north
        self.row_south = DIFFUSION_RATE * wet[ROWS - 1 :] * wet_south
        column_west = DIFFUSION_RATE * wet * wet_west
        column_east = DIFFUSION_RATE * wet * wet_east
        zero = jnp.zeros((ROWS, LANES), F32)
        self.border = (
            jnp.where(sub == 0, self.row_north, zero),
            jnp.where(sub == ROWS - 1, self.row_south, zero),
            jnp.where(lane == 0, column_west, zero),
            jnp.where(lane == LANES - 1, column_east, zero),
        )
        self.total = sum(self.inner) + sum(self.border)
        self.step_west = [west[2 + tracer] - own_west[2 + tracer] for tracer in range(2)]
        self.step_east = [east[2 + tracer] - own_east[2 + tracer] for tracer in range(2)]
        ends = (
            (self.north, CORNER, wet_north, 0),
            (self.south, CORNER, wet_south, ROWS - 1),
        )
        self.side_west, self.side_east = [], []
        self.corner_weight = []
        for ref, base, wet_row, row in ends:
            diagonal_west = ref[base : base + 1, MASK_LANE : MASK_LANE + 1]
            diagonal_east = ref[base + 2 : base + 3, MASK_LANE : MASK_LANE + 1]
            self.corner_weight.append(
                jnp.where(lane[0:1] == 0, DIFFUSION_RATE * wet_row * diagonal_west, 0.0)
                + jnp.where(lane[0:1] == LANES - 1, DIFFUSION_RATE * wet_row * diagonal_east, 0.0)
            )
        for side, tiles, wet_side, column, steps, offset in (
            (self.side_west, west, wet_west[:, 0:1], column_west[:, 0:1], self.step_west, 0),
            (
                self.side_east,
                east,
                wet_east[:, LANES - 1 :],
                column_east[:, LANES - 1 :],
                self.step_east,
                2,
            ),
        ):
            for tracer in range(2):
                value = tiles[tracer] - column * steps[tracer]
                for ref, base, _, row in ends:
                    diagonal = ref[base + offset : base + offset + 1, MASK_LANE : MASK_LANE + 1]
                    corner = ref[base + offset + tracer : base + offset + tracer + 1, :]
                    value = value + jnp.where(
                        sub == row,
                        (DIFFUSION_RATE * wet_side * diagonal) * (corner - tiles[2 + tracer]),
                        0.0,
                    )
                side.append(value)
        self.corners = []
        for tracer in range(2):
            rows = []
            for ref in (self.north, self.south):
                rows.append(ref[CORNER + tracer : CORNER + tracer + 1, :])
                rows.append(roll(ref[CORNER + 2 : CORNER + 4, :], LANES - 1, 1)[tracer : tracer + 1])
            value = zero
            for at, row in enumerate(rows):
                value = jnp.where(sub == at, row, value)
            self.corners.append(value)

    def after(self, tracer, level):
        cell = tracer * LEVELS + level
        at = pl.ds(BEFORE + cell, 1)
        value = tile(self.partial, cell)
        value = value + self.border[0] * (self.north[at, :] - self.own_north[at, :])
        value = value + self.border[1] * (self.south[at, :] - self.own_south[at, :])
        value = value + self.border[2] * to_first(self.step_west[tracer], level)
        return value + self.border[3] * to_last(self.step_east[tracer], level)

    def lateral(self, tracer, level, here):
        cell = tracer * LEVELS + level
        now, before = pl.ds(cell, 1), pl.ds(BEFORE + cell, 1)
        turned = to_first(self.corners[tracer], level)
        lane = self.lane[0:1]
        value = here - self.total * here
        for ref, own, row, weight, border, at in (
            (self.north, self.own_north, self.row_north, self.corner_weight[0], self.border[0], 0),
            (self.south, self.own_south, self.row_south, self.corner_weight[1], self.border[1], 2),
        ):
            old = ref[before, :]
            corner = jnp.where(lane == 0, turned[at : at + 1], turned[at + 1 : at + 2])
            edge = ref[now, :] - row * (old - own[before, :]) + weight * (corner - old)
            value = value + border * edge
        value = value + self.border[2] * to_first(self.side_west[tracer], level)
        value = value + self.border[3] * to_last(self.side_east[tracer], level)
        value = value + self.inner[0] * roll(here, 1, 0)
        value = value + self.inner[1] * roll(here, ROWS - 1, 0)
        value = value + self.inner[2] * roll(here, 1, 1)
        return value + self.inner[3] * roll(here, LANES - 1, 1)


def reply_kernel(
    partial, own_north, own_south, own_west, own_east, north, south, west, east, coefficients,
    weight, slots, replies,
):
    pairs = weight.shape[1]
    own, halo = (own_north, own_south, own_west, own_east), (north, south, west, east)
    rim = Rim(partial, own, halo, coefficients)
    here = rim.after(0, 0)
    fall = (coefficients[5] + coefficients[6]) * (rim.after(0, 1) - here)
    surface = rim.lateral(0, 0, here) + (fall + coefficients[7])
    left = jnp.concatenate(split3(surface) + (jnp.ones((ROWS, LANES), F32),), axis=0).astype(BF16)
    replies[...] = jnp.zeros_like(replies)
    for row in range(ROWS):
        right = jnp.concatenate([weight[row, pair] for pair in range(pairs)], axis=1)
        product = lax.dot_general(left, right, (((1,), (0,)), ((), ())), preferred_element_type=F32)
        numer = product[row : row + 1] + product[8 + row : 9 + row] + product[16 + row : 17 + row]
        denom = product[24:25]
        both = jnp.concatenate([numer, denom], axis=0)
        for pair in range(pairs):
            slot = slots[pair, row]
            replies[slot] = replies[slot] + both[:, pair * LANES : (pair + 1) * LANES]


def second_kernel(
    partial, own_north, own_south, own_west, own_east, north, south, west, east, coefficients, _,
    output,
):
    own, halo = (own_north, own_south, own_west, own_east), (north, south, west, east)
    rim = Rim(partial, own, halo, coefficients)
    constant, decaying = coefficients[5], coefficients[6]
    unroll = 4
    decay = [math.exp(-inner_level / 8.0) for inner_level in range(unroll + 1)]

    def step(group, carry):
        now, flow, depth = list(carry[0]), list(carry[1]), carry[2]
        for inner_level in range(unroll):
            level = group * unroll + inner_level
            later = jnp.minimum(level + 1, LEVELS - 1)
            rate = constant + depth * decay[inner_level]
            for tracer in range(2):
                here = now[tracer]
                below = rim.after(tracer, later)
                fall = rate * (below - here)
                total = rim.lateral(tracer, level, here) + (fall - flow[tracer])
                at = pl.multiple_of((tracer * LEVELS + level) * ROWS, ROWS)
                output[pl.ds(at, ROWS), :] = total
                now[tracer] = below
                flow[tracer] = fall
        return tuple(now), tuple(flow), depth * decay[unroll]

    first = (
        (rim.after(0, 0), rim.after(1, 0)),
        (-coefficients[7], -coefficients[8]),
        decaying,
    )
    lax.fori_loop(0, LEVELS // unroll, step, first)


def final_kernel(returned, index, counts, previous, output):
    blocks = previous.shape[0]
    peers = counts.shape[1]
    block = lax.broadcasted_iota(jnp.int32, (blocks, peers), 0)
    numer = denom = None
    for place in range(2):
        chosen = (block == index[place : place + 1, :]) & (place < counts[...])
        chosen = chosen.astype(F32).astype(BF16)
        rows = [returned[pl.ds(2 * place + at, peers, stride=4), :] for at in range(2)]
        parts = jnp.concatenate(split3(rows[0]) + split3(rows[1]), axis=1).astype(BF16)
        product = lax.dot_general(
            chosen, parts, (((1,), (0,)), ((), ())), preferred_element_type=F32
        )
        cut = [product[:, at * LANES : (at + 1) * LANES] for at in range(6)]
        numer = cut[0] + cut[1] + cut[2] + (0.0 if numer is None else numer)
        denom = cut[3] + cut[4] + cut[5] + (0.0 if denom is None else denom)
    output[...] = (previous[...] + numer) / (1.0 + denom)


def shards(
    atmos_profile_state,
    previous_surface_temp,
    outbound_block_index,
    outbound_slot_counts,
    pair_source_slot,
    overlay_weight,
    ocean_tracer_state,
    ocean_cell_mask,
):
    peers, levs = lax.axis_size("tile"), lax.axis_size("lev")
    slot_total = 2 * peers
    blocks = previous_surface_temp.shape[0] // LANES
    shape = jax.ShapeDtypeStruct
    index = outbound_block_index.T
    slots = pair_source_slot.T
    tracers = ocean_tracer_state.reshape(CELLS * ROWS, LANES)
    prior = previous_surface_temp.reshape(1, -1)

    packed = call(
        flux_kernel,
        shape((slot_total, 4, LANES), F32),
        [AN, AN, AN],
        [
            pltpu.VMEM((blocks, 4, LANES), F32),
            pltpu.VMEM(atmos_profile_state.shape, BF16),
            pltpu.VMEM(prior.shape, F32),
            pltpu.SMEM(index.shape, jnp.int32),
            pltpu.SemaphoreType.DMA((6,)),
        ],
        "flux",
    )(hbm(atmos_profile_state), hbm(prior), hbm(index))
    arrived = lax.all_to_all(packed, "tile", split_axis=0, concat_axis=0, tiled=True)

    weight = vm(overlay_weight)
    row_message, column_message = shape((MESSAGE, LANES), F32), shape((4, ROWS, LANES), F32)
    partial, north, south, west, east, coefficients = call(
        first_kernel,
        (
            shape((CELLS * ROWS, LANES), F32),
            row_message,
            row_message,
            column_message,
            column_message,
            shape((9, ROWS, LANES), F32),
        ),
        [VM, SM] + [VM] * 3,
        [pltpu.VMEM((ROWS // 2, ROWS, 4 * LANES), F32), pltpu.VMEM((4, ROWS, LANES), F32)],
        "first",
    )(vm(arrived), slots, weight, vm(tracers), vm(ocean_cell_mask))
    halo_west = vm(lax.ppermute(east, "lev", [(i, i + 1) for i in range(levs - 1)]))
    halo_east = vm(lax.ppermute(west, "lev", [(i + 1, i) for i in range(levs - 1)]))
    north, south = call(
        corner_kernel,
        (row_message, row_message),
        [VM] * 4,
        (),
        "corner",
        {2: 0, 3: 1},
    )(halo_west, halo_east, vm(north), vm(south))
    halo_north = vm(lax.ppermute(south, "tile", [(i, i + 1) for i in range(peers - 1)]))
    halo_south = vm(lax.ppermute(north, "tile", [(i + 1, i) for i in range(peers - 1)]))
    edges = [
        vm(value)
        for value in (
            partial, north, south, west, east, halo_north, halo_south, halo_west, halo_east, coefficients,
        )
    ]
    replies = call(
        reply_kernel,
        shape((slot_total, 2, LANES), F32),
        [VM] * 11 + [SM],
        (),
        "reply",
    )(*edges, weight, slots)
    returned = lax.all_to_all(replies, "tile", split_axis=0, concat_axis=0, tiled=True)
    output = call(
        second_kernel,
        shape((CELLS * ROWS, LANES), F32),
        [VM] * 10 + [AN],
        (),
        "second",
    )(*edges, replies)
    surface = call(
        final_kernel,
        shape((blocks, LANES), F32),
        [VM] * 4,
        (),
        "final",
    )(
        returned.reshape(2 * slot_total, LANES),
        index,
        outbound_slot_counts,
        previous_surface_temp.reshape(blocks, LANES),
    )
    return (output.reshape(ocean_tracer_state.shape), surface.reshape(-1))


def solution(mesh):
    placed = (
        P(None, None, ("sec", "tile", "lev")),
        P(("sec", "tile", "lev")),
        P(("sec", "tile", "lev"), None),
        P(("sec", "tile", "lev"), None),
        P(("sec", "tile", "lev"), None),
        P(("sec", "tile", "lev"), None, None, None),
        P(None, None, ("sec", "tile"), "lev"),
        P(("sec", "tile"), "lev"),
    )
    return jax.shard_map(
        shards,
        mesh=mesh,
        in_specs=placed,
        out_specs=(P(None, None, ("sec", "tile"), "lev"), P(("sec", "tile", "lev"))),
        check_vma=False,
    )
```

```python
import math

import jax
import jax.numpy as jnp
from jax import lax
from jax.experimental import pallas as pl
from jax.experimental.pallas import tpu as pltpu
from jax.sharding import PartitionSpec as P

F32 = jnp.float32
BF16 = jnp.bfloat16
DIFFUSION_RATE = 0.15
LANES = 128
ROWS = 8
LEVELS = 80
MASK_LANE = LEVELS
CELLS = 2 * LEVELS
BEFORE = CELLS
WET = 2 * CELLS
MESSAGE = WET + ROWS
STAGED = 7
VMEM_LIMIT = 16 * 1024 * 1024

VM = pl.BlockSpec(memory_space=pltpu.VMEM)
SM = pl.BlockSpec(memory_space=pltpu.SMEM)
AN = pl.BlockSpec(memory_space=pl.ANY)


def vm(value):
    return pltpu.with_memory_space_constraint(value, pltpu.VMEM)


def hbm(value):
    return pltpu.with_memory_space_constraint(value, pltpu.HBM)


def call(kernel, out_shape, in_specs, scratch=(), name=None, aliases=None, outs=None):
    outs = outs or jax.tree.map(lambda _: VM, out_shape)
    return pl.pallas_call(
        kernel,
        out_shape=out_shape,
        in_specs=in_specs,
        out_specs=outs,
        scratch_shapes=list(scratch),
        name=name,
        input_output_aliases=aliases or {},
        compiler_params=pltpu.CompilerParams(vmem_limit_bytes=VMEM_LIMIT),
    )


def split3(value):
    high = value.astype(BF16).astype(F32)
    rest = value - high
    middle = rest.astype(BF16).astype(F32)
    return high, middle, rest - middle


def iota(axis):
    return lax.broadcasted_iota(jnp.int32, (ROWS, LANES), axis)


def roll(value, shift, axis):
    return pltpu.roll(value, shift, axis)


def flux_kernel(
    atmos_in, previous_in, index_in, *refs,
):
    staged_in, (packed, *staged) = refs[:STAGED], refs[STAGED : 2 * STAGED + 1]
    blocks, atmos, previous, index, arrivals, stage_arrivals = refs[2 * STAGED + 1 :]
    copies = [pltpu.make_async_copy(index_in, index, arrivals.at[0])]
    copies.append(pltpu.make_async_copy(previous_in, previous, arrivals.at[1]))
    for field in range(4):
        copies.append(
            pltpu.make_async_copy(atmos_in.at[field], atmos.at[field], arrivals.at[2 + field])
        )
    for copy in copies:
        copy.start()
    staging = [
        pltpu.make_async_copy(source, target, stage_arrivals.at[at])
        for at, (source, target) in enumerate(zip(staged_in[1:], staged[1:]))
    ]
    inside = staged[0].at[pl.ds(ROWS, CELLS * ROWS), :]
    staging.append(pltpu.make_async_copy(staged_in[0], inside, stage_arrivals.at[STAGED - 1]))
    for copy in staging:
        copy.start()
    levels = atmos.shape[1]
    row = lax.broadcasted_iota(jnp.int32, (ROWS, levels), 0)
    level = lax.broadcasted_iota(jnp.int32, (ROWS, levels), 1).astype(F32)
    bottom_total = sum(math.exp(-l / 3.0) for l in range(levels))
    radiative_total = sum(math.exp(-l / 24.0) for l in range(levels))
    bottom = split3(jnp.exp(-level / 3.0) / bottom_total)
    radiative = split3(jnp.exp(-level / 24.0) / radiative_total)
    table = jnp.zeros((ROWS, levels), F32)
    for at, part in enumerate(bottom + radiative):
        table = jnp.where(row == at, part, table)
    table = table.astype(BF16)

    def sums(field):
        copies[2 + field].wait()
        return lax.dot_general(
            table, atmos[field], (((1,), (0,)), ((), ())), preferred_element_type=F32
        )

    def low(value):
        return value[0:1] + value[1:2] + value[2:3]

    staged[0][0:ROWS, :] = jnp.zeros((ROWS, LANES), F32)
    staged[0][(CELLS + 1) * ROWS :, :] = jnp.zeros((ROWS, LANES), F32)
    copies[0].wait()
    copies[1].wait()
    temperature = sums(0)
    humidity = sums(1)
    radiation = temperature[3:4] + temperature[4:5] + temperature[5:6]
    east = low(sums(2))
    north = low(sums(3))
    speed = jnp.sqrt(east * east + north * north + 1.0)
    prior = previous[...]
    terms = (
        0.3 * speed * (low(temperature) - prior) + 0.5 * radiation,
        0.3 * speed * (jnp.exp(0.2 * prior) - 1.0 - low(humidity)),
        0.1 * speed * east,
        0.1 * speed * north,
    )
    for term, value in enumerate(terms):
        for block in range(blocks.shape[0]):
            blocks[block, term : term + 1, :] = value[:, block * LANES : (block + 1) * LANES]
    for slot in range(packed.shape[0]):
        packed[slot] = blocks[index[slot % 2, slot // 2]]
    for copy in staging:
        copy.wait()


def tile(ref, at):
    return ref[pl.ds(pl.multiple_of(at * ROWS, ROWS), ROWS), :]


def inside(ref, at):
    return ref[pl.ds(pl.multiple_of((at + 1) * ROWS, ROWS), ROWS), :]


def to_first(value, level):
    return roll(value, lax.rem(LANES - level, LANES), 1)


def to_last(value, level):
    return roll(value, LANES - 1 - level, 1)


def edge_rows():
    core_row = (ROWS - 1) * (1 - lax.rem(lax.axis_index("tile"), 2))
    return ROWS - 1 - core_row, core_row


def first_kernel(
    arrived, slots, weight, tracers, mask,
    partial, zed, core, coefficients, picked, forcing,
):
    pairs = weight.shape[1]
    for row in range(ROWS):
        for pair in range(pairs):
            picked[row // 2, 4 * (row % 2) : 4 * (row % 2) + 4, pair * LANES : (pair + 1) * LANES] = (
                arrived[slots[pair, row]]
            )
    for half in range(ROWS // 2):
        left = jnp.concatenate(split3(picked[half]), axis=0).astype(BF16)
        for parity in range(2):
            row = 2 * half + parity
            right = jnp.concatenate([weight[row, pair] for pair in range(pairs)], axis=1)
            product = lax.dot_general(
                left, right, (((1,), (1,)), ((), ())), preferred_element_type=F32
            )
            product = product[0:8] + product[8:16] + product[16:24]
            for term in range(4):
                at = 4 * parity + term
                forcing[term, row : row + 1, :] = product[at : at + 1]
    sub, lane = iota(0), iota(1)
    wet = mask[...].astype(F32)
    inner = (
        DIFFUSION_RATE * jnp.where(sub == 0, 0.0, wet * roll(wet, 1, 0)),
        DIFFUSION_RATE * jnp.where(sub == ROWS - 1, 0.0, wet * roll(wet, ROWS - 1, 0)),
        DIFFUSION_RATE * jnp.where(lane == 0, 0.0, wet * roll(wet, 1, 1)),
        DIFFUSION_RATE * jnp.where(lane == LANES - 1, 0.0, wet * roll(wet, LANES - 1, 1)),
    )
    total_weight = inner[0] + inner[1] + inner[2] + inner[3]
    stress_east, stress_north = forcing[2], forcing[3]
    stress = jnp.sqrt(stress_east * stress_east + stress_north * stress_north)
    constant = 0.05 * wet
    decaying = 0.15 * wet * (stress / (1.0 + stress))
    surface = [0.5 * wet * forcing[0], 0.5 * wet * forcing[1]]
    for at, value in enumerate(inner + (wet, constant, decaying, surface[0], surface[1])):
        coefficients[at] = value
    unroll = 8
    decay = [math.exp(-inner_level / 8.0) for inner_level in range(unroll + 1)]

    def step(group, carry):
        now, flow, depth = list(carry[0]), list(carry[1]), carry[2]
        for inner_level in range(unroll):
            level = group * unroll + inner_level
            later = jnp.minimum(level + 1, LEVELS - 1)
            rate = constant + depth * decay[inner_level]
            for tracer in range(2):
                here = now[tracer]
                at = pl.multiple_of((tracer * LEVELS + level) * ROWS, ROWS)
                below = inside(tracers, tracer * LEVELS + later)
                fall = rate * (below - here)
                total = here - total_weight * here + (fall - flow[tracer])
                total = total + inner[0] * tracers[pl.ds(at + ROWS - 1, ROWS), :]
                total = total + inner[1] * tracers[pl.ds(at + ROWS + 1, ROWS), :]
                total = total + inner[2] * roll(here, 1, 1)
                total = total + inner[3] * roll(here, LANES - 1, 1)
                partial[pl.ds(at, ROWS), :] = total
                now[tracer] = below
                flow[tracer] = fall
        return tuple(now), tuple(flow), depth * decay[unroll]

    first = (
        (inside(tracers, 0), inside(tracers, LEVELS)),
        (-surface[0], -surface[1]),
        decaying,
    )
    lax.fori_loop(0, LEVELS // unroll, step, first)
    for target, row in zip((zed, core), edge_rows()):
        for group in range(CELLS // ROWS):
            start = group * ROWS * ROWS + row
            at = pl.ds(start, ROWS, stride=ROWS)
            target[group * ROWS : (group + 1) * ROWS, :] = partial[at, :]
            at = pl.ds(start + ROWS, ROWS, stride=ROWS)
            target[BEFORE + group * ROWS : BEFORE + (group + 1) * ROWS, :] = tracers[at, :]
        target[WET:MESSAGE, :] = jnp.broadcast_to(coefficients[4, pl.ds(row, 1), :], (ROWS, LANES))


def column_kernel(partial, tracers, mask, west, east):
    lane = iota(1)
    wet = mask[...].astype(F32)
    unroll = 8

    def step(group, carry):
        kept = list(carry)
        for inner_level in range(unroll):
            level = group * unroll + inner_level
            marked = lane == level
            for tracer in range(2):
                cell = tracer * LEVELS + level
                for place, value in ((0, tile(partial, cell)), (2, inside(tracers, cell))):
                    at = place + tracer
                    kept[at] = jnp.where(marked, roll(value, level, 1), kept[at])
                    kept[4 + at] = jnp.where(marked, roll(value, level + 1, 1), kept[4 + at])
        return tuple(kept)

    zero = jnp.zeros((ROWS, LANES), F32)
    kept = list(lax.fori_loop(0, LEVELS // unroll, step, (zero,) * 8))
    kept[2] = jnp.where(lane == MASK_LANE, roll(wet, MASK_LANE, 1), kept[2])
    kept[6] = jnp.where(lane == MASK_LANE, roll(wet, MASK_LANE + 1, 1), kept[6])
    for at in range(4):
        west[at] = kept[at]
        east[at] = kept[4 + at]
    west[4] = zero
    east[4] = zero


def corner_kernel(zed, core, _, __, west, east):
    lane = lax.broadcasted_iota(jnp.int32, (1, LANES), 1)
    padding = jnp.zeros((LANES - LEVELS, LANES), F32)
    for place, source in enumerate((zed, core)):
        for tracer in range(2):
            start = BEFORE + tracer * LEVELS
            turned = jnp.concatenate([source[start : start + LEVELS, :], padding], axis=0).T
            for target, end in ((west, 0), (east, LANES - 1)):
                row = turned[end : end + 1, :]
                if tracer == 0:
                    row = jnp.where(lane == MASK_LANE, source[WET : WET + 1, end : end + 1], row)
                at = 2 * place + tracer
                target[4, at : at + 1, :] = row


class Rim:
    def __init__(self, partial, own, halo, coefficients):
        self.partial = partial
        self.own, self.halo = own[0:2], halo[0:2]
        own_west, own_east, west, east = own[2], own[3], halo[2], halo[3]
        self.west, self.east = west, east
        sub, lane = iota(0), iota(1)
        self.lane = lane[0:1]
        wet = coefficients[4]
        rows = edge_rows()
        self.inner = [coefficients[at] for at in range(4)]
        wet_rows = [ref[WET : WET + 1, :] for ref in self.halo]
        wet_west = to_first(west[2], MASK_LANE)
        wet_east = to_last(east[2], MASK_LANE)
        self.rows = [
            DIFFUSION_RATE * coefficients[4, pl.ds(row, 1), :] * wet_row
            for row, wet_row in zip(rows, wet_rows)
        ]
        column_west = DIFFUSION_RATE * wet * wet_west
        column_east = DIFFUSION_RATE * wet * wet_east
        zero = jnp.zeros((ROWS, LANES), F32)
        self.border = (
            jnp.where(sub == rows[0], self.rows[0], zero),
            jnp.where(sub == rows[1], self.rows[1], zero),
            jnp.where(lane == 0, column_west, zero),
            jnp.where(lane == LANES - 1, column_east, zero),
        )
        self.total = sum(self.inner) + sum(self.border)
        self.step_west = [west[2 + tracer] - own_west[2 + tracer] for tracer in range(2)]
        self.step_east = [east[2 + tracer] - own_east[2 + tracer] for tracer in range(2)]
        self.corner_weight = []
        for place, wet_row in enumerate(wet_rows):
            mask = slice(2 * place, 2 * place + 1), slice(MASK_LANE, MASK_LANE + 1)
            self.corner_weight.append(
                jnp.where(self.lane == 0, DIFFUSION_RATE * wet_row * west[(4,) + mask], 0.0)
                + jnp.where(self.lane == LANES - 1, DIFFUSION_RATE * wet_row * east[(4,) + mask], 0.0)
            )
        self.side_west, self.side_east = [], []
        for side, tiles, wet_side, column, steps in (
            (self.side_west, west, wet_west[:, 0:1], column_west[:, 0:1], self.step_west),
            (
                self.side_east,
                east,
                wet_east[:, LANES - 1 :],
                column_east[:, LANES - 1 :],
                self.step_east,
            ),
        ):
            for tracer in range(2):
                value = tiles[tracer] - column * steps[tracer]
                for place, row in enumerate(rows):
                    diagonal = tiles[4, 2 * place : 2 * place + 1, MASK_LANE : MASK_LANE + 1]
                    corner = tiles[4, 2 * place + tracer : 2 * place + tracer + 1, :]
                    value = value + jnp.where(
                        sub == row,
                        (DIFFUSION_RATE * wet_side * diagonal) * (corner - tiles[2 + tracer]),
                        0.0,
                    )
                side.append(value)

    def beyond(self, place, now, before, corner):
        halo = self.halo[place]
        old = halo[before, :]
        step = old - self.own[place][before, :]
        edge = halo[now, :] - self.rows[place] * step + self.corner_weight[place] * (corner - old)
        return step, edge

    def after(self, tracer, level, steps):
        value = tile(self.partial, tracer * LEVELS + level)
        value = value + self.border[0] * steps[0] + self.border[1] * steps[1]
        value = value + self.border[2] * to_first(self.step_west[tracer], level)
        return value + self.border[3] * to_last(self.step_east[tracer], level)

    def lateral(self, tracer, level, here, edges):
        value = here - self.total * here
        value = value + self.border[0] * edges[0] + self.border[1] * edges[1]
        value = value + self.border[2] * to_first(self.side_west[tracer], level)
        value = value + self.border[3] * to_last(self.side_east[tracer], level)
        value = value + self.inner[0] * roll(here, 1, 0)
        value = value + self.inner[1] * roll(here, ROWS - 1, 0)
        value = value + self.inner[2] * roll(here, 1, 1)
        return value + self.inner[3] * roll(here, LANES - 1, 1)


def reply_kernel(
    partial, own_zed, own_core, own_west, own_east, zed, core, west, east, coefficients,
    weight, slots, replies,
):
    pairs = weight.shape[1]
    own, halo = (own_zed, own_core, own_west, own_east), (zed, core, west, east)
    rim = Rim(partial, own, halo, coefficients)
    steps, edges = [], []
    for place in range(2):
        row = slice(2 * place, 2 * place + 1)
        corner = jnp.where(rim.lane == 0, west[4, row, 0:1], east[4, row, 0:1])
        step, edge = rim.beyond(place, slice(0, 1), slice(BEFORE, BEFORE + 1), corner)
        steps.append(step)
        edges.append(edge)
    below = slice(BEFORE + 1, BEFORE + 2)
    here = rim.after(0, 0, steps)
    later = rim.after(0, 1, [rim.halo[at][below, :] - rim.own[at][below, :] for at in range(2)])
    fall = (coefficients[5] + coefficients[6]) * (later - here)
    surface = rim.lateral(0, 0, here, edges) + (fall + coefficients[7])
    left = jnp.concatenate(split3(surface) + (jnp.ones((ROWS, LANES), F32),), axis=0).astype(BF16)
    replies[...] = jnp.zeros_like(replies)
    for row in range(ROWS):
        right = jnp.concatenate([weight[row, pair] for pair in range(pairs)], axis=1)
        product = lax.dot_general(left, right, (((1,), (0,)), ((), ())), preferred_element_type=F32)
        numer = product[row : row + 1] + product[8 + row : 9 + row] + product[16 + row : 17 + row]
        denom = product[24:25]
        both = jnp.concatenate([numer, denom], axis=0)
        for pair in range(pairs):
            slot = slots[pair, row]
            replies[slot] = replies[slot] + both[:, pair * LANES : (pair + 1) * LANES]


def final_kernel(
    returned, index, counts, previous, surface,
):
    blocks = previous.shape[0]
    peers = counts.shape[1]
    block = lax.broadcasted_iota(jnp.int32, (blocks, peers), 0)
    numer, denom = 0.0, 0.0
    for place in range(2):
        chosen = (block == index[place : place + 1, :]) & (place < counts[...])
        chosen = chosen.astype(F32).astype(BF16)
        rows = [returned[pl.ds(2 * place + at, peers, stride=4), :] for at in range(2)]
        parts = jnp.concatenate(split3(rows[0]) + split3(rows[1]), axis=1).astype(BF16)
        product = lax.dot_general(
            chosen, parts, (((1,), (0,)), ((), ())), preferred_element_type=F32
        )
        cuts = [product[:, at * LANES : (at + 1) * LANES] for at in range(6)]
        numer = cuts[0] + cuts[1] + cuts[2] + numer
        denom = cuts[3] + cuts[4] + cuts[5] + denom
    surface[...] = (previous[...] + numer) / (1.0 + denom)


def second_kernel(
    partial, own_zed, own_core, own_west, own_east, zed, core, west, east, coefficients, _,
    output, result, step_core, step_zed, edge_core, edge_zed, sent,
):
    own, halo = (own_zed, own_core, own_west, own_east), (zed, core, west, east)
    rim = Rim(partial, own, halo, coefficients)
    ends = jnp.concatenate([west[4, 0:4, :], east[4, 0:4, :]], axis=0).T
    lane = lax.broadcasted_iota(jnp.int32, (LEVELS, LANES), 1)
    for place, (steps, edges) in enumerate(((step_zed, edge_zed), (step_core, edge_core))):
        for tracer in range(2):
            at = 2 * place + tracer
            corner = jnp.where(lane == 0, ends[0:LEVELS, at : at + 1], ends[0:LEVELS, at + 4 : at + 5])
            now = slice(tracer * LEVELS, (tracer + 1) * LEVELS)
            before = slice(BEFORE + tracer * LEVELS, BEFORE + (tracer + 1) * LEVELS)
            steps[now, :], edges[now, :] = rim.beyond(place, now, before, corner)
    constant, decaying = coefficients[5], coefficients[6]
    unroll, parts = 4, 4
    decay = [math.exp(-inner_level / 8.0) for inner_level in range(unroll + 1)]

    def pick(refs, tracer, level):
        return [ref[pl.ds(tracer * LEVELS + level, 1), :] for ref in refs]

    def after(tracer, level):
        return rim.after(tracer, level, pick((step_zed, step_core), tracer, level))

    def step(group, carry):
        now, flow, depth = list(carry[0]), list(carry[1]), carry[2]
        for inner_level in range(unroll):
            level = group * unroll + inner_level
            later = jnp.minimum(level + 1, LEVELS - 1)
            rate = constant + depth * decay[inner_level]
            for tracer in range(2):
                here = now[tracer]
                below = after(tracer, later)
                fall = rate * (below - here)
                edges = pick((edge_zed, edge_core), tracer, level)
                total = rim.lateral(tracer, level, here, edges) + (fall - flow[tracer])
                at = pl.multiple_of((tracer * LEVELS + level) * ROWS, ROWS)
                result[pl.ds(at, ROWS), :] = total
                now[tracer] = below
                flow[tracer] = fall
        return tuple(now), tuple(flow), depth * decay[unroll]

    carry = ((after(0, 0), after(1, 0)), (-coefficients[7], -coefficients[8]), decaying)
    groups = LEVELS // unroll // parts
    copies = []
    for part in range(parts):
        carry = lax.fori_loop(part * groups, (part + 1) * groups, step, carry)
        count = groups * unroll * ROWS
        for tracer in range(2):
            at = pl.ds(tracer * LEVELS * ROWS + part * count, count)
            copies.append(
                pltpu.make_async_copy(result.at[at, :], output.at[at, :], sent.at[len(copies)])
            )
            copies[-1].start()
    for copy in copies:
        copy.wait()


def shards(
    atmos_profile_state,
    previous_surface_temp,
    outbound_block_index,
    outbound_slot_counts,
    pair_source_slot,
    overlay_weight,
    ocean_tracer_state,
    ocean_cell_mask,
):
    peers, levs = lax.axis_size("tile"), lax.axis_size("lev")
    slot_total = 2 * peers
    blocks = previous_surface_temp.shape[0] // LANES
    shape = jax.ShapeDtypeStruct
    index = outbound_block_index.T
    slots = pair_source_slot.T
    tracers = ocean_tracer_state.reshape(CELLS * ROWS, LANES)
    prior = previous_surface_temp.reshape(1, -1)
    square = previous_surface_temp.reshape(blocks, LANES)

    staged = (tracers, overlay_weight, ocean_cell_mask, slots, index, outbound_slot_counts, square)
    packed, *staged = call(
        flux_kernel,
        (pltpu.VMEM((slot_total, 4, LANES), F32),)
        + (pltpu.VMEM(((CELLS + 2) * ROWS, LANES), F32),)
        + tuple(pltpu.VMEM(value.shape, value.dtype) for value in staged[1:]),
        [AN] * (3 + STAGED),
        [
            pltpu.VMEM((blocks, 4, LANES), F32),
            pltpu.VMEM(atmos_profile_state.shape, BF16),
            pltpu.VMEM(prior.shape, F32),
            pltpu.SMEM(index.shape, jnp.int32),
            pltpu.SemaphoreType.DMA((6,)),
            pltpu.SemaphoreType.DMA((STAGED,)),
        ],
        "flux",
        outs=(VM,) * (1 + STAGED),
    )(hbm(atmos_profile_state), hbm(prior), hbm(index), *[hbm(value) for value in staged])
    tracers, weight, mask, slots, index, counts, square = staged
    arrived = lax.all_to_all(packed, "tile", split_axis=0, concat_axis=0, tiled=True)

    row_message, column_message = shape((MESSAGE, LANES), F32), shape((5, ROWS, LANES), F32)
    partial, zed, core, coefficients = call(
        first_kernel,
        (
            shape((CELLS * ROWS, LANES), F32),
            row_message,
            row_message,
            shape((9, ROWS, LANES), F32),
        ),
        [VM, SM] + [VM] * 3,
        [pltpu.VMEM((ROWS // 2, ROWS, 4 * LANES), F32), pltpu.VMEM((4, ROWS, LANES), F32)],
        "first",
    )(vm(arrived), slots, vm(weight), vm(tracers), vm(mask))
    across = [(i, i + 1) for i in range(1, peers - 1, 2)]
    across += [(target, source) for source, target in across]
    halo_core = vm(lax.ppermute(core, "tile", [(i, i ^ 1) for i in range(peers)]))
    halo_zed = vm(lax.ppermute(zed, "tile", across))
    west, east = call(
        column_kernel,
        (column_message, column_message),
        [VM] * 3,
        (),
        "columns",
    )(vm(partial), vm(tracers), vm(mask))
    west, east = call(
        corner_kernel,
        (column_message, column_message),
        [VM] * 4,
        (),
        "corner",
        {2: 0, 3: 1},
    )(halo_zed, halo_core, vm(west), vm(east))
    halo_west = vm(lax.ppermute(east, "lev", [(i, i + 1) for i in range(levs - 1)]))
    halo_east = vm(lax.ppermute(west, "lev", [(i + 1, i) for i in range(levs - 1)]))
    edges = [
        vm(value)
        for value in (
            partial, zed, core, west, east, halo_zed, halo_core, halo_west, halo_east, coefficients,
        )
    ]
    replies = call(
        reply_kernel,
        shape((slot_total, 2, LANES), F32),
        [VM] * 11 + [SM],
        (),
        "reply",
    )(*edges, vm(weight), slots)
    returned = lax.all_to_all(replies, "tile", split_axis=0, concat_axis=0, tiled=True)
    output = call(
        second_kernel,
        shape((CELLS * ROWS, LANES), F32),
        [VM] * 10 + [AN],
        [pltpu.VMEM((CELLS * ROWS, LANES), F32)]
        + [pltpu.VMEM((CELLS, LANES), F32)] * 4
        + [pltpu.SemaphoreType.DMA((8,))],
        "second",
        outs=AN,
    )(*edges, replies)
    surface = call(
        final_kernel,
        shape((blocks, LANES), F32),
        [VM] * 4,
        (),
        "final",
    )(vm(returned.reshape(2 * slot_total, LANES)), vm(index), vm(counts), vm(square))
    return (output.reshape(ocean_tracer_state.shape), surface.reshape(-1))


def solution(mesh):
    placed = (
        P(None, None, ("sec", "tile", "lev")),
        P(("sec", "tile", "lev")),
        P(("sec", "tile", "lev"), None),
        P(("sec", "tile", "lev"), None),
        P(("sec", "tile", "lev"), None),
        P(("sec", "tile", "lev"), None, None, None),
        P(None, None, ("sec", "tile"), "lev"),
        P(("sec", "tile"), "lev"),
    )
    return jax.shard_map(
        shards,
        mesh=mesh,
        in_specs=placed,
        out_specs=(P(None, None, ("sec", "tile"), "lev"), P(("sec", "tile", "lev"))),
        check_vma=False,
    )
```

```python
import math

import jax
import jax.numpy as jnp
from jax import lax
from jax.experimental import pallas as pl
from jax.experimental.pallas import tpu as pltpu
from jax.sharding import PartitionSpec as P

F32 = jnp.float32
BF16 = jnp.bfloat16
DIFFUSION_RATE = 0.15
LANES = 128
ROWS = 8
LEVELS = 80
MASK_LANE = LEVELS
CELLS = 2 * LEVELS
BEFORE = CELLS
WET = 2 * CELLS
MESSAGE = WET + ROWS
STAGED = 7
VMEM_LIMIT = 16 * 1024 * 1024

VM = pl.BlockSpec(memory_space=pltpu.VMEM)
SM = pl.BlockSpec(memory_space=pltpu.SMEM)
AN = pl.BlockSpec(memory_space=pl.ANY)


def vm(value):
    return pltpu.with_memory_space_constraint(value, pltpu.VMEM)


def hbm(value):
    return pltpu.with_memory_space_constraint(value, pltpu.HBM)


def call(kernel, out_shape, in_specs, scratch=(), name=None, aliases=None, outs=None):
    outs = outs or jax.tree.map(lambda _: VM, out_shape)
    return pl.pallas_call(
        kernel,
        out_shape=out_shape,
        in_specs=in_specs,
        out_specs=outs,
        scratch_shapes=list(scratch),
        name=name,
        input_output_aliases=aliases or {},
        compiler_params=pltpu.CompilerParams(vmem_limit_bytes=VMEM_LIMIT),
    )


def split3(value):
    high = value.astype(BF16).astype(F32)
    rest = value - high
    middle = rest.astype(BF16).astype(F32)
    return high, middle, rest - middle


def iota(axis):
    return lax.broadcasted_iota(jnp.int32, (ROWS, LANES), axis)


def roll(value, shift, axis):
    return pltpu.roll(value, shift, axis)


def flux_kernel(
    atmos_in, previous_in, index_in, *refs,
):
    staged_in, (packed, *staged) = refs[:STAGED], refs[STAGED : 2 * STAGED + 1]
    blocks, atmos, previous, index, arrivals, stage_arrivals = refs[2 * STAGED + 1 :]
    copies = [pltpu.make_async_copy(index_in, index, arrivals.at[0])]
    copies.append(pltpu.make_async_copy(previous_in, previous, arrivals.at[1]))
    for field in range(4):
        copies.append(
            pltpu.make_async_copy(atmos_in.at[field], atmos.at[field], arrivals.at[2 + field])
        )
    for copy in copies:
        copy.start()
    staging = [
        pltpu.make_async_copy(source, target, stage_arrivals.at[at])
        for at, (source, target) in enumerate(zip(staged_in[1:], staged[1:]))
    ]
    inside = staged[0].at[pl.ds(ROWS, CELLS * ROWS), :]
    staging.append(pltpu.make_async_copy(staged_in[0], inside, stage_arrivals.at[STAGED - 1]))
    for copy in staging:
        copy.start()
    levels = atmos.shape[1]
    row = lax.broadcasted_iota(jnp.int32, (ROWS, levels), 0)
    level = lax.broadcasted_iota(jnp.int32, (ROWS, levels), 1).astype(F32)
    bottom_total = sum(math.exp(-l / 3.0) for l in range(levels))
    radiative_total = sum(math.exp(-l / 24.0) for l in range(levels))
    bottom = split3(jnp.exp(-level / 3.0) / bottom_total)
    radiative = split3(jnp.exp(-level / 24.0) / radiative_total)
    table = jnp.zeros((ROWS, levels), F32)
    for at, part in enumerate(bottom + radiative):
        table = jnp.where(row == at, part, table)
    table = table.astype(BF16)

    def sums(field):
        copies[2 + field].wait()
        return lax.dot_general(
            table, atmos[field], (((1,), (0,)), ((), ())), preferred_element_type=F32
        )

    def low(value):
        return value[0:1] + value[1:2] + value[2:3]

    staged[0][0:ROWS, :] = jnp.zeros((ROWS, LANES), F32)
    staged[0][(CELLS + 1) * ROWS :, :] = jnp.zeros((ROWS, LANES), F32)
    copies[0].wait()
    copies[1].wait()
    temperature = sums(0)
    humidity = sums(1)
    radiation = temperature[3:4] + temperature[4:5] + temperature[5:6]
    east = low(sums(2))
    north = low(sums(3))
    speed = jnp.sqrt(east * east + north * north + 1.0)
    prior = previous[...]
    terms = (
        0.3 * speed * (low(temperature) - prior) + 0.5 * radiation,
        0.3 * speed * (jnp.exp(0.2 * prior) - 1.0 - low(humidity)),
        0.1 * speed * east,
        0.1 * speed * north,
    )
    for term, value in enumerate(terms):
        for block in range(blocks.shape[0]):
            blocks[block, term : term + 1, :] = value[:, block * LANES : (block + 1) * LANES]
    for slot in range(packed.shape[0]):
        packed[slot] = blocks[index[slot % 2, slot // 2]]
    for copy in staging:
        copy.wait()


def tile(ref, at):
    return ref[pl.ds(pl.multiple_of(at * ROWS, ROWS), ROWS), :]


def inside(ref, at):
    return ref[pl.ds(pl.multiple_of((at + 1) * ROWS, ROWS), ROWS), :]


def to_first(value, level):
    return roll(value, lax.rem(LANES - level, LANES), 1)


def to_last(value, level):
    return roll(value, LANES - 1 - level, 1)


def edge_rows():
    core_row = (ROWS - 1) * (1 - lax.rem(lax.axis_index("tile"), 2))
    return ROWS - 1 - core_row, core_row


def first_kernel(
    arrived, slots, weight, tracers, mask,
    zed, core, coefficients, picked, forcing,
):
    pairs = weight.shape[1]
    for row in range(ROWS):
        for pair in range(pairs):
            picked[row // 2, 4 * (row % 2) : 4 * (row % 2) + 4, pair * LANES : (pair + 1) * LANES] = (
                arrived[slots[pair, row]]
            )
    for half in range(ROWS // 2):
        left = jnp.concatenate(split3(picked[half]), axis=0).astype(BF16)
        for parity in range(2):
            row = 2 * half + parity
            right = jnp.concatenate([weight[row, pair] for pair in range(pairs)], axis=1)
            product = lax.dot_general(
                left, right, (((1,), (1,)), ((), ())), preferred_element_type=F32
            )
            product = product[0:8] + product[8:16] + product[16:24]
            for term in range(4):
                at = 4 * parity + term
                forcing[term, row : row + 1, :] = product[at : at + 1]
    sub, lane = iota(0), iota(1)
    wet = mask[...].astype(F32)
    inner = (
        DIFFUSION_RATE * jnp.where(sub == 0, 0.0, wet * roll(wet, 1, 0)),
        DIFFUSION_RATE * jnp.where(sub == ROWS - 1, 0.0, wet * roll(wet, ROWS - 1, 0)),
        DIFFUSION_RATE * jnp.where(lane == 0, 0.0, wet * roll(wet, 1, 1)),
        DIFFUSION_RATE * jnp.where(lane == LANES - 1, 0.0, wet * roll(wet, LANES - 1, 1)),
    )
    total_weight = inner[0] + inner[1] + inner[2] + inner[3]
    stress_east, stress_north = forcing[2], forcing[3]
    stress = jnp.sqrt(stress_east * stress_east + stress_north * stress_north)
    constant = 0.05 * wet
    decaying = 0.15 * wet * (stress / (1.0 + stress))
    surface = [0.5 * wet * forcing[0], 0.5 * wet * forcing[1]]
    for at, value in enumerate(inner + (wet, constant, decaying, surface[0], surface[1])):
        coefficients[at] = value
    for target, row in zip((zed, core), edge_rows()):
        inner_rows = [coefficients[at, pl.ds(row, 1), :] for at in range(9)]
        total_row = inner_rows[0] + inner_rows[1] + inner_rows[2] + inner_rows[3]
        decays = jnp.exp(sub.astype(F32) / -8.0)
        for cell in range(0, CELLS, ROWS):
            level = cell % LEVELS
            start = (cell + 1) * ROWS + row

            def rows(skip, start=start):
                return tracers[pl.ds(start + skip, ROWS, stride=ROWS), :]

            here = rows(0)
            slow = (decays * math.exp(-level / 8.0)) * inner_rows[6]
            fall = (inner_rows[5] + slow) * (rows(ROWS) - here)
            flow = (inner_rows[5] + slow * math.exp(1.0 / 8.0)) * (here - rows(-ROWS))
            if level == 0:
                flow = jnp.where(sub == 0, -inner_rows[7 + cell // LEVELS], flow)
            if level == LEVELS - ROWS:
                fall = jnp.where(sub == ROWS - 1, 0.0, fall)
            value = here - total_row * here + (fall - flow)
            value = value + inner_rows[0] * rows(-1) + inner_rows[1] * rows(1)
            value = value + inner_rows[2] * roll(here, 1, 1)
            value = value + inner_rows[3] * roll(here, LANES - 1, 1)
            target[cell : cell + ROWS, :] = value
            target[BEFORE + cell : BEFORE + cell + ROWS, :] = here
        target[WET:MESSAGE, :] = jnp.broadcast_to(inner_rows[4], (ROWS, LANES))


def column_kernel(tracers, coefficients, west, east):
    lane = iota(1)
    inner = [coefficients[at] for at in range(9)]
    wet, constant, decaying = inner[4], inner[5], inner[6]
    total_weight = inner[0] + inner[1] + inner[2] + inner[3]
    unroll = 8

    def step(group, carry):
        kept = list(carry)
        for inner_level in range(unroll):
            level = group * unroll + inner_level
            spots = [lane == lax.rem(level + skip, LANES) for skip in (0, 1, LANES - 1, LANES - 2)]
            for tracer in range(2):
                turned = roll(inside(tracers, tracer * LEVELS + level), level, 1)
                for place, spot in enumerate(spots):
                    at = 2 * place + tracer
                    kept[at] = jnp.where(spot, turned, kept[at])
        return tuple(kept)

    zero = jnp.zeros((ROWS, LANES), F32)
    kept = list(lax.fori_loop(0, LEVELS // unroll, step, (zero,) * 8))
    for tracer in range(2):
        for place, shift in ((1, LANES - 1), (2, 1), (3, 2)):
            kept[2 * place + tracer] = roll(kept[2 * place + tracer], shift, 1)
    decays = jnp.exp(lane.astype(F32) / -8.0)
    for target, end, at_end, at_next, side in ((west, 0, 0, 2, 3), (east, LANES - 1, 4, 6, 2)):
        cut = slice(end, end + 1)
        rate = constant[:, cut] + decays * decaying[:, cut]
        for tracer in range(2):
            column, beside = kept[at_end + tracer], kept[at_next + tracer]
            fall = rate * (roll(column, LANES - 1, 1) - column)
            fall = jnp.where(lane < LEVELS - 1, fall, 0.0)
            flow = jnp.where(lane == 0, -inner[7 + tracer][:, cut], roll(fall, 1, 1))
            total = column - total_weight[:, cut] * column + (fall - flow)
            total = total + inner[0][:, cut] * roll(column, 1, 0)
            total = total + inner[1][:, cut] * roll(column, ROWS - 1, 0)
            target[tracer] = total + inner[side][:, cut] * beside
            target[2 + tracer] = column
        target[2] = jnp.where(lane == MASK_LANE, wet[:, cut], kept[at_end])
        target[4] = zero


def corner_kernel(zed, core, _, __, west, east):
    lane = lax.broadcasted_iota(jnp.int32, (1, LANES), 1)
    padding = jnp.zeros((LANES - LEVELS, LANES), F32)
    for place, source in enumerate((zed, core)):
        for tracer in range(2):
            start = BEFORE + tracer * LEVELS
            turned = jnp.concatenate([source[start : start + LEVELS, :], padding], axis=0).T
            for target, end in ((west, 0), (east, LANES - 1)):
                row = turned[end : end + 1, :]
                if tracer == 0:
                    row = jnp.where(lane == MASK_LANE, source[WET : WET + 1, end : end + 1], row)
                at = 2 * place + tracer
                target[4, at : at + 1, :] = row


class Rim:
    def __init__(self, own, halo, coefficients):
        self.own, self.halo = own[0:2], halo[0:2]
        own_west, own_east, west, east = own[2], own[3], halo[2], halo[3]
        self.west, self.east = west, east
        sub, lane = iota(0), iota(1)
        self.lane = lane[0:1]
        wet = coefficients[4]
        rows = edge_rows()
        self.inner = [coefficients[at] for at in range(4)]
        wet_rows = [ref[WET : WET + 1, :] for ref in self.halo]
        wet_west = to_first(west[2], MASK_LANE)
        wet_east = to_last(east[2], MASK_LANE)
        self.rows = [
            DIFFUSION_RATE * coefficients[4, pl.ds(row, 1), :] * wet_row
            for row, wet_row in zip(rows, wet_rows)
        ]
        column_west = DIFFUSION_RATE * wet * wet_west
        column_east = DIFFUSION_RATE * wet * wet_east
        zero = jnp.zeros((ROWS, LANES), F32)
        self.border = (
            jnp.where(sub == rows[0], self.rows[0], zero),
            jnp.where(sub == rows[1], self.rows[1], zero),
            jnp.where(lane == 0, column_west, zero),
            jnp.where(lane == LANES - 1, column_east, zero),
        )
        self.inner_total = sum(self.inner)
        self.total = self.inner_total + sum(self.border)
        self.step_west = [west[2 + tracer] - own_west[2 + tracer] for tracer in range(2)]
        self.step_east = [east[2 + tracer] - own_east[2 + tracer] for tracer in range(2)]
        self.corner_weight = []
        for place, wet_row in enumerate(wet_rows):
            mask = slice(2 * place, 2 * place + 1), slice(MASK_LANE, MASK_LANE + 1)
            self.corner_weight.append(
                jnp.where(self.lane == 0, DIFFUSION_RATE * wet_row * west[(4,) + mask], 0.0)
                + jnp.where(self.lane == LANES - 1, DIFFUSION_RATE * wet_row * east[(4,) + mask], 0.0)
            )
        self.side_west, self.side_east = [], []
        for side, tiles, wet_side, column, steps in (
            (self.side_west, west, wet_west[:, 0:1], column_west[:, 0:1], self.step_west),
            (
                self.side_east,
                east,
                wet_east[:, LANES - 1 :],
                column_east[:, LANES - 1 :],
                self.step_east,
            ),
        ):
            for tracer in range(2):
                value = tiles[tracer] - column * steps[tracer]
                for place, row in enumerate(rows):
                    diagonal = tiles[4, 2 * place : 2 * place + 1, MASK_LANE : MASK_LANE + 1]
                    corner = tiles[4, 2 * place + tracer : 2 * place + tracer + 1, :]
                    value = value + jnp.where(
                        sub == row,
                        (DIFFUSION_RATE * wet_side * diagonal) * (corner - tiles[2 + tracer]),
                        0.0,
                    )
                side.append(value)

    def beyond(self, place, now, before, corner):
        halo = self.halo[place]
        old = halo[before, :]
        step = old - self.own[place][before, :]
        edge = halo[now, :] - self.rows[place] * step + self.corner_weight[place] * (corner - old)
        return step, edge

    def after(self, tracers, tracer, level, steps, here, vertical):
        at = pl.multiple_of((tracer * LEVELS + level) * ROWS, ROWS)
        value = here - self.inner_total * here + vertical
        value = value + self.inner[0] * tracers[pl.ds(at + ROWS - 1, ROWS), :]
        value = value + self.inner[1] * tracers[pl.ds(at + ROWS + 1, ROWS), :]
        value = value + self.inner[2] * roll(here, 1, 1)
        value = value + self.inner[3] * roll(here, LANES - 1, 1)
        value = value + self.border[0] * steps[0] + self.border[1] * steps[1]
        value = value + self.border[2] * to_first(self.step_west[tracer], level)
        return value + self.border[3] * to_last(self.step_east[tracer], level)

    def lateral(self, tracer, level, here, edges):
        value = here - self.total * here
        value = value + self.border[0] * edges[0] + self.border[1] * edges[1]
        value = value + self.border[2] * to_first(self.side_west[tracer], level)
        value = value + self.border[3] * to_last(self.side_east[tracer], level)
        value = value + self.inner[0] * roll(here, 1, 0)
        value = value + self.inner[1] * roll(here, ROWS - 1, 0)
        value = value + self.inner[2] * roll(here, 1, 1)
        return value + self.inner[3] * roll(here, LANES - 1, 1)


def reply_kernel(
    tracers, own_zed, own_core, own_west, own_east, zed, core, west, east, coefficients,
    weight, slots, replies,
):
    pairs = weight.shape[1]
    own, halo = (own_zed, own_core, own_west, own_east), (zed, core, west, east)
    rim = Rim(own, halo, coefficients)
    steps, edges = [], []
    for place in range(2):
        row = slice(2 * place, 2 * place + 1)
        corner = jnp.where(rim.lane == 0, west[4, row, 0:1], east[4, row, 0:1])
        step, edge = rim.beyond(place, slice(0, 1), slice(BEFORE, BEFORE + 1), corner)
        steps.append(step)
        edges.append(edge)
    below = slice(BEFORE + 1, BEFORE + 2)
    first, second, third = [inside(tracers, level) for level in range(3)]
    rate = coefficients[5] + coefficients[6]
    rate_below = coefficients[5] + coefficients[6] * math.exp(-1.0 / 8.0)
    flow = rate * (second - first)
    here = rim.after(tracers, 0, 0, steps, first, flow + coefficients[7])
    steps = [rim.halo[at][below, :] - rim.own[at][below, :] for at in range(2)]
    later = rim.after(tracers, 0, 1, steps, second, rate_below * (third - second) - flow)
    fall = rate * (later - here)
    surface = rim.lateral(0, 0, here, edges) + (fall + coefficients[7])
    left = jnp.concatenate(split3(surface) + (jnp.ones((ROWS, LANES), F32),), axis=0).astype(BF16)
    replies[...] = jnp.zeros_like(replies)
    for row in range(ROWS):
        right = jnp.concatenate([weight[row, pair] for pair in range(pairs)], axis=1)
        product = lax.dot_general(left, right, (((1,), (0,)), ((), ())), preferred_element_type=F32)
        numer = product[row : row + 1] + product[8 + row : 9 + row] + product[16 + row : 17 + row]
        denom = product[24:25]
        both = jnp.concatenate([numer, denom], axis=0)
        for pair in range(pairs):
            slot = slots[pair, row]
            replies[slot] = replies[slot] + both[:, pair * LANES : (pair + 1) * LANES]


def final_kernel(
    returned, index, counts, previous, surface,
):
    blocks = previous.shape[0]
    peers = counts.shape[1]
    block = lax.broadcasted_iota(jnp.int32, (blocks, peers), 0)
    numer, denom = 0.0, 0.0
    for place in range(2):
        chosen = (block == index[place : place + 1, :]) & (place < counts[...])
        chosen = chosen.astype(F32).astype(BF16)
        rows = [returned[pl.ds(2 * place + at, peers, stride=4), :] for at in range(2)]
        parts = jnp.concatenate(split3(rows[0]) + split3(rows[1]), axis=1).astype(BF16)
        product = lax.dot_general(
            chosen, parts, (((1,), (0,)), ((), ())), preferred_element_type=F32
        )
        cuts = [product[:, at * LANES : (at + 1) * LANES] for at in range(6)]
        numer = cuts[0] + cuts[1] + cuts[2] + numer
        denom = cuts[3] + cuts[4] + cuts[5] + denom
    surface[...] = (previous[...] + numer) / (1.0 + denom)


def second_kernel(
    tracers, own_zed, own_core, own_west, own_east, zed, core, west, east, coefficients, _,
    output, result, step_core, step_zed, edge_core, edge_zed, sent,
):
    own, halo = (own_zed, own_core, own_west, own_east), (zed, core, west, east)
    rim = Rim(own, halo, coefficients)
    ends = jnp.concatenate([west[4, 0:4, :], east[4, 0:4, :]], axis=0).T
    lane = lax.broadcasted_iota(jnp.int32, (LEVELS, LANES), 1)
    for place, (steps, edges) in enumerate(((step_zed, edge_zed), (step_core, edge_core))):
        for tracer in range(2):
            at = 2 * place + tracer
            corner = jnp.where(lane == 0, ends[0:LEVELS, at : at + 1], ends[0:LEVELS, at + 4 : at + 5])
            now = slice(tracer * LEVELS, (tracer + 1) * LEVELS)
            before = slice(BEFORE + tracer * LEVELS, BEFORE + (tracer + 1) * LEVELS)
            steps[now, :], edges[now, :] = rim.beyond(place, now, before, corner)
    constant, decaying = coefficients[5], coefficients[6]
    unroll, parts = 4, 4
    decay = [math.exp(-inner_level / 8.0) for inner_level in range(unroll + 1)]

    def pick(refs, tracer, level):
        return [ref[pl.ds(tracer * LEVELS + level, 1), :] for ref in refs]

    def after(tracer, level, here, flow, rate):
        below = inside(tracers, tracer * LEVELS + jnp.minimum(level + 1, LEVELS - 1))
        fall = rate * (below - here)
        steps = pick((step_zed, step_core), tracer, level)
        return rim.after(tracers, tracer, level, steps, here, fall - flow), below, fall

    def step(group, carry):
        now, flow, state, fell, depth = [list(value) for value in carry[:4]] + [carry[4]]
        for inner_level in range(unroll):
            level = group * unroll + inner_level
            later = jnp.minimum(level + 1, LEVELS - 1)
            rate = constant + depth * decay[inner_level]
            rate_below = constant + depth * decay[inner_level + 1]
            for tracer in range(2):
                here = now[tracer]
                below, state[tracer], fell[tracer] = after(
                    tracer, later, state[tracer], fell[tracer], rate_below
                )
                fall = jnp.where(level < LEVELS - 1, rate * (below - here), 0.0)
                edges = pick((edge_zed, edge_core), tracer, level)
                total = rim.lateral(tracer, level, here, edges) + (fall - flow[tracer])
                at = pl.multiple_of((tracer * LEVELS + level) * ROWS, ROWS)
                result[pl.ds(at, ROWS), :] = total
                now[tracer] = below
                flow[tracer] = fall
        return tuple(now), tuple(flow), tuple(state), tuple(fell), depth * decay[unroll]

    starts = [
        after(tracer, 0, inside(tracers, tracer * LEVELS), -coefficients[7 + tracer], constant + decaying)
        for tracer in range(2)
    ]
    now, state, fell = zip(*starts)
    carry = (now, (-coefficients[7], -coefficients[8]), state, fell, decaying)
    groups = LEVELS // unroll // parts
    copies = []
    for part in range(parts):
        carry = lax.fori_loop(part * groups, (part + 1) * groups, step, carry)
        count = groups * unroll * ROWS
        for tracer in range(2):
            at = pl.ds(tracer * LEVELS * ROWS + part * count, count)
            copies.append(
                pltpu.make_async_copy(result.at[at, :], output.at[at, :], sent.at[len(copies)])
            )
            copies[-1].start()
    for copy in copies:
        copy.wait()


def shards(
    atmos_profile_state,
    previous_surface_temp,
    outbound_block_index,
    outbound_slot_counts,
    pair_source_slot,
    overlay_weight,
    ocean_tracer_state,
    ocean_cell_mask,
):
    peers, levs = lax.axis_size("tile"), lax.axis_size("lev")
    slot_total = 2 * peers
    blocks = previous_surface_temp.shape[0] // LANES
    shape = jax.ShapeDtypeStruct
    index = outbound_block_index.T
    slots = pair_source_slot.T
    tracers = ocean_tracer_state.reshape(CELLS * ROWS, LANES)
    prior = previous_surface_temp.reshape(1, -1)
    square = previous_surface_temp.reshape(blocks, LANES)

    staged = (tracers, overlay_weight, ocean_cell_mask, slots, index, outbound_slot_counts, square)
    packed, *staged = call(
        flux_kernel,
        (pltpu.VMEM((slot_total, 4, LANES), F32),)
        + (pltpu.VMEM(((CELLS + 2) * ROWS, LANES), F32),)
        + tuple(pltpu.VMEM(value.shape, value.dtype) for value in staged[1:]),
        [AN] * (3 + STAGED),
        [
            pltpu.VMEM((blocks, 4, LANES), F32),
            pltpu.VMEM(atmos_profile_state.shape, BF16),
            pltpu.VMEM(prior.shape, F32),
            pltpu.SMEM(index.shape, jnp.int32),
            pltpu.SemaphoreType.DMA((6,)),
            pltpu.SemaphoreType.DMA((STAGED,)),
        ],
        "flux",
        outs=(VM,) * (1 + STAGED),
    )(hbm(atmos_profile_state), hbm(prior), hbm(index), *[hbm(value) for value in staged])
    tracers, weight, mask, slots, index, counts, square = staged
    arrived = lax.all_to_all(packed, "tile", split_axis=0, concat_axis=0, tiled=True)

    row_message, column_message = shape((MESSAGE, LANES), F32), shape((5, ROWS, LANES), F32)
    zed, core, coefficients = call(
        first_kernel,
        (
            row_message,
            row_message,
            shape((9, ROWS, LANES), F32),
        ),
        [VM, SM] + [VM] * 3,
        [pltpu.VMEM((ROWS // 2, ROWS, 4 * LANES), F32), pltpu.VMEM((4, ROWS, LANES), F32)],
        "first",
    )(vm(arrived), slots, vm(weight), vm(tracers), vm(mask))
    across = [(i, i + 1) for i in range(1, peers - 1, 2)]
    across += [(target, source) for source, target in across]
    halo_core = vm(lax.ppermute(core, "tile", [(i, i ^ 1) for i in range(peers)]))
    halo_zed = vm(lax.ppermute(zed, "tile", across))
    west, east = call(
        column_kernel,
        (column_message, column_message),
        [VM] * 2,
        (),
        "columns",
    )(vm(tracers), vm(coefficients))
    west, east = call(
        corner_kernel,
        (column_message, column_message),
        [VM] * 4,
        (),
        "corner",
        {2: 0, 3: 1},
    )(halo_zed, halo_core, vm(west), vm(east))
    halo_west = vm(lax.ppermute(east, "lev", [(i, i + 1) for i in range(levs - 1)]))
    halo_east = vm(lax.ppermute(west, "lev", [(i + 1, i) for i in range(levs - 1)]))
    edges = [
        vm(value)
        for value in (
            tracers, zed, core, west, east, halo_zed, halo_core, halo_west, halo_east, coefficients,
        )
    ]
    replies = call(
        reply_kernel,
        shape((slot_total, 2, LANES), F32),
        [VM] * 11 + [SM],
        (),
        "reply",
    )(*edges, vm(weight), slots)
    returned = lax.all_to_all(replies, "tile", split_axis=0, concat_axis=0, tiled=True)
    output = call(
        second_kernel,
        shape((CELLS * ROWS, LANES), F32),
        [VM] * 10 + [AN],
        [pltpu.VMEM((CELLS * ROWS, LANES), F32)]
        + [pltpu.VMEM((CELLS, LANES), F32)] * 4
        + [pltpu.SemaphoreType.DMA((8,))],
        "second",
        outs=AN,
    )(*edges, replies)
    surface = call(
        final_kernel,
        shape((blocks, LANES), F32),
        [VM] * 4,
        (),
        "final",
    )(vm(returned.reshape(2 * slot_total, LANES)), vm(index), vm(counts), vm(square))
    return (output.reshape(ocean_tracer_state.shape), surface.reshape(-1))


def solution(mesh):
    placed = (
        P(None, None, ("sec", "tile", "lev")),
        P(("sec", "tile", "lev")),
        P(("sec", "tile", "lev"), None),
        P(("sec", "tile", "lev"), None),
        P(("sec", "tile", "lev"), None),
        P(("sec", "tile", "lev"), None, None, None),
        P(None, None, ("sec", "tile"), "lev"),
        P(("sec", "tile"), "lev"),
    )
    return jax.shard_map(
        shards,
        mesh=mesh,
        in_specs=placed,
        out_specs=(P(None, None, ("sec", "tile"), "lev"), P(("sec", "tile", "lev"))),
        check_vma=False,
    )
```

```python
import math

import jax
import jax.numpy as jnp
from jax import lax
from jax.experimental import pallas as pl
from jax.experimental.pallas import tpu as pltpu
from jax.sharding import PartitionSpec as P

F32 = jnp.float32
BF16 = jnp.bfloat16
DIFFUSION_RATE = 0.15
LANES = 128
ROWS = 8
LEVELS = 80
MASK_LANE = LEVELS
CELLS = 2 * LEVELS
BEFORE = CELLS
WET = 2 * CELLS
MESSAGE = WET + ROWS
STAGED = 7
VMEM_LIMIT = 16 * 1024 * 1024

VM = pl.BlockSpec(memory_space=pltpu.VMEM)
SM = pl.BlockSpec(memory_space=pltpu.SMEM)
AN = pl.BlockSpec(memory_space=pl.ANY)


def vm(value):
    return pltpu.with_memory_space_constraint(value, pltpu.VMEM)


def hbm(value):
    return pltpu.with_memory_space_constraint(value, pltpu.HBM)


def call(kernel, out_shape, in_specs, scratch=(), name=None, aliases=None, outs=None):
    outs = outs or jax.tree.map(lambda _: VM, out_shape)
    return pl.pallas_call(
        kernel,
        out_shape=out_shape,
        in_specs=in_specs,
        out_specs=outs,
        scratch_shapes=list(scratch),
        name=name,
        input_output_aliases=aliases or {},
        compiler_params=pltpu.CompilerParams(vmem_limit_bytes=VMEM_LIMIT),
    )


def split3(value):
    high = value.astype(BF16).astype(F32)
    rest = value - high
    middle = rest.astype(BF16).astype(F32)
    return high, middle, rest - middle


def iota(axis):
    return lax.broadcasted_iota(jnp.int32, (ROWS, LANES), axis)


def roll(value, shift, axis):
    return pltpu.roll(value, shift, axis)


def flux_kernel(
    atmos_in, previous_in, index_in, *refs,
):
    staged_in, (packed, *staged) = refs[:STAGED], refs[STAGED : 2 * STAGED + 1]
    blocks, atmos, previous, index, arrivals, stage_arrivals = refs[2 * STAGED + 1 :]
    copies = [pltpu.make_async_copy(index_in, index, arrivals.at[0])]
    copies.append(pltpu.make_async_copy(previous_in, previous, arrivals.at[1]))
    for field in range(4):
        copies.append(
            pltpu.make_async_copy(atmos_in.at[field], atmos.at[field], arrivals.at[2 + field])
        )
    for copy in copies:
        copy.start()
    staging = [
        pltpu.make_async_copy(source, target, stage_arrivals.at[at])
        for at, (source, target) in enumerate(zip(staged_in[1:], staged[1:]))
    ]
    inside = staged[0].at[pl.ds(ROWS, CELLS * ROWS), :]
    staging.append(pltpu.make_async_copy(staged_in[0], inside, stage_arrivals.at[STAGED - 1]))
    for copy in staging:
        copy.start()
    levels = atmos.shape[1]
    row = lax.broadcasted_iota(jnp.int32, (ROWS, levels), 0)
    level = lax.broadcasted_iota(jnp.int32, (ROWS, levels), 1).astype(F32)
    bottom_total = sum(math.exp(-l / 3.0) for l in range(levels))
    radiative_total = sum(math.exp(-l / 24.0) for l in range(levels))
    bottom = split3(jnp.exp(-level / 3.0) / bottom_total)
    radiative = split3(jnp.exp(-level / 24.0) / radiative_total)
    table = jnp.zeros((ROWS, levels), F32)
    for at, part in enumerate(bottom + radiative):
        table = jnp.where(row == at, part, table)
    table = table.astype(BF16)

    def sums(field):
        copies[2 + field].wait()
        return lax.dot_general(
            table, atmos[field], (((1,), (0,)), ((), ())), preferred_element_type=F32
        )

    def low(value):
        return value[0:1] + value[1:2] + value[2:3]

    staged[0][0:ROWS, :] = jnp.zeros((ROWS, LANES), F32)
    staged[0][(CELLS + 1) * ROWS :, :] = jnp.zeros((ROWS, LANES), F32)
    copies[0].wait()
    copies[1].wait()
    temperature = sums(0)
    humidity = sums(1)
    radiation = temperature[3:4] + temperature[4:5] + temperature[5:6]
    east = low(sums(2))
    north = low(sums(3))
    speed = jnp.sqrt(east * east + north * north + 1.0)
    prior = previous[...]
    terms = (
        0.3 * speed * (low(temperature) - prior) + 0.5 * radiation,
        0.3 * speed * (jnp.exp(0.2 * prior) - 1.0 - low(humidity)),
        0.1 * speed * east,
        0.1 * speed * north,
    )
    for term, value in enumerate(terms):
        for block in range(blocks.shape[0]):
            blocks[block, term : term + 1, :] = value[:, block * LANES : (block + 1) * LANES]
    for slot in range(packed.shape[0]):
        packed[slot] = blocks[index[slot % 2, slot // 2]]
    for copy in staging:
        copy.wait()


def tile(ref, at):
    return ref[pl.ds(pl.multiple_of(at * ROWS, ROWS), ROWS), :]


def inside(ref, at):
    return ref[pl.ds(pl.multiple_of((at + 1) * ROWS, ROWS), ROWS), :]


def to_first(value, level):
    return roll(value, lax.rem(LANES - level, LANES), 1)


def to_last(value, level):
    return roll(value, LANES - 1 - level, 1)


def edge_rows():
    core_row = (ROWS - 1) * (1 - lax.rem(lax.axis_index("tile"), 2))
    return ROWS - 1 - core_row, core_row


def first_kernel(
    arrived, slots, weight, tracers, mask,
    zed, core, coefficients, picked, forcing,
):
    pairs = weight.shape[1]
    for row in range(ROWS):
        for pair in range(pairs):
            picked[row // 2, 4 * (row % 2) : 4 * (row % 2) + 4, pair * LANES : (pair + 1) * LANES] = (
                arrived[slots[pair, row]]
            )
    for half in range(ROWS // 2):
        left = jnp.concatenate(split3(picked[half]), axis=0).astype(BF16)
        for parity in range(2):
            row = 2 * half + parity
            right = jnp.concatenate([weight[row, pair] for pair in range(pairs)], axis=1)
            product = lax.dot_general(
                left, right, (((1,), (1,)), ((), ())), preferred_element_type=F32
            )
            product = product[0:8] + product[8:16] + product[16:24]
            for term in range(4):
                at = 4 * parity + term
                forcing[term, row : row + 1, :] = product[at : at + 1]
    sub, lane = iota(0), iota(1)
    wet = mask[...].astype(F32)
    inner = (
        DIFFUSION_RATE * jnp.where(sub == 0, 0.0, wet * roll(wet, 1, 0)),
        DIFFUSION_RATE * jnp.where(sub == ROWS - 1, 0.0, wet * roll(wet, ROWS - 1, 0)),
        DIFFUSION_RATE * jnp.where(lane == 0, 0.0, wet * roll(wet, 1, 1)),
        DIFFUSION_RATE * jnp.where(lane == LANES - 1, 0.0, wet * roll(wet, LANES - 1, 1)),
    )
    total_weight = inner[0] + inner[1] + inner[2] + inner[3]
    stress_east, stress_north = forcing[2], forcing[3]
    stress = jnp.sqrt(stress_east * stress_east + stress_north * stress_north)
    constant = 0.05 * wet
    decaying = 0.15 * wet * (stress / (1.0 + stress))
    surface = [0.5 * wet * forcing[0], 0.5 * wet * forcing[1]]
    for at, value in enumerate(inner + (wet, constant, decaying, surface[0], surface[1])):
        coefficients[at] = value
    for target, row in zip((zed, core), edge_rows()):
        inner_rows = [coefficients[at, pl.ds(row, 1), :] for at in range(9)]
        total_row = inner_rows[0] + inner_rows[1] + inner_rows[2] + inner_rows[3]
        decays = jnp.exp(sub.astype(F32) / -8.0)
        for cell in range(0, CELLS, ROWS):
            level = cell % LEVELS
            start = (cell + 1) * ROWS + row

            def rows(skip, start=start):
                return tracers[pl.ds(start + skip, ROWS, stride=ROWS), :]

            here = rows(0)
            slow = (decays * math.exp(-level / 8.0)) * inner_rows[6]
            fall = (inner_rows[5] + slow) * (rows(ROWS) - here)
            flow = (inner_rows[5] + slow * math.exp(1.0 / 8.0)) * (here - rows(-ROWS))
            if level == 0:
                flow = jnp.where(sub == 0, -inner_rows[7 + cell // LEVELS], flow)
            if level == LEVELS - ROWS:
                fall = jnp.where(sub == ROWS - 1, 0.0, fall)
            value = here - total_row * here + (fall - flow)
            value = value + inner_rows[0] * rows(-1) + inner_rows[1] * rows(1)
            value = value + inner_rows[2] * roll(here, 1, 1)
            value = value + inner_rows[3] * roll(here, LANES - 1, 1)
            target[cell : cell + ROWS, :] = value
            target[BEFORE + cell : BEFORE + cell + ROWS, :] = here
        target[WET:MESSAGE, :] = jnp.broadcast_to(inner_rows[4], (ROWS, LANES))


def column_kernel(tracers, coefficients, west, east):
    lane = iota(1)
    inner = [coefficients[at] for at in range(9)]
    wet, constant, decaying = inner[4], inner[5], inner[6]
    total_weight = inner[0] + inner[1] + inner[2] + inner[3]
    unroll = 8

    def step(group, carry):
        kept = list(carry)
        for inner_level in range(unroll):
            level = group * unroll + inner_level
            spots = [lane == lax.rem(level + skip, LANES) for skip in (0, 1, LANES - 1, LANES - 2)]
            for tracer in range(2):
                turned = roll(inside(tracers, tracer * LEVELS + level), level, 1)
                for place, spot in enumerate(spots):
                    at = 2 * place + tracer
                    kept[at] = jnp.where(spot, turned, kept[at])
        return tuple(kept)

    zero = jnp.zeros((ROWS, LANES), F32)
    kept = list(lax.fori_loop(0, LEVELS // unroll, step, (zero,) * 8))
    for tracer in range(2):
        for place, shift in ((1, LANES - 1), (2, 1), (3, 2)):
            kept[2 * place + tracer] = roll(kept[2 * place + tracer], shift, 1)
    decays = jnp.exp(lane.astype(F32) / -8.0)
    for target, end, at_end, at_next, side in ((west, 0, 0, 2, 3), (east, LANES - 1, 4, 6, 2)):
        cut = slice(end, end + 1)
        rate = constant[:, cut] + decays * decaying[:, cut]
        for tracer in range(2):
            column, beside = kept[at_end + tracer], kept[at_next + tracer]
            fall = rate * (roll(column, LANES - 1, 1) - column)
            fall = jnp.where(lane < LEVELS - 1, fall, 0.0)
            flow = jnp.where(lane == 0, -inner[7 + tracer][:, cut], roll(fall, 1, 1))
            total = column - total_weight[:, cut] * column + (fall - flow)
            total = total + inner[0][:, cut] * roll(column, 1, 0)
            total = total + inner[1][:, cut] * roll(column, ROWS - 1, 0)
            target[tracer] = total + inner[side][:, cut] * beside
            target[2 + tracer] = column
        target[2] = jnp.where(lane == MASK_LANE, wet[:, cut], kept[at_end])
        target[4] = zero


def corner_kernel(zed, core, _, __, west, east):
    lane = lax.broadcasted_iota(jnp.int32, (1, LANES), 1)
    padding = jnp.zeros((LANES - LEVELS, LANES), F32)
    for place, source in enumerate((zed, core)):
        for tracer in range(2):
            start = BEFORE + tracer * LEVELS
            turned = jnp.concatenate([source[start : start + LEVELS, :], padding], axis=0).T
            for target, end in ((west, 0), (east, LANES - 1)):
                row = turned[end : end + 1, :]
                if tracer == 0:
                    row = jnp.where(lane == MASK_LANE, source[WET : WET + 1, end : end + 1], row)
                at = 2 * place + tracer
                target[4, at : at + 1, :] = row


class Rim:
    def __init__(self, own, halo, coefficients):
        self.own, self.halo = own[0:2], halo[0:2]
        own_west, own_east, west, east = own[2], own[3], halo[2], halo[3]
        self.west, self.east = west, east
        sub, lane = iota(0), iota(1)
        self.lane = lane[0:1]
        wet = coefficients[4]
        rows = edge_rows()
        self.inner = [coefficients[at] for at in range(4)]
        wet_rows = [ref[WET : WET + 1, :] for ref in self.halo]
        wet_west = to_first(west[2], MASK_LANE)
        wet_east = to_last(east[2], MASK_LANE)
        self.rows = [
            DIFFUSION_RATE * coefficients[4, pl.ds(row, 1), :] * wet_row
            for row, wet_row in zip(rows, wet_rows)
        ]
        column_west = DIFFUSION_RATE * wet * wet_west
        column_east = DIFFUSION_RATE * wet * wet_east
        zero = jnp.zeros((ROWS, LANES), F32)
        self.border = (
            jnp.where(sub == rows[0], self.rows[0], zero),
            jnp.where(sub == rows[1], self.rows[1], zero),
            jnp.where(lane == 0, column_west, zero),
            jnp.where(lane == LANES - 1, column_east, zero),
        )
        self.inner_total = sum(self.inner)
        self.total = self.inner_total + sum(self.border)
        self.step_west = [west[2 + tracer] - own_west[2 + tracer] for tracer in range(2)]
        self.step_east = [east[2 + tracer] - own_east[2 + tracer] for tracer in range(2)]
        self.corner_weight = []
        for place, wet_row in enumerate(wet_rows):
            mask = slice(2 * place, 2 * place + 1), slice(MASK_LANE, MASK_LANE + 1)
            self.corner_weight.append(
                jnp.where(self.lane == 0, DIFFUSION_RATE * wet_row * west[(4,) + mask], 0.0)
                + jnp.where(self.lane == LANES - 1, DIFFUSION_RATE * wet_row * east[(4,) + mask], 0.0)
            )
        self.side_west, self.side_east = [], []
        for side, tiles, wet_side, column, steps in (
            (self.side_west, west, wet_west[:, 0:1], column_west[:, 0:1], self.step_west),
            (
                self.side_east,
                east,
                wet_east[:, LANES - 1 :],
                column_east[:, LANES - 1 :],
                self.step_east,
            ),
        ):
            for tracer in range(2):
                value = tiles[tracer] - column * steps[tracer]
                for place, row in enumerate(rows):
                    diagonal = tiles[4, 2 * place : 2 * place + 1, MASK_LANE : MASK_LANE + 1]
                    corner = tiles[4, 2 * place + tracer : 2 * place + tracer + 1, :]
                    value = value + jnp.where(
                        sub == row,
                        (DIFFUSION_RATE * wet_side * diagonal) * (corner - tiles[2 + tracer]),
                        0.0,
                    )
                side.append(value)

    def beyond(self, place, now, before, corner):
        halo = self.halo[place]
        old = halo[before, :]
        step = old - self.own[place][before, :]
        edge = halo[now, :] - self.rows[place] * step + self.corner_weight[place] * (corner - old)
        return step, edge

    def after(self, tracers, tracer, level, steps, here, vertical):
        at = pl.multiple_of((tracer * LEVELS + level) * ROWS, ROWS)
        value = here - self.inner_total * here + vertical
        value = value + self.inner[0] * tracers[pl.ds(at + ROWS - 1, ROWS), :]
        value = value + self.inner[1] * tracers[pl.ds(at + ROWS + 1, ROWS), :]
        value = value + self.inner[2] * roll(here, 1, 1)
        value = value + self.inner[3] * roll(here, LANES - 1, 1)
        value = value + self.border[0] * steps[0] + self.border[1] * steps[1]
        value = value + self.border[2] * to_first(self.step_west[tracer], level)
        return value + self.border[3] * to_last(self.step_east[tracer], level)

    def lateral(self, tracer, level, here, edges):
        value = here - self.total * here
        value = value + self.border[0] * edges[0] + self.border[1] * edges[1]
        value = value + self.border[2] * to_first(self.side_west[tracer], level)
        value = value + self.border[3] * to_last(self.side_east[tracer], level)
        value = value + self.inner[0] * roll(here, 1, 0)
        value = value + self.inner[1] * roll(here, ROWS - 1, 0)
        value = value + self.inner[2] * roll(here, 1, 1)
        return value + self.inner[3] * roll(here, LANES - 1, 1)


def reply_kernel(
    tracers, own_zed, own_core, own_west, own_east, zed, core, west, east, coefficients,
    weight, slots, replies,
):
    pairs = weight.shape[1]
    own, halo = (own_zed, own_core, own_west, own_east), (zed, core, west, east)
    rim = Rim(own, halo, coefficients)
    steps, edges = [], []
    for place in range(2):
        row = slice(2 * place, 2 * place + 1)
        corner = jnp.where(rim.lane == 0, west[4, row, 0:1], east[4, row, 0:1])
        step, edge = rim.beyond(place, slice(0, 1), slice(BEFORE, BEFORE + 1), corner)
        steps.append(step)
        edges.append(edge)
    below = slice(BEFORE + 1, BEFORE + 2)
    first, second, third = [inside(tracers, level) for level in range(3)]
    rate = coefficients[5] + coefficients[6]
    rate_below = coefficients[5] + coefficients[6] * math.exp(-1.0 / 8.0)
    flow = rate * (second - first)
    here = rim.after(tracers, 0, 0, steps, first, flow + coefficients[7])
    steps = [rim.halo[at][below, :] - rim.own[at][below, :] for at in range(2)]
    later = rim.after(tracers, 0, 1, steps, second, rate_below * (third - second) - flow)
    fall = rate * (later - here)
    surface = rim.lateral(0, 0, here, edges) + (fall + coefficients[7])
    left = jnp.concatenate(split3(surface) + (jnp.ones((ROWS, LANES), F32),), axis=0).astype(BF16)
    replies[...] = jnp.zeros_like(replies)
    for row in range(ROWS):
        right = jnp.concatenate([weight[row, pair] for pair in range(pairs)], axis=1)
        product = lax.dot_general(left, right, (((1,), (0,)), ((), ())), preferred_element_type=F32)
        numer = product[row : row + 1] + product[8 + row : 9 + row] + product[16 + row : 17 + row]
        denom = product[24:25]
        both = jnp.concatenate([numer, denom], axis=0)
        for pair in range(pairs):
            slot = slots[pair, row]
            replies[slot] = replies[slot] + both[:, pair * LANES : (pair + 1) * LANES]


def final_kernel(
    returned, index, counts, previous, surface,
):
    blocks = previous.shape[0]
    peers = counts.shape[1]
    block = lax.broadcasted_iota(jnp.int32, (blocks, peers), 0)
    numer, denom = 0.0, 0.0
    for place in range(2):
        chosen = (block == index[place : place + 1, :]) & (place < counts[...])
        chosen = chosen.astype(F32).astype(BF16)
        rows = [returned[pl.ds(2 * place + at, peers, stride=4), :] for at in range(2)]
        parts = jnp.concatenate(split3(rows[0]) + split3(rows[1]), axis=1).astype(BF16)
        product = lax.dot_general(
            chosen, parts, (((1,), (0,)), ((), ())), preferred_element_type=F32
        )
        cuts = [product[:, at * LANES : (at + 1) * LANES] for at in range(6)]
        numer = cuts[0] + cuts[1] + cuts[2] + numer
        denom = cuts[3] + cuts[4] + cuts[5] + denom
    surface[...] = (previous[...] + numer) / (1.0 + denom)


def second_kernel(
    tracers, own_zed, own_core, own_west, own_east, zed, core, west, east, coefficients, _,
    output, result, step_core, step_zed, edge_core, edge_zed, sent,
):
    own, halo = (own_zed, own_core, own_west, own_east), (zed, core, west, east)
    rim = Rim(own, halo, coefficients)
    ends = jnp.concatenate([west[4, 0:4, :], east[4, 0:4, :]], axis=0).T
    lane = lax.broadcasted_iota(jnp.int32, (LEVELS, LANES), 1)
    for place, (steps, edges) in enumerate(((step_zed, edge_zed), (step_core, edge_core))):
        for tracer in range(2):
            at = 2 * place + tracer
            corner = jnp.where(lane == 0, ends[0:LEVELS, at : at + 1], ends[0:LEVELS, at + 4 : at + 5])
            now = slice(tracer * LEVELS, (tracer + 1) * LEVELS)
            before = slice(BEFORE + tracer * LEVELS, BEFORE + (tracer + 1) * LEVELS)
            steps[now, :], edges[now, :] = rim.beyond(place, now, before, corner)
    constant, decaying = coefficients[5], coefficients[6]
    unroll, parts = 4, 4
    decay = [math.exp(-inner_level / 8.0) for inner_level in range(unroll + 1)]

    def pick(refs, tracer, level):
        return [ref[pl.ds(tracer * LEVELS + level, 1), :] for ref in refs]

    def after(tracer, level, here, flow, rate):
        below = inside(tracers, tracer * LEVELS + jnp.minimum(level + 1, LEVELS - 1))
        fall = rate * (below - here)
        steps = pick((step_zed, step_core), tracer, level)
        return rim.after(tracers, tracer, level, steps, here, fall - flow), below, fall

    def step(group, carry):
        now, flow, state, fell, depth = [list(value) for value in carry[:4]] + [carry[4]]
        for inner_level in range(unroll):
            level = group * unroll + inner_level
            later = jnp.minimum(level + 1, LEVELS - 1)
            rate = constant + depth * decay[inner_level]
            rate_below = constant + depth * decay[inner_level + 1]
            for tracer in range(2):
                here = now[tracer]
                below, state[tracer], fell[tracer] = after(
                    tracer, later, state[tracer], fell[tracer], rate_below
                )
                fall = jnp.where(level < LEVELS - 1, rate * (below - here), 0.0)
                edges = pick((edge_zed, edge_core), tracer, level)
                total = rim.lateral(tracer, level, here, edges) + (fall - flow[tracer])
                at = pl.multiple_of((tracer * LEVELS + level) * ROWS, ROWS)
                result[pl.ds(at, ROWS), :] = total
                now[tracer] = below
                flow[tracer] = fall
        return tuple(now), tuple(flow), tuple(state), tuple(fell), depth * decay[unroll]

    starts = [
        after(tracer, 0, inside(tracers, tracer * LEVELS), -coefficients[7 + tracer], constant + decaying)
        for tracer in range(2)
    ]
    now, state, fell = zip(*starts)
    carry = (now, (-coefficients[7], -coefficients[8]), state, fell, decaying)
    groups = LEVELS // unroll // parts
    copies = []
    for part in range(parts):
        carry = lax.fori_loop(part * groups, (part + 1) * groups, step, carry)
        count = groups * unroll * ROWS
        for tracer in range(2):
            at = pl.ds(tracer * LEVELS * ROWS + part * count, count)
            copies.append(
                pltpu.make_async_copy(result.at[at, :], output.at[at, :], sent.at[len(copies)])
            )
            copies[-1].start()
    for copy in copies:
        copy.wait()


def shards(
    atmos_profile_state,
    previous_surface_temp,
    outbound_block_index,
    outbound_slot_counts,
    pair_source_slot,
    overlay_weight,
    ocean_tracer_state,
    ocean_cell_mask,
):
    peers, levs = lax.axis_size("tile"), lax.axis_size("lev")
    slot_total = 2 * peers
    blocks = previous_surface_temp.shape[0] // LANES
    shape = jax.ShapeDtypeStruct
    index = outbound_block_index.T
    slots = pair_source_slot.T
    tracers = ocean_tracer_state.reshape(CELLS * ROWS, LANES)
    prior = previous_surface_temp.reshape(1, -1)
    square = previous_surface_temp.reshape(blocks, LANES)

    staged = (tracers, overlay_weight, ocean_cell_mask, slots, index, outbound_slot_counts, square)
    packed, *staged = call(
        flux_kernel,
        (pltpu.VMEM((slot_total, 4, LANES), F32),)
        + (pltpu.VMEM(((CELLS + 2) * ROWS, LANES), F32),)
        + tuple(
            (pltpu.SMEM if value is slots else pltpu.VMEM)(value.shape, value.dtype)
            for value in staged[1:]
        ),
        [AN] * (3 + STAGED),
        [
            pltpu.VMEM((blocks, 4, LANES), F32),
            pltpu.VMEM(atmos_profile_state.shape, BF16),
            pltpu.VMEM(prior.shape, F32),
            pltpu.SMEM(index.shape, jnp.int32),
            pltpu.SemaphoreType.DMA((6,)),
            pltpu.SemaphoreType.DMA((STAGED,)),
        ],
        "flux",
        outs=(VM,) * 4 + (SM,) + (VM,) * (STAGED - 4),
    )(hbm(atmos_profile_state), hbm(prior), hbm(index), *[hbm(value) for value in staged])
    tracers, weight, mask, slots, index, counts, square = staged
    slots = pltpu.with_memory_space_constraint(slots, pltpu.SMEM)
    arrived = lax.all_to_all(packed, "tile", split_axis=0, concat_axis=0, tiled=True)

    row_message, column_message = shape((MESSAGE, LANES), F32), shape((5, ROWS, LANES), F32)
    zed, core, coefficients = call(
        first_kernel,
        (
            row_message,
            row_message,
            shape((9, ROWS, LANES), F32),
        ),
        [VM, SM] + [VM] * 3,
        [pltpu.VMEM((ROWS // 2, ROWS, 4 * LANES), F32), pltpu.VMEM((4, ROWS, LANES), F32)],
        "first",
    )(vm(arrived), slots, vm(weight), vm(tracers), vm(mask))
    across = [(i, i + 1) for i in range(1, peers - 1, 2)]
    across += [(target, source) for source, target in across]
    halo_core = vm(lax.ppermute(core, "tile", [(i, i ^ 1) for i in range(peers)]))
    halo_zed = vm(lax.ppermute(zed, "tile", across))
    west, east = call(
        column_kernel,
        (column_message, column_message),
        [VM] * 2,
        (),
        "columns",
    )(vm(tracers), vm(coefficients))
    west, east = call(
        corner_kernel,
        (column_message, column_message),
        [VM] * 4,
        (),
        "corner",
        {2: 0, 3: 1},
    )(halo_zed, halo_core, vm(west), vm(east))
    halo_west = vm(lax.ppermute(east, "lev", [(i, i + 1) for i in range(levs - 1)]))
    halo_east = vm(lax.ppermute(west, "lev", [(i + 1, i) for i in range(levs - 1)]))
    edges = [
        vm(value)
        for value in (
            tracers, zed, core, west, east, halo_zed, halo_core, halo_west, halo_east, coefficients,
        )
    ]
    replies = call(
        reply_kernel,
        shape((slot_total, 2, LANES), F32),
        [VM] * 11 + [SM],
        (),
        "reply",
    )(*edges, vm(weight), slots)
    returned = lax.all_to_all(replies, "tile", split_axis=0, concat_axis=0, tiled=True)
    output = call(
        second_kernel,
        shape((CELLS * ROWS, LANES), F32),
        [VM] * 10 + [AN],
        [pltpu.VMEM((CELLS * ROWS, LANES), F32)]
        + [pltpu.VMEM((CELLS, LANES), F32)] * 4
        + [pltpu.SemaphoreType.DMA((8,))],
        "second",
        outs=AN,
    )(*edges, replies)
    surface = call(
        final_kernel,
        shape((blocks, LANES), F32),
        [VM] * 4,
        (),
        "final",
    )(vm(returned.reshape(2 * slot_total, LANES)), vm(index), vm(counts), vm(square))
    return (output.reshape(ocean_tracer_state.shape), surface.reshape(-1))


def solution(mesh):
    placed = (
        P(None, None, ("sec", "tile", "lev")),
        P(("sec", "tile", "lev")),
        P(("sec", "tile", "lev"), None),
        P(("sec", "tile", "lev"), None),
        P(("sec", "tile", "lev"), None),
        P(("sec", "tile", "lev"), None, None, None),
        P(None, None, ("sec", "tile"), "lev"),
        P(("sec", "tile"), "lev"),
    )
    return jax.shard_map(
        shards,
        mesh=mesh,
        in_specs=placed,
        out_specs=(P(None, None, ("sec", "tile"), "lev"), P(("sec", "tile", "lev"))),
        check_vma=False,
    )
```

```python
import math

import jax
import jax.numpy as jnp
from jax import lax
from jax.experimental import pallas as pl
from jax.experimental.pallas import tpu as pltpu
from jax.sharding import PartitionSpec as P

F32 = jnp.float32
BF16 = jnp.bfloat16
DIFFUSION_RATE = 0.15
LANES = 128
ROWS = 8
LEVELS = 80
MASK_LANE = LEVELS
CELLS = 2 * LEVELS
BEFORE = CELLS
WET = 2 * CELLS
MESSAGE = WET + ROWS
STAGED = 7
VMEM_LIMIT = 16 * 1024 * 1024

VM = pl.BlockSpec(memory_space=pltpu.VMEM)
SM = pl.BlockSpec(memory_space=pltpu.SMEM)
AN = pl.BlockSpec(memory_space=pl.ANY)


def vm(value):
    return pltpu.with_memory_space_constraint(value, pltpu.VMEM)


def hbm(value):
    return pltpu.with_memory_space_constraint(value, pltpu.HBM)


def call(kernel, out_shape, in_specs, scratch=(), name=None, aliases=None, outs=None):
    outs = outs or jax.tree.map(lambda _: VM, out_shape)
    return pl.pallas_call(
        kernel,
        out_shape=out_shape,
        in_specs=in_specs,
        out_specs=outs,
        scratch_shapes=list(scratch),
        name=name,
        input_output_aliases=aliases or {},
        compiler_params=pltpu.CompilerParams(vmem_limit_bytes=VMEM_LIMIT),
    )


def split3(value):
    high = value.astype(BF16).astype(F32)
    rest = value - high
    middle = rest.astype(BF16).astype(F32)
    return high, middle, rest - middle


def iota(axis):
    return lax.broadcasted_iota(jnp.int32, (ROWS, LANES), axis)


def roll(value, shift, axis):
    return pltpu.roll(value, shift, axis)


def flux_kernel(
    atmos_in, previous_in, index_in, *refs,
):
    staged_in, (packed, *staged) = refs[:STAGED], refs[STAGED : 2 * STAGED + 1]
    blocks, atmos, previous, index, arrivals, stage_arrivals = refs[2 * STAGED + 1 :]
    copies = [pltpu.make_async_copy(index_in, index, arrivals.at[0])]
    copies.append(pltpu.make_async_copy(previous_in, previous, arrivals.at[1]))
    for field in range(4):
        copies.append(
            pltpu.make_async_copy(atmos_in.at[field], atmos.at[field], arrivals.at[2 + field])
        )
    for copy in copies:
        copy.start()
    staging = [
        pltpu.make_async_copy(source, target, stage_arrivals.at[at])
        for at, (source, target) in enumerate(zip(staged_in[1:], staged[1:]))
    ]
    inside = staged[0].at[pl.ds(ROWS, CELLS * ROWS), :]
    staging.append(pltpu.make_async_copy(staged_in[0], inside, stage_arrivals.at[STAGED - 1]))
    for copy in staging:
        copy.start()
    levels = atmos.shape[1]
    row = lax.broadcasted_iota(jnp.int32, (ROWS, levels), 0)
    level = lax.broadcasted_iota(jnp.int32, (ROWS, levels), 1).astype(F32)
    bottom_total = sum(math.exp(-l / 3.0) for l in range(levels))
    radiative_total = sum(math.exp(-l / 24.0) for l in range(levels))
    bottom = split3(jnp.exp(-level / 3.0) / bottom_total)
    radiative = split3(jnp.exp(-level / 24.0) / radiative_total)
    table = jnp.zeros((ROWS, levels), F32)
    for at, part in enumerate(bottom + radiative):
        table = jnp.where(row == at, part, table)
    table = table.astype(BF16)

    def sums(field):
        copies[2 + field].wait()
        return lax.dot_general(
            table, atmos[field], (((1,), (0,)), ((), ())), preferred_element_type=F32
        )

    def low(value):
        return value[0:1] + value[1:2] + value[2:3]

    staged[0][0:ROWS, :] = jnp.zeros((ROWS, LANES), F32)
    staged[0][(CELLS + 1) * ROWS :, :] = jnp.zeros((ROWS, LANES), F32)
    copies[0].wait()
    copies[1].wait()
    temperature = sums(0)
    humidity = sums(1)
    radiation = temperature[3:4] + temperature[4:5] + temperature[5:6]
    east = low(sums(2))
    north = low(sums(3))
    speed = jnp.sqrt(east * east + north * north + 1.0)
    prior = previous[...]
    terms = (
        0.3 * speed * (low(temperature) - prior) + 0.5 * radiation,
        0.3 * speed * (jnp.exp(0.2 * prior) - 1.0 - low(humidity)),
        0.1 * speed * east,
        0.1 * speed * north,
    )
    for term, value in enumerate(terms):
        for block in range(blocks.shape[0]):
            blocks[block, term : term + 1, :] = value[:, block * LANES : (block + 1) * LANES]
    for peer in range(packed.shape[0]):
        for place in range(2):
            packed[peer, 4 * place : 4 * place + 4, :] = blocks[index[place, peer]]
    for copy in staging:
        copy.wait()


def tile(ref, at):
    return ref[pl.ds(pl.multiple_of(at * ROWS, ROWS), ROWS), :]


def inside(ref, at):
    return ref[pl.ds(pl.multiple_of((at + 1) * ROWS, ROWS), ROWS), :]


def to_first(value, level):
    return roll(value, lax.rem(LANES - level, LANES), 1)


def to_last(value, level):
    return roll(value, LANES - 1 - level, 1)


def edge_rows():
    core_row = (ROWS - 1) * (1 - lax.rem(lax.axis_index("tile"), 2))
    return ROWS - 1 - core_row, core_row


def first_kernel(
    arrived, slots, weight, tracers, mask,
    zed, core, coefficients, picked, forcing,
):
    pairs = weight.shape[1]
    for row in range(ROWS):
        for pair in range(pairs):
            picked[row // 2, 4 * (row % 2) : 4 * (row % 2) + 4, pair * LANES : (pair + 1) * LANES] = (
                arrived[pl.ds(pl.multiple_of(4 * slots[pair, row], 4), 4), :]
            )
    for half in range(ROWS // 2):
        left = jnp.concatenate(split3(picked[half]), axis=0).astype(BF16)
        for parity in range(2):
            row = 2 * half + parity
            right = jnp.concatenate([weight[row, pair] for pair in range(pairs)], axis=1)
            product = lax.dot_general(
                left, right, (((1,), (1,)), ((), ())), preferred_element_type=F32
            )
            product = product[0:8] + product[8:16] + product[16:24]
            for term in range(4):
                at = 4 * parity + term
                forcing[term, row : row + 1, :] = product[at : at + 1]
    sub, lane = iota(0), iota(1)
    wet = mask[...].astype(F32)
    inner = (
        DIFFUSION_RATE * jnp.where(sub == 0, 0.0, wet * roll(wet, 1, 0)),
        DIFFUSION_RATE * jnp.where(sub == ROWS - 1, 0.0, wet * roll(wet, ROWS - 1, 0)),
        DIFFUSION_RATE * jnp.where(lane == 0, 0.0, wet * roll(wet, 1, 1)),
        DIFFUSION_RATE * jnp.where(lane == LANES - 1, 0.0, wet * roll(wet, LANES - 1, 1)),
    )
    total_weight = inner[0] + inner[1] + inner[2] + inner[3]
    stress_east, stress_north = forcing[2], forcing[3]
    stress = jnp.sqrt(stress_east * stress_east + stress_north * stress_north)
    constant = 0.05 * wet
    decaying = 0.15 * wet * (stress / (1.0 + stress))
    surface = [0.5 * wet * forcing[0], 0.5 * wet * forcing[1]]
    for at, value in enumerate(inner + (wet, constant, decaying, surface[0], surface[1])):
        coefficients[at] = value
    for target, row in zip((zed, core), edge_rows()):
        inner_rows = [coefficients[at, pl.ds(row, 1), :] for at in range(9)]
        total_row = inner_rows[0] + inner_rows[1] + inner_rows[2] + inner_rows[3]
        decays = jnp.exp(sub.astype(F32) / -8.0)
        for cell in range(0, CELLS, ROWS):
            level = cell % LEVELS
            start = (cell + 1) * ROWS + row

            def rows(skip, start=start):
                return tracers[pl.ds(start + skip, ROWS, stride=ROWS), :]

            here = rows(0)
            slow = (decays * math.exp(-level / 8.0)) * inner_rows[6]
            fall = (inner_rows[5] + slow) * (rows(ROWS) - here)
            flow = (inner_rows[5] + slow * math.exp(1.0 / 8.0)) * (here - rows(-ROWS))
            if level == 0:
                flow = jnp.where(sub == 0, -inner_rows[7 + cell // LEVELS], flow)
            if level == LEVELS - ROWS:
                fall = jnp.where(sub == ROWS - 1, 0.0, fall)
            value = here - total_row * here + (fall - flow)
            value = value + inner_rows[0] * rows(-1) + inner_rows[1] * rows(1)
            value = value + inner_rows[2] * roll(here, 1, 1)
            value = value + inner_rows[3] * roll(here, LANES - 1, 1)
            target[cell : cell + ROWS, :] = value
            target[BEFORE + cell : BEFORE + cell + ROWS, :] = here
        target[WET:MESSAGE, :] = jnp.broadcast_to(inner_rows[4], (ROWS, LANES))


def column_kernel(tracers, coefficients, west, east):
    lane = iota(1)
    inner = [coefficients[at] for at in range(9)]
    wet, constant, decaying = inner[4], inner[5], inner[6]
    total_weight = inner[0] + inner[1] + inner[2] + inner[3]
    unroll = 8

    def step(group, carry):
        kept = list(carry)
        for inner_level in range(unroll):
            level = group * unroll + inner_level
            spots = [lane == lax.rem(level + skip, LANES) for skip in (0, 1, LANES - 1, LANES - 2)]
            for tracer in range(2):
                turned = roll(inside(tracers, tracer * LEVELS + level), level, 1)
                for place, spot in enumerate(spots):
                    at = 2 * place + tracer
                    kept[at] = jnp.where(spot, turned, kept[at])
        return tuple(kept)

    zero = jnp.zeros((ROWS, LANES), F32)
    kept = list(lax.fori_loop(0, LEVELS // unroll, step, (zero,) * 8))
    for tracer in range(2):
        for place, shift in ((1, LANES - 1), (2, 1), (3, 2)):
            kept[2 * place + tracer] = roll(kept[2 * place + tracer], shift, 1)
    decays = jnp.exp(lane.astype(F32) / -8.0)
    for target, end, at_end, at_next, side in ((west, 0, 0, 2, 3), (east, LANES - 1, 4, 6, 2)):
        cut = slice(end, end + 1)
        rate = constant[:, cut] + decays * decaying[:, cut]
        for tracer in range(2):
            column, beside = kept[at_end + tracer], kept[at_next + tracer]
            fall = rate * (roll(column, LANES - 1, 1) - column)
            fall = jnp.where(lane < LEVELS - 1, fall, 0.0)
            flow = jnp.where(lane == 0, -inner[7 + tracer][:, cut], roll(fall, 1, 1))
            total = column - total_weight[:, cut] * column + (fall - flow)
            total = total + inner[0][:, cut] * roll(column, 1, 0)
            total = total + inner[1][:, cut] * roll(column, ROWS - 1, 0)
            target[tracer] = total + inner[side][:, cut] * beside
            target[2 + tracer] = column
        target[2] = jnp.where(lane == MASK_LANE, wet[:, cut], kept[at_end])
        target[4] = zero


def corner_kernel(zed, core, _, __, west, east):
    lane = lax.broadcasted_iota(jnp.int32, (1, LANES), 1)
    padding = jnp.zeros((LANES - LEVELS, LANES), F32)
    for place, source in enumerate((zed, core)):
        for tracer in range(2):
            start = BEFORE + tracer * LEVELS
            turned = jnp.concatenate([source[start : start + LEVELS, :], padding], axis=0).T
            for target, end in ((west, 0), (east, LANES - 1)):
                row = turned[end : end + 1, :]
                if tracer == 0:
                    row = jnp.where(lane == MASK_LANE, source[WET : WET + 1, end : end + 1], row)
                at = 2 * place + tracer
                target[4, at : at + 1, :] = row


class Rim:
    def __init__(self, own, halo, coefficients):
        self.own, self.halo = own[0:2], halo[0:2]
        own_west, own_east, west, east = own[2], own[3], halo[2], halo[3]
        self.west, self.east = west, east
        sub, lane = iota(0), iota(1)
        self.lane = lane[0:1]
        wet = coefficients[4]
        rows = edge_rows()
        self.inner = [coefficients[at] for at in range(4)]
        wet_rows = [ref[WET : WET + 1, :] for ref in self.halo]
        wet_west = to_first(west[2], MASK_LANE)
        wet_east = to_last(east[2], MASK_LANE)
        self.rows = [
            DIFFUSION_RATE * coefficients[4, pl.ds(row, 1), :] * wet_row
            for row, wet_row in zip(rows, wet_rows)
        ]
        column_west = DIFFUSION_RATE * wet * wet_west
        column_east = DIFFUSION_RATE * wet * wet_east
        zero = jnp.zeros((ROWS, LANES), F32)
        self.border = (
            jnp.where(sub == rows[0], self.rows[0], zero),
            jnp.where(sub == rows[1], self.rows[1], zero),
            jnp.where(lane == 0, column_west, zero),
            jnp.where(lane == LANES - 1, column_east, zero),
        )
        self.inner_total = sum(self.inner)
        self.total = self.inner_total + sum(self.border)
        self.step_west = [west[2 + tracer] - own_west[2 + tracer] for tracer in range(2)]
        self.step_east = [east[2 + tracer] - own_east[2 + tracer] for tracer in range(2)]
        self.corner_weight = []
        for place, wet_row in enumerate(wet_rows):
            mask = slice(2 * place, 2 * place + 1), slice(MASK_LANE, MASK_LANE + 1)
            self.corner_weight.append(
                jnp.where(self.lane == 0, DIFFUSION_RATE * wet_row * west[(4,) + mask], 0.0)
                + jnp.where(self.lane == LANES - 1, DIFFUSION_RATE * wet_row * east[(4,) + mask], 0.0)
            )
        self.side_west, self.side_east = [], []
        for side, tiles, wet_side, column, steps in (
            (self.side_west, west, wet_west[:, 0:1], column_west[:, 0:1], self.step_west),
            (
                self.side_east,
                east,
                wet_east[:, LANES - 1 :],
                column_east[:, LANES - 1 :],
                self.step_east,
            ),
        ):
            for tracer in range(2):
                value = tiles[tracer] - column * steps[tracer]
                for place, row in enumerate(rows):
                    diagonal = tiles[4, 2 * place : 2 * place + 1, MASK_LANE : MASK_LANE + 1]
                    corner = tiles[4, 2 * place + tracer : 2 * place + tracer + 1, :]
                    value = value + jnp.where(
                        sub == row,
                        (DIFFUSION_RATE * wet_side * diagonal) * (corner - tiles[2 + tracer]),
                        0.0,
                    )
                side.append(value)

    def beyond(self, place, now, before, corner):
        halo = self.halo[place]
        old = halo[before, :]
        step = old - self.own[place][before, :]
        edge = halo[now, :] - self.rows[place] * step + self.corner_weight[place] * (corner - old)
        return step, edge

    def after(self, tracers, tracer, level, steps, here, vertical):
        at = pl.multiple_of((tracer * LEVELS + level) * ROWS, ROWS)
        value = here - self.inner_total * here + vertical
        value = value + self.inner[0] * tracers[pl.ds(at + ROWS - 1, ROWS), :]
        value = value + self.inner[1] * tracers[pl.ds(at + ROWS + 1, ROWS), :]
        value = value + self.inner[2] * roll(here, 1, 1)
        value = value + self.inner[3] * roll(here, LANES - 1, 1)
        value = value + self.border[0] * steps[0] + self.border[1] * steps[1]
        value = value + self.border[2] * to_first(self.step_west[tracer], level)
        return value + self.border[3] * to_last(self.step_east[tracer], level)

    def lateral(self, tracer, level, here, edges):
        value = here - self.total * here
        value = value + self.border[0] * edges[0] + self.border[1] * edges[1]
        value = value + self.border[2] * to_first(self.side_west[tracer], level)
        value = value + self.border[3] * to_last(self.side_east[tracer], level)
        value = value + self.inner[0] * roll(here, 1, 0)
        value = value + self.inner[1] * roll(here, ROWS - 1, 0)
        value = value + self.inner[2] * roll(here, 1, 1)
        return value + self.inner[3] * roll(here, LANES - 1, 1)


def reply_kernel(
    tracers, own_zed, own_core, own_west, own_east, zed, core, west, east, coefficients,
    weight, slots, replies,
):
    pairs = weight.shape[1]
    own, halo = (own_zed, own_core, own_west, own_east), (zed, core, west, east)
    rim = Rim(own, halo, coefficients)
    steps, edges = [], []
    for place in range(2):
        row = slice(2 * place, 2 * place + 1)
        corner = jnp.where(rim.lane == 0, west[4, row, 0:1], east[4, row, 0:1])
        step, edge = rim.beyond(place, slice(0, 1), slice(BEFORE, BEFORE + 1), corner)
        steps.append(step)
        edges.append(edge)
    below = slice(BEFORE + 1, BEFORE + 2)
    first, second, third = [inside(tracers, level) for level in range(3)]
    rate = coefficients[5] + coefficients[6]
    rate_below = coefficients[5] + coefficients[6] * math.exp(-1.0 / 8.0)
    flow = rate * (second - first)
    here = rim.after(tracers, 0, 0, steps, first, flow + coefficients[7])
    steps = [rim.halo[at][below, :] - rim.own[at][below, :] for at in range(2)]
    later = rim.after(tracers, 0, 1, steps, second, rate_below * (third - second) - flow)
    fall = rate * (later - here)
    surface = rim.lateral(0, 0, here, edges) + (fall + coefficients[7])
    left = jnp.concatenate(split3(surface) + (jnp.ones((ROWS, LANES), F32),), axis=0).astype(BF16)
    replies[...] = jnp.zeros_like(replies)
    for row in range(ROWS):
        right = jnp.concatenate([weight[row, pair] for pair in range(pairs)], axis=1)
        product = lax.dot_general(left, right, (((1,), (0,)), ((), ())), preferred_element_type=F32)
        numer = product[row : row + 1] + product[8 + row : 9 + row] + product[16 + row : 17 + row]
        denom = product[24:25]
        both = jnp.concatenate([numer, denom], axis=0)
        for pair in range(pairs):
            slot = slots[pair, row]
            replies[slot] = replies[slot] + both[:, pair * LANES : (pair + 1) * LANES]


def final_kernel(
    returned, index, counts, previous, surface,
):
    blocks = previous.shape[0]
    peers = counts.shape[1]
    block = lax.broadcasted_iota(jnp.int32, (blocks, peers), 0)
    numer, denom = 0.0, 0.0
    for place in range(2):
        chosen = (block == index[place : place + 1, :]) & (place < counts[...])
        chosen = chosen.astype(F32).astype(BF16)
        rows = [returned[pl.ds(2 * place + at, peers, stride=4), :] for at in range(2)]
        parts = jnp.concatenate(split3(rows[0]) + split3(rows[1]), axis=1).astype(BF16)
        product = lax.dot_general(
            chosen, parts, (((1,), (0,)), ((), ())), preferred_element_type=F32
        )
        cuts = [product[:, at * LANES : (at + 1) * LANES] for at in range(6)]
        numer = cuts[0] + cuts[1] + cuts[2] + numer
        denom = cuts[3] + cuts[4] + cuts[5] + denom
    surface[...] = (previous[...] + numer) / (1.0 + denom)


def second_kernel(
    tracers, own_zed, own_core, own_west, own_east, zed, core, west, east, coefficients, _,
    output, result, step_core, step_zed, edge_core, edge_zed, sent,
):
    own, halo = (own_zed, own_core, own_west, own_east), (zed, core, west, east)
    rim = Rim(own, halo, coefficients)
    ends = jnp.concatenate([west[4, 0:4, :], east[4, 0:4, :]], axis=0).T
    lane = lax.broadcasted_iota(jnp.int32, (LEVELS, LANES), 1)
    for place, (steps, edges) in enumerate(((step_zed, edge_zed), (step_core, edge_core))):
        for tracer in range(2):
            at = 2 * place + tracer
            corner = jnp.where(lane == 0, ends[0:LEVELS, at : at + 1], ends[0:LEVELS, at + 4 : at + 5])
            now = slice(tracer * LEVELS, (tracer + 1) * LEVELS)
            before = slice(BEFORE + tracer * LEVELS, BEFORE + (tracer + 1) * LEVELS)
            steps[now, :], edges[now, :] = rim.beyond(place, now, before, corner)
    constant, decaying = coefficients[5], coefficients[6]
    unroll, parts = 4, 4
    decay = [math.exp(-inner_level / 8.0) for inner_level in range(unroll + 1)]

    def pick(refs, tracer, level):
        return [ref[pl.ds(tracer * LEVELS + level, 1), :] for ref in refs]

    def after(tracer, level, here, flow, rate):
        below = inside(tracers, tracer * LEVELS + jnp.minimum(level + 1, LEVELS - 1))
        fall = rate * (below - here)
        steps = pick((step_zed, step_core), tracer, level)
        return rim.after(tracers, tracer, level, steps, here, fall - flow), below, fall

    def step(group, carry):
        now, flow, state, fell, depth = [list(value) for value in carry[:4]] + [carry[4]]
        for inner_level in range(unroll):
            level = group * unroll + inner_level
            later = jnp.minimum(level + 1, LEVELS - 1)
            rate = constant + depth * decay[inner_level]
            rate_below = constant + depth * decay[inner_level + 1]
            for tracer in range(2):
                here = now[tracer]
                below, state[tracer], fell[tracer] = after(
                    tracer, later, state[tracer], fell[tracer], rate_below
                )
                fall = jnp.where(level < LEVELS - 1, rate * (below - here), 0.0)
                edges = pick((edge_zed, edge_core), tracer, level)
                total = rim.lateral(tracer, level, here, edges) + (fall - flow[tracer])
                at = pl.multiple_of((tracer * LEVELS + level) * ROWS, ROWS)
                result[pl.ds(at, ROWS), :] = total
                now[tracer] = below
                flow[tracer] = fall
        return tuple(now), tuple(flow), tuple(state), tuple(fell), depth * decay[unroll]

    starts = [
        after(tracer, 0, inside(tracers, tracer * LEVELS), -coefficients[7 + tracer], constant + decaying)
        for tracer in range(2)
    ]
    now, state, fell = zip(*starts)
    carry = (now, (-coefficients[7], -coefficients[8]), state, fell, decaying)
    groups = LEVELS // unroll // parts
    copies = []
    for part in range(parts):
        carry = lax.fori_loop(part * groups, (part + 1) * groups, step, carry)
        count = groups * unroll * ROWS
        for tracer in range(2):
            at = pl.ds(tracer * LEVELS * ROWS + part * count, count)
            copies.append(
                pltpu.make_async_copy(result.at[at, :], output.at[at, :], sent.at[len(copies)])
            )
            copies[-1].start()
    for copy in copies:
        copy.wait()


def shards(
    atmos_profile_state,
    previous_surface_temp,
    outbound_block_index,
    outbound_slot_counts,
    pair_source_slot,
    overlay_weight,
    ocean_tracer_state,
    ocean_cell_mask,
):
    peers, levs = lax.axis_size("tile"), lax.axis_size("lev")
    slot_total = 2 * peers
    blocks = previous_surface_temp.shape[0] // LANES
    shape = jax.ShapeDtypeStruct
    index = outbound_block_index.T
    slots = pair_source_slot.T
    tracers = ocean_tracer_state.reshape(CELLS * ROWS, LANES)
    prior = previous_surface_temp.reshape(1, -1)
    square = previous_surface_temp.reshape(blocks, LANES)

    staged = (tracers, overlay_weight, ocean_cell_mask, slots, index, outbound_slot_counts, square)
    packed, *staged = call(
        flux_kernel,
        (pltpu.VMEM((peers, ROWS, LANES), F32),)
        + (pltpu.VMEM(((CELLS + 2) * ROWS, LANES), F32),)
        + tuple(
            (pltpu.SMEM if value is slots else pltpu.VMEM)(value.shape, value.dtype)
            for value in staged[1:]
        ),
        [AN] * (3 + STAGED),
        [
            pltpu.VMEM((blocks, 4, LANES), F32),
            pltpu.VMEM(atmos_profile_state.shape, BF16),
            pltpu.VMEM(prior.shape, F32),
            pltpu.SMEM(index.shape, jnp.int32),
            pltpu.SemaphoreType.DMA((6,)),
            pltpu.SemaphoreType.DMA((STAGED,)),
        ],
        "flux",
        outs=(VM,) * 4 + (SM,) + (VM,) * (STAGED - 4),
    )(hbm(atmos_profile_state), hbm(prior), hbm(index), *[hbm(value) for value in staged])
    tracers, weight, mask, slots, index, counts, square = staged
    slots = pltpu.with_memory_space_constraint(slots, pltpu.SMEM)
    arrived = lax.all_to_all(packed, "tile", split_axis=0, concat_axis=0, tiled=True)
    arrived = arrived.reshape(4 * slot_total, LANES)

    row_message, column_message = shape((MESSAGE, LANES), F32), shape((5, ROWS, LANES), F32)
    zed, core, coefficients = call(
        first_kernel,
        (
            row_message,
            row_message,
            shape((9, ROWS, LANES), F32),
        ),
        [VM, SM] + [VM] * 3,
        [pltpu.VMEM((ROWS // 2, ROWS, 4 * LANES), F32), pltpu.VMEM((4, ROWS, LANES), F32)],
        "first",
    )(vm(arrived), slots, vm(weight), vm(tracers), vm(mask))
    across = [(i, i + 1) for i in range(1, peers - 1, 2)]
    across += [(target, source) for source, target in across]
    halo_core = vm(lax.ppermute(core, "tile", [(i, i ^ 1) for i in range(peers)]))
    halo_zed = vm(lax.ppermute(zed, "tile", across))
    west, east = call(
        column_kernel,
        (column_message, column_message),
        [VM] * 2,
        (),
        "columns",
    )(vm(tracers), vm(coefficients))
    west, east = call(
        corner_kernel,
        (column_message, column_message),
        [VM] * 4,
        (),
        "corner",
        {2: 0, 3: 1},
    )(halo_zed, halo_core, vm(west), vm(east))
    halo_west = vm(lax.ppermute(east, "lev", [(i, i + 1) for i in range(levs - 1)]))
    halo_east = vm(lax.ppermute(west, "lev", [(i + 1, i) for i in range(levs - 1)]))
    edges = [
        vm(value)
        for value in (
            tracers, zed, core, west, east, halo_zed, halo_core, halo_west, halo_east, coefficients,
        )
    ]
    replies = call(
        reply_kernel,
        shape((slot_total, 2, LANES), F32),
        [VM] * 11 + [SM],
        (),
        "reply",
    )(*edges, vm(weight), slots)
    returned = lax.all_to_all(replies, "tile", split_axis=0, concat_axis=0, tiled=True)
    output = call(
        second_kernel,
        shape((CELLS * ROWS, LANES), F32),
        [VM] * 10 + [AN],
        [pltpu.VMEM((CELLS * ROWS, LANES), F32)]
        + [pltpu.VMEM((CELLS, LANES), F32)] * 4
        + [pltpu.SemaphoreType.DMA((8,))],
        "second",
        outs=AN,
    )(*edges, replies)
    surface = call(
        final_kernel,
        shape((blocks, LANES), F32),
        [VM] * 4,
        (),
        "final",
    )(vm(returned.reshape(2 * slot_total, LANES)), vm(index), vm(counts), vm(square))
    return (output.reshape(ocean_tracer_state.shape), surface.reshape(-1))


def solution(mesh):
    placed = (
        P(None, None, ("sec", "tile", "lev")),
        P(("sec", "tile", "lev")),
        P(("sec", "tile", "lev"), None),
        P(("sec", "tile", "lev"), None),
        P(("sec", "tile", "lev"), None),
        P(("sec", "tile", "lev"), None, None, None),
        P(None, None, ("sec", "tile"), "lev"),
        P(("sec", "tile"), "lev"),
    )
    return jax.shard_map(
        shards,
        mesh=mesh,
        in_specs=placed,
        out_specs=(P(None, None, ("sec", "tile"), "lev"), P(("sec", "tile", "lev"))),
        check_vma=False,
    )
```

```python
import math

import jax
import jax.numpy as jnp
from jax import lax
from jax.experimental import pallas as pl
from jax.experimental.pallas import tpu as pltpu
from jax.sharding import PartitionSpec as P

F32 = jnp.float32
BF16 = jnp.bfloat16
DIFFUSION_RATE = 0.15
LANES = 128
ROWS = 8
LEVELS = 80
MASK_LANE = LEVELS
CELLS = 2 * LEVELS
BEFORE = CELLS
WET = 2 * CELLS
MESSAGE = WET + ROWS
STAGED = 6
VMEM_LIMIT = 16 * 1024 * 1024

VM = pl.BlockSpec(memory_space=pltpu.VMEM)
SM = pl.BlockSpec(memory_space=pltpu.SMEM)
AN = pl.BlockSpec(memory_space=pl.ANY)


def vm(value):
    return pltpu.with_memory_space_constraint(value, pltpu.VMEM)


def hbm(value):
    return pltpu.with_memory_space_constraint(value, pltpu.HBM)


def call(kernel, out_shape, in_specs, scratch=(), name=None, aliases=None, outs=None):
    outs = outs or jax.tree.map(lambda _: VM, out_shape)
    return pl.pallas_call(
        kernel,
        out_shape=out_shape,
        in_specs=in_specs,
        out_specs=outs,
        scratch_shapes=list(scratch),
        name=name,
        input_output_aliases=aliases or {},
        compiler_params=pltpu.CompilerParams(vmem_limit_bytes=VMEM_LIMIT),
    )


def split3(value):
    high = value.astype(BF16).astype(F32)
    rest = value - high
    middle = rest.astype(BF16).astype(F32)
    return high, middle, rest - middle


def iota(axis):
    return lax.broadcasted_iota(jnp.int32, (ROWS, LANES), axis)


def roll(value, shift, axis):
    return pltpu.roll(value, shift, axis)


def flux_kernel(
    atmos_in, previous_in, index_in, *refs,
):
    staged_in, (packed, *staged) = refs[:STAGED], refs[STAGED : 2 * STAGED + 1]
    blocks, atmos, previous, index, arrivals, stage_arrivals = refs[2 * STAGED + 1 :]
    copies = [pltpu.make_async_copy(index_in, index, arrivals.at[0])]
    copies.append(pltpu.make_async_copy(previous_in, previous, arrivals.at[1]))
    for field in range(4):
        copies.append(
            pltpu.make_async_copy(atmos_in.at[field], atmos.at[field], arrivals.at[2 + field])
        )
    for copy in copies:
        copy.start()
    staging = [
        pltpu.make_async_copy(source, target, stage_arrivals.at[at])
        for at, (source, target) in enumerate(zip(staged_in[1:], staged[1:]))
    ]
    inside = staged[0].at[pl.ds(ROWS, CELLS * ROWS), :]
    staging.append(pltpu.make_async_copy(staged_in[0], inside, stage_arrivals.at[STAGED - 1]))
    for copy in staging:
        copy.start()
    levels = atmos.shape[1]
    row = lax.broadcasted_iota(jnp.int32, (ROWS, levels), 0)
    level = lax.broadcasted_iota(jnp.int32, (ROWS, levels), 1).astype(F32)
    bottom_total = sum(math.exp(-l / 3.0) for l in range(levels))
    radiative_total = sum(math.exp(-l / 24.0) for l in range(levels))
    bottom = split3(jnp.exp(-level / 3.0) / bottom_total)
    radiative = split3(jnp.exp(-level / 24.0) / radiative_total)
    table = jnp.zeros((ROWS, levels), F32)
    for at, part in enumerate(bottom + radiative):
        table = jnp.where(row == at, part, table)
    table = table.astype(BF16)

    def sums(field):
        copies[2 + field].wait()
        return lax.dot_general(
            table, atmos[field], (((1,), (0,)), ((), ())), preferred_element_type=F32
        )

    def low(value):
        return value[0:1] + value[1:2] + value[2:3]

    staged[0][0:ROWS, :] = jnp.zeros((ROWS, LANES), F32)
    staged[0][(CELLS + 1) * ROWS :, :] = jnp.zeros((ROWS, LANES), F32)
    copies[0].wait()
    copies[1].wait()
    temperature = sums(0)
    humidity = sums(1)
    radiation = temperature[3:4] + temperature[4:5] + temperature[5:6]
    east = low(sums(2))
    north = low(sums(3))
    speed = jnp.sqrt(east * east + north * north + 1.0)
    prior = previous[...]
    terms = (
        0.3 * speed * (low(temperature) - prior) + 0.5 * radiation,
        0.3 * speed * (jnp.exp(0.2 * prior) - 1.0 - low(humidity)),
        0.1 * speed * east,
        0.1 * speed * north,
    )
    for term, value in enumerate(terms):
        for block in range(blocks.shape[0]):
            blocks[block, term : term + 1, :] = value[:, block * LANES : (block + 1) * LANES]
    for slot in range(packed.shape[0]):
        packed[slot] = blocks[index[slot % 2, slot // 2]]
    for copy in staging:
        copy.wait()


def tile(ref, at):
    return ref[pl.ds(pl.multiple_of(at * ROWS, ROWS), ROWS), :]


def inside(ref, at):
    return ref[pl.ds(pl.multiple_of((at + 1) * ROWS, ROWS), ROWS), :]


def to_first(value, level):
    return roll(value, lax.rem(LANES - level, LANES), 1)


def to_last(value, level):
    return roll(value, LANES - 1 - level, 1)


def edge_rows():
    core_row = (ROWS - 1) * (1 - lax.rem(lax.axis_index("tile"), 2))
    return ROWS - 1 - core_row, core_row


def first_kernel(
    arrived, slots, weight, tracers, mask,
    zed, core, coefficients, picked, forcing,
):
    pairs = weight.shape[1]
    for row in range(ROWS):
        for pair in range(pairs):
            picked[row // 2, 4 * (row % 2) : 4 * (row % 2) + 4, pair * LANES : (pair + 1) * LANES] = (
                arrived[slots[pair, row]]
            )
    for half in range(ROWS // 2):
        left = jnp.concatenate(split3(picked[half]), axis=0).astype(BF16)
        for parity in range(2):
            row = 2 * half + parity
            right = jnp.concatenate([weight[row, pair] for pair in range(pairs)], axis=1)
            product = lax.dot_general(
                left, right, (((1,), (1,)), ((), ())), preferred_element_type=F32
            )
            product = product[0:8] + product[8:16] + product[16:24]
            for term in range(4):
                at = 4 * parity + term
                forcing[term, row : row + 1, :] = product[at : at + 1]
    sub, lane = iota(0), iota(1)
    wet = mask[...].astype(F32)
    inner = (
        DIFFUSION_RATE * jnp.where(sub == 0, 0.0, wet * roll(wet, 1, 0)),
        DIFFUSION_RATE * jnp.where(sub == ROWS - 1, 0.0, wet * roll(wet, ROWS - 1, 0)),
        DIFFUSION_RATE * jnp.where(lane == 0, 0.0, wet * roll(wet, 1, 1)),
        DIFFUSION_RATE * jnp.where(lane == LANES - 1, 0.0, wet * roll(wet, LANES - 1, 1)),
    )
    total_weight = inner[0] + inner[1] + inner[2] + inner[3]
    stress_east, stress_north = forcing[2], forcing[3]
    stress = jnp.sqrt(stress_east * stress_east + stress_north * stress_north)
    constant = 0.05 * wet
    decaying = 0.15 * wet * (stress / (1.0 + stress))
    surface = [0.5 * wet * forcing[0], 0.5 * wet * forcing[1]]
    for at, value in enumerate(inner + (wet, constant, decaying, surface[0], surface[1])):
        coefficients[at] = value
    for target, row in zip((zed, core), edge_rows()):
        inner_rows = [coefficients[at, pl.ds(row, 1), :] for at in range(9)]
        total_row = inner_rows[0] + inner_rows[1] + inner_rows[2] + inner_rows[3]
        decays = jnp.exp(sub.astype(F32) / -8.0)
        for cell in range(0, CELLS, ROWS):
            level = cell % LEVELS
            start = (cell + 1) * ROWS + row

            def rows(skip, start=start):
                return tracers[pl.ds(start + skip, ROWS, stride=ROWS), :]

            here = rows(0)
            slow = (decays * math.exp(-level / 8.0)) * inner_rows[6]
            fall = (inner_rows[5] + slow) * (rows(ROWS) - here)
            flow = (inner_rows[5] + slow * math.exp(1.0 / 8.0)) * (here - rows(-ROWS))
            if level == 0:
                flow = jnp.where(sub == 0, -inner_rows[7 + cell // LEVELS], flow)
            if level == LEVELS - ROWS:
                fall = jnp.where(sub == ROWS - 1, 0.0, fall)
            value = here - total_row * here + (fall - flow)
            value = value + inner_rows[0] * rows(-1) + inner_rows[1] * rows(1)
            value = value + inner_rows[2] * roll(here, 1, 1)
            value = value + inner_rows[3] * roll(here, LANES - 1, 1)
            target[cell : cell + ROWS, :] = value
            target[BEFORE + cell : BEFORE + cell + ROWS, :] = here
        target[WET:MESSAGE, :] = jnp.broadcast_to(inner_rows[4], (ROWS, LANES))


def column_kernel(tracers, coefficients, west, east):
    lane = iota(1)
    inner = [coefficients[at] for at in range(9)]
    wet, constant, decaying = inner[4], inner[5], inner[6]
    total_weight = inner[0] + inner[1] + inner[2] + inner[3]
    unroll = 8

    def step(group, carry):
        kept = list(carry)
        for inner_level in range(unroll):
            level = group * unroll + inner_level
            spots = [lane == lax.rem(level + skip, LANES) for skip in (0, 1, LANES - 1, LANES - 2)]
            for tracer in range(2):
                turned = roll(inside(tracers, tracer * LEVELS + level), level, 1)
                for place, spot in enumerate(spots):
                    at = 2 * place + tracer
                    kept[at] = jnp.where(spot, turned, kept[at])
        return tuple(kept)

    zero = jnp.zeros((ROWS, LANES), F32)
    kept = list(lax.fori_loop(0, LEVELS // unroll, step, (zero,) * 8))
    for tracer in range(2):
        for place, shift in ((1, LANES - 1), (2, 1), (3, 2)):
            kept[2 * place + tracer] = roll(kept[2 * place + tracer], shift, 1)
    decays = jnp.exp(lane.astype(F32) / -8.0)
    for target, end, at_end, at_next, side in ((west, 0, 0, 2, 3), (east, LANES - 1, 4, 6, 2)):
        cut = slice(end, end + 1)
        rate = constant[:, cut] + decays * decaying[:, cut]
        for tracer in range(2):
            column, beside = kept[at_end + tracer], kept[at_next + tracer]
            fall = rate * (roll(column, LANES - 1, 1) - column)
            fall = jnp.where(lane < LEVELS - 1, fall, 0.0)
            flow = jnp.where(lane == 0, -inner[7 + tracer][:, cut], roll(fall, 1, 1))
            total = column - total_weight[:, cut] * column + (fall - flow)
            total = total + inner[0][:, cut] * roll(column, 1, 0)
            total = total + inner[1][:, cut] * roll(column, ROWS - 1, 0)
            target[tracer] = total + inner[side][:, cut] * beside
            target[2 + tracer] = column
        target[2] = jnp.where(lane == MASK_LANE, wet[:, cut], kept[at_end])
        target[4] = zero


def corner_kernel(zed, core, _, __, west, east):
    lane = lax.broadcasted_iota(jnp.int32, (1, LANES), 1)
    padding = jnp.zeros((LANES - LEVELS, LANES), F32)
    for place, source in enumerate((zed, core)):
        for tracer in range(2):
            start = BEFORE + tracer * LEVELS
            turned = jnp.concatenate([source[start : start + LEVELS, :], padding], axis=0).T
            for target, end in ((west, 0), (east, LANES - 1)):
                row = turned[end : end + 1, :]
                if tracer == 0:
                    row = jnp.where(lane == MASK_LANE, source[WET : WET + 1, end : end + 1], row)
                at = 2 * place + tracer
                target[4, at : at + 1, :] = row


class Rim:
    def __init__(self, own, halo, coefficients):
        self.own, self.halo = own[0:2], halo[0:2]
        own_west, own_east, west, east = own[2], own[3], halo[2], halo[3]
        self.west, self.east = west, east
        sub, lane = iota(0), iota(1)
        self.lane = lane[0:1]
        wet = coefficients[4]
        rows = edge_rows()
        self.inner = [coefficients[at] for at in range(4)]
        wet_rows = [ref[WET : WET + 1, :] for ref in self.halo]
        wet_west = to_first(west[2], MASK_LANE)
        wet_east = to_last(east[2], MASK_LANE)
        self.rows = [
            DIFFUSION_RATE * coefficients[4, pl.ds(row, 1), :] * wet_row
            for row, wet_row in zip(rows, wet_rows)
        ]
        column_west = DIFFUSION_RATE * wet * wet_west
        column_east = DIFFUSION_RATE * wet * wet_east
        zero = jnp.zeros((ROWS, LANES), F32)
        self.border = (
            jnp.where(sub == rows[0], self.rows[0], zero),
            jnp.where(sub == rows[1], self.rows[1], zero),
            jnp.where(lane == 0, column_west, zero),
            jnp.where(lane == LANES - 1, column_east, zero),
        )
        self.inner_total = sum(self.inner)
        self.total = self.inner_total + sum(self.border)
        self.step_west = [west[2 + tracer] - own_west[2 + tracer] for tracer in range(2)]
        self.step_east = [east[2 + tracer] - own_east[2 + tracer] for tracer in range(2)]
        self.corner_weight = []
        for place, wet_row in enumerate(wet_rows):
            mask = slice(2 * place, 2 * place + 1), slice(MASK_LANE, MASK_LANE + 1)
            self.corner_weight.append(
                jnp.where(self.lane == 0, DIFFUSION_RATE * wet_row * west[(4,) + mask], 0.0)
                + jnp.where(self.lane == LANES - 1, DIFFUSION_RATE * wet_row * east[(4,) + mask], 0.0)
            )
        self.side_west, self.side_east = [], []
        for side, tiles, wet_side, column, steps in (
            (self.side_west, west, wet_west[:, 0:1], column_west[:, 0:1], self.step_west),
            (
                self.side_east,
                east,
                wet_east[:, LANES - 1 :],
                column_east[:, LANES - 1 :],
                self.step_east,
            ),
        ):
            for tracer in range(2):
                value = tiles[tracer] - column * steps[tracer]
                for place, row in enumerate(rows):
                    diagonal = tiles[4, 2 * place : 2 * place + 1, MASK_LANE : MASK_LANE + 1]
                    corner = tiles[4, 2 * place + tracer : 2 * place + tracer + 1, :]
                    value = value + jnp.where(
                        sub == row,
                        (DIFFUSION_RATE * wet_side * diagonal) * (corner - tiles[2 + tracer]),
                        0.0,
                    )
                side.append(value)

    def beyond(self, place, now, before, corner):
        halo = self.halo[place]
        old = halo[before, :]
        step = old - self.own[place][before, :]
        edge = halo[now, :] - self.rows[place] * step + self.corner_weight[place] * (corner - old)
        return step, edge

    def after(self, tracers, tracer, level, steps, here, vertical):
        at = pl.multiple_of((tracer * LEVELS + level) * ROWS, ROWS)
        value = here - self.inner_total * here + vertical
        value = value + self.inner[0] * tracers[pl.ds(at + ROWS - 1, ROWS), :]
        value = value + self.inner[1] * tracers[pl.ds(at + ROWS + 1, ROWS), :]
        value = value + self.inner[2] * roll(here, 1, 1)
        value = value + self.inner[3] * roll(here, LANES - 1, 1)
        value = value + self.border[0] * steps[0] + self.border[1] * steps[1]
        value = value + self.border[2] * to_first(self.step_west[tracer], level)
        return value + self.border[3] * to_last(self.step_east[tracer], level)

    def lateral(self, tracer, level, here, edges):
        value = here - self.total * here
        value = value + self.border[0] * edges[0] + self.border[1] * edges[1]
        value = value + self.border[2] * to_first(self.side_west[tracer], level)
        value = value + self.border[3] * to_last(self.side_east[tracer], level)
        value = value + self.inner[0] * roll(here, 1, 0)
        value = value + self.inner[1] * roll(here, ROWS - 1, 0)
        value = value + self.inner[2] * roll(here, 1, 1)
        return value + self.inner[3] * roll(here, LANES - 1, 1)


def reply_kernel(
    tracers, own_zed, own_core, own_west, own_east, zed, core, east, west, coefficients,
    weight, slots, replies,
):
    pairs = weight.shape[1]
    own, halo = (own_zed, own_core, own_west, own_east), (zed, core, west, east)
    rim = Rim(own, halo, coefficients)
    steps, edges = [], []
    for place in range(2):
        row = slice(2 * place, 2 * place + 1)
        corner = jnp.where(rim.lane == 0, west[4, row, 0:1], east[4, row, 0:1])
        step, edge = rim.beyond(place, slice(0, 1), slice(BEFORE, BEFORE + 1), corner)
        steps.append(step)
        edges.append(edge)
    below = slice(BEFORE + 1, BEFORE + 2)
    first, second, third = [inside(tracers, level) for level in range(3)]
    rate = coefficients[5] + coefficients[6]
    rate_below = coefficients[5] + coefficients[6] * math.exp(-1.0 / 8.0)
    flow = rate * (second - first)
    here = rim.after(tracers, 0, 0, steps, first, flow + coefficients[7])
    steps = [rim.halo[at][below, :] - rim.own[at][below, :] for at in range(2)]
    later = rim.after(tracers, 0, 1, steps, second, rate_below * (third - second) - flow)
    fall = rate * (later - here)
    surface = rim.lateral(0, 0, here, edges) + (fall + coefficients[7])
    left = jnp.concatenate(split3(surface) + (jnp.ones((ROWS, LANES), F32),), axis=0).astype(BF16)
    replies[...] = jnp.zeros_like(replies)
    for row in range(ROWS):
        right = jnp.concatenate([weight[row, pair] for pair in range(pairs)], axis=1)
        product = lax.dot_general(left, right, (((1,), (0,)), ((), ())), preferred_element_type=F32)
        numer = product[row : row + 1] + product[8 + row : 9 + row] + product[16 + row : 17 + row]
        denom = product[24:25]
        both = jnp.concatenate([numer, denom], axis=0)
        for pair in range(pairs):
            slot = slots[pair, row]
            replies[slot] = replies[slot] + both[:, pair * LANES : (pair + 1) * LANES]


def final_kernel(
    returned, index, counts, previous, surface,
):
    blocks = previous.shape[0]
    peers = counts.shape[1]
    block = lax.broadcasted_iota(jnp.int32, (blocks, peers), 0)
    numer, denom = 0.0, 0.0
    for place in range(2):
        chosen = (block == index[place : place + 1, :]) & (place < counts[...])
        chosen = chosen.astype(F32).astype(BF16)
        rows = [returned[pl.ds(2 * place + at, peers, stride=4), :] for at in range(2)]
        parts = jnp.concatenate(split3(rows[0]) + split3(rows[1]), axis=1).astype(BF16)
        product = lax.dot_general(
            chosen, parts, (((1,), (0,)), ((), ())), preferred_element_type=F32
        )
        cuts = [product[:, at * LANES : (at + 1) * LANES] for at in range(6)]
        numer = cuts[0] + cuts[1] + cuts[2] + numer
        denom = cuts[3] + cuts[4] + cuts[5] + denom
    surface[...] = (previous[...] + numer) / (1.0 + denom)


def second_kernel(
    tracers, own_zed, own_core, own_west, own_east, zed, core, east, west, coefficients, _,
    output, result, step_core, step_zed, edge_core, edge_zed, sent,
):
    own, halo = (own_zed, own_core, own_west, own_east), (zed, core, west, east)
    rim = Rim(own, halo, coefficients)
    ends = jnp.concatenate([west[4, 0:4, :], east[4, 0:4, :]], axis=0).T
    lane = lax.broadcasted_iota(jnp.int32, (LEVELS, LANES), 1)
    for place, (steps, edges) in enumerate(((step_zed, edge_zed), (step_core, edge_core))):
        for tracer in range(2):
            at = 2 * place + tracer
            corner = jnp.where(lane == 0, ends[0:LEVELS, at : at + 1], ends[0:LEVELS, at + 4 : at + 5])
            now = slice(tracer * LEVELS, (tracer + 1) * LEVELS)
            before = slice(BEFORE + tracer * LEVELS, BEFORE + (tracer + 1) * LEVELS)
            steps[now, :], edges[now, :] = rim.beyond(place, now, before, corner)
    constant, decaying = coefficients[5], coefficients[6]
    unroll, parts = 4, 4
    decay = [math.exp(-inner_level / 8.0) for inner_level in range(unroll + 1)]

    def pick(refs, tracer, level):
        return [ref[pl.ds(tracer * LEVELS + level, 1), :] for ref in refs]

    def after(tracer, level, here, flow, rate):
        below = inside(tracers, tracer * LEVELS + jnp.minimum(level + 1, LEVELS - 1))
        fall = rate * (below - here)
        steps = pick((step_zed, step_core), tracer, level)
        return rim.after(tracers, tracer, level, steps, here, fall - flow), below, fall

    def step(group, carry):
        now, flow, state, fell, depth = [list(value) for value in carry[:4]] + [carry[4]]
        for inner_level in range(unroll):
            level = group * unroll + inner_level
            later = jnp.minimum(level + 1, LEVELS - 1)
            rate = constant + depth * decay[inner_level]
            rate_below = constant + depth * decay[inner_level + 1]
            for tracer in range(2):
                here = now[tracer]
                below, state[tracer], fell[tracer] = after(
                    tracer, later, state[tracer], fell[tracer], rate_below
                )
                fall = jnp.where(level < LEVELS - 1, rate * (below - here), 0.0)
                edges = pick((edge_zed, edge_core), tracer, level)
                total = rim.lateral(tracer, level, here, edges) + (fall - flow[tracer])
                at = pl.multiple_of((tracer * LEVELS + level) * ROWS, ROWS)
                result[pl.ds(at, ROWS), :] = total
                now[tracer] = below
                flow[tracer] = fall
        return tuple(now), tuple(flow), tuple(state), tuple(fell), depth * decay[unroll]

    starts = [
        after(tracer, 0, inside(tracers, tracer * LEVELS), -coefficients[7 + tracer], constant + decaying)
        for tracer in range(2)
    ]
    now, state, fell = zip(*starts)
    carry = (now, (-coefficients[7], -coefficients[8]), state, fell, decaying)
    groups = LEVELS // unroll // parts
    copies = []
    for part in range(parts):
        carry = lax.fori_loop(part * groups, (part + 1) * groups, step, carry)
        count = groups * unroll * ROWS
        for tracer in range(2):
            at = pl.ds(tracer * LEVELS * ROWS + part * count, count)
            copies.append(
                pltpu.make_async_copy(result.at[at, :], output.at[at, :], sent.at[len(copies)])
            )
            copies[-1].start()
    for copy in copies:
        copy.wait()


def shards(
    atmos_profile_state,
    previous_surface_temp,
    outbound_block_index,
    outbound_slot_counts,
    pair_source_slot,
    overlay_weight,
    ocean_tracer_state,
    ocean_cell_mask,
):
    peers, levs = lax.axis_size("tile"), lax.axis_size("lev")
    slot_total = 2 * peers
    blocks = previous_surface_temp.shape[0] // LANES
    shape = jax.ShapeDtypeStruct
    index = outbound_block_index.T
    slots = pair_source_slot.T
    tracers = ocean_tracer_state.reshape(CELLS * ROWS, LANES)
    prior = previous_surface_temp.reshape(1, -1)
    square = previous_surface_temp.reshape(blocks, LANES)

    staged = (tracers, ocean_cell_mask, slots, index, outbound_slot_counts, square)
    packed, *staged = call(
        flux_kernel,
        (pltpu.VMEM((slot_total, 4, LANES), F32),)
        + (pltpu.VMEM(((CELLS + 2) * ROWS, LANES), F32),)
        + tuple(
            (pltpu.SMEM if value is slots else pltpu.VMEM)(value.shape, value.dtype)
            for value in staged[1:]
        ),
        [AN] * (3 + STAGED),
        [
            pltpu.VMEM((blocks, 4, LANES), F32),
            pltpu.VMEM(atmos_profile_state.shape, BF16),
            pltpu.VMEM(prior.shape, F32),
            pltpu.SMEM(index.shape, jnp.int32),
            pltpu.SemaphoreType.DMA((6,)),
            pltpu.SemaphoreType.DMA((STAGED,)),
        ],
        "flux",
        outs=(VM,) * 3 + (SM,) + (VM,) * (STAGED - 3),
    )(hbm(atmos_profile_state), hbm(prior), hbm(index), *[hbm(value) for value in staged])
    tracers, mask, slots, index, counts, square = staged
    weight = overlay_weight
    slots = pltpu.with_memory_space_constraint(slots, pltpu.SMEM)
    arrived = lax.all_to_all(packed, "tile", split_axis=0, concat_axis=0, tiled=True)

    row_message, column_message = shape((MESSAGE, LANES), F32), shape((5, ROWS, LANES), F32)
    zed, core, coefficients = call(
        first_kernel,
        (
            row_message,
            row_message,
            shape((9, ROWS, LANES), F32),
        ),
        [VM, SM] + [VM] * 3,
        [pltpu.VMEM((ROWS // 2, ROWS, 4 * LANES), F32), pltpu.VMEM((4, ROWS, LANES), F32)],
        "first",
    )(vm(arrived), slots, vm(weight), vm(tracers), vm(mask))
    across = [(i, i + 1) for i in range(1, peers - 1, 2)]
    across += [(target, source) for source, target in across]
    halo_core = vm(lax.ppermute(core, "tile", [(i, i ^ 1) for i in range(peers)]))
    halo_zed = vm(lax.ppermute(zed, "tile", across))
    west, east = call(
        column_kernel,
        (column_message, column_message),
        [VM] * 2,
        (),
        "columns",
    )(vm(tracers), vm(coefficients))
    west, east = call(
        corner_kernel,
        (column_message, column_message),
        [VM] * 4,
        (),
        "corner",
        {2: 0, 3: 1},
    )(halo_zed, halo_core, vm(west), vm(east))
    halo_west = vm(lax.ppermute(east, "lev", [(i, i + 1) for i in range(levs - 1)]))
    halo_east = vm(lax.ppermute(west, "lev", [(i + 1, i) for i in range(levs - 1)]))
    edges = [
        vm(value)
        for value in (
            tracers, zed, core, west, east, halo_zed, halo_core, halo_east, halo_west, coefficients,
        )
    ]
    replies = call(
        reply_kernel,
        shape((slot_total, 2, LANES), F32),
        [VM] * 11 + [SM],
        (),
        "reply",
    )(*edges, vm(weight), slots)
    returned = lax.all_to_all(replies, "tile", split_axis=0, concat_axis=0, tiled=True)
    output = call(
        second_kernel,
        shape((CELLS * ROWS, LANES), F32),
        [VM] * 10 + [AN],
        [pltpu.VMEM((CELLS * ROWS, LANES), F32)]
        + [pltpu.VMEM((CELLS, LANES), F32)] * 4
        + [pltpu.SemaphoreType.DMA((8,))],
        "second",
        outs=AN,
    )(*edges, replies)
    surface = call(
        final_kernel,
        shape((blocks, LANES), F32),
        [VM] * 4,
        (),
        "final",
    )(vm(returned.reshape(2 * slot_total, LANES)), vm(index), vm(counts), vm(square))
    return (output.reshape(ocean_tracer_state.shape), surface.reshape(-1))


def solution(mesh):
    placed = (
        P(None, None, ("sec", "tile", "lev")),
        P(("sec", "tile", "lev")),
        P(("sec", "tile", "lev"), None),
        P(("sec", "tile", "lev"), None),
        P(("sec", "tile", "lev"), None),
        P(("sec", "tile", "lev"), None, None, None),
        P(None, None, ("sec", "tile"), "lev"),
        P(("sec", "tile"), "lev"),
    )
    return jax.shard_map(
        shards,
        mesh=mesh,
        in_specs=placed,
        out_specs=(P(None, None, ("sec", "tile"), "lev"), P(("sec", "tile", "lev"))),
        check_vma=False,
    )
```

```python
import math

import jax
import jax.numpy as jnp
from jax import lax
from jax.experimental import pallas as pl
from jax.experimental.pallas import tpu as pltpu
from jax.sharding import PartitionSpec as P

F32 = jnp.float32
BF16 = jnp.bfloat16
DIFFUSION_RATE = 0.15
LANES = 128
ROWS = 8
LEVELS = 80
MASK_LANE = LEVELS
CELLS = 2 * LEVELS
BEFORE = CELLS
WET = 2 * CELLS
MESSAGE = WET + ROWS
STAGED = 6
VMEM_LIMIT = 16 * 1024 * 1024

VM = pl.BlockSpec(memory_space=pltpu.VMEM)
SM = pl.BlockSpec(memory_space=pltpu.SMEM)
AN = pl.BlockSpec(memory_space=pl.ANY)


def vm(value):
    return pltpu.with_memory_space_constraint(value, pltpu.VMEM)


def hbm(value):
    return pltpu.with_memory_space_constraint(value, pltpu.HBM)


def call(kernel, out_shape, in_specs, scratch=(), name=None, aliases=None, outs=None):
    outs = outs or jax.tree.map(lambda _: VM, out_shape)
    return pl.pallas_call(
        kernel,
        out_shape=out_shape,
        in_specs=in_specs,
        out_specs=outs,
        scratch_shapes=list(scratch),
        name=name,
        input_output_aliases=aliases or {},
        compiler_params=pltpu.CompilerParams(vmem_limit_bytes=VMEM_LIMIT),
    )


def split3(value):
    high = value.astype(BF16).astype(F32)
    rest = value - high
    middle = rest.astype(BF16).astype(F32)
    return high, middle, rest - middle


def iota(axis):
    return lax.broadcasted_iota(jnp.int32, (ROWS, LANES), axis)


def roll(value, shift, axis):
    return pltpu.roll(value, shift, axis)


def flux_kernel(
    atmos_in, previous_in, index_in, *refs,
):
    staged_in, (packed, *staged) = refs[:STAGED], refs[STAGED : 2 * STAGED + 1]
    blocks, atmos, previous, index, arrivals, stage_arrivals = refs[2 * STAGED + 1 :]
    copies = [pltpu.make_async_copy(index_in, index, arrivals.at[0])]
    copies.append(pltpu.make_async_copy(previous_in, previous, arrivals.at[1]))
    for field in range(4):
        copies.append(
            pltpu.make_async_copy(atmos_in.at[field], atmos.at[field], arrivals.at[2 + field])
        )
    for copy in copies:
        copy.start()
    staging = [
        pltpu.make_async_copy(source, target, stage_arrivals.at[at])
        for at, (source, target) in enumerate(zip(staged_in[1:], staged[1:]))
    ]
    inside = staged[0].at[pl.ds(ROWS, CELLS * ROWS), :]
    staging.append(pltpu.make_async_copy(staged_in[0], inside, stage_arrivals.at[STAGED - 1]))
    for copy in staging:
        copy.start()
    levels = atmos.shape[1]
    row = lax.broadcasted_iota(jnp.int32, (ROWS, levels), 0)
    level = lax.broadcasted_iota(jnp.int32, (ROWS, levels), 1).astype(F32)
    bottom_total = sum(math.exp(-l / 3.0) for l in range(levels))
    radiative_total = sum(math.exp(-l / 24.0) for l in range(levels))
    bottom = split3(jnp.exp(-level / 3.0) / bottom_total)
    radiative = split3(jnp.exp(-level / 24.0) / radiative_total)
    table = jnp.zeros((ROWS, levels), F32)
    for at, part in enumerate(bottom + radiative):
        table = jnp.where(row == at, part, table)
    table = table.astype(BF16)

    def sums(field):
        copies[2 + field].wait()
        return lax.dot_general(
            table, atmos[field], (((1,), (0,)), ((), ())), preferred_element_type=F32
        )

    def low(value):
        return value[0:1] + value[1:2] + value[2:3]

    staged[0][0:ROWS, :] = jnp.zeros((ROWS, LANES), F32)
    staged[0][(CELLS + 1) * ROWS :, :] = jnp.zeros((ROWS, LANES), F32)
    copies[0].wait()
    copies[1].wait()
    temperature = sums(0)
    humidity = sums(1)
    radiation = temperature[3:4] + temperature[4:5] + temperature[5:6]
    east = low(sums(2))
    north = low(sums(3))
    speed = jnp.sqrt(east * east + north * north + 1.0)
    prior = previous[...]
    terms = (
        0.3 * speed * (low(temperature) - prior) + 0.5 * radiation,
        0.3 * speed * (jnp.exp(0.2 * prior) - 1.0 - low(humidity)),
        0.1 * speed * east,
        0.1 * speed * north,
    )
    for term, value in enumerate(terms):
        for block in range(blocks.shape[0]):
            blocks[block, term : term + 1, :] = value[:, block * LANES : (block + 1) * LANES]
    for slot in range(packed.shape[0]):
        packed[slot] = blocks[index[slot % 2, slot // 2]]
    for copy in staging:
        copy.wait()


def tile(ref, at):
    return ref[pl.ds(pl.multiple_of(at * ROWS, ROWS), ROWS), :]


def inside(ref, at):
    return ref[pl.ds(pl.multiple_of((at + 1) * ROWS, ROWS), ROWS), :]


def to_first(value, level):
    return roll(value, lax.rem(LANES - level, LANES), 1)


def to_last(value, level):
    return roll(value, LANES - 1 - level, 1)


def edge_rows():
    core_row = (ROWS - 1) * (1 - lax.rem(lax.axis_index("tile"), 2))
    return ROWS - 1 - core_row, core_row


def first_kernel(
    arrived, slots, weight, tracers, mask,
    zed, core, coefficients, picked, forcing,
):
    pairs = weight.shape[1]
    for row in range(ROWS):
        for pair in range(pairs):
            picked[row // 2, 4 * (row % 2) : 4 * (row % 2) + 4, pair * LANES : (pair + 1) * LANES] = (
                arrived[slots[pair, row]]
            )
    for half in range(ROWS // 2):
        left = jnp.concatenate(split3(picked[half]), axis=0).astype(BF16)
        for parity in range(2):
            row = 2 * half + parity
            right = jnp.concatenate([weight[row, pair] for pair in range(pairs)], axis=1)
            product = lax.dot_general(
                left, right, (((1,), (1,)), ((), ())), preferred_element_type=F32
            )
            product = product[0:8] + product[8:16] + product[16:24]
            for term in range(4):
                at = 4 * parity + term
                forcing[term, row : row + 1, :] = product[at : at + 1]
    sub, lane = iota(0), iota(1)
    wet = mask[...].astype(F32)
    inner = (
        DIFFUSION_RATE * jnp.where(sub == 0, 0.0, wet * roll(wet, 1, 0)),
        DIFFUSION_RATE * jnp.where(sub == ROWS - 1, 0.0, wet * roll(wet, ROWS - 1, 0)),
        DIFFUSION_RATE * jnp.where(lane == 0, 0.0, wet * roll(wet, 1, 1)),
        DIFFUSION_RATE * jnp.where(lane == LANES - 1, 0.0, wet * roll(wet, LANES - 1, 1)),
    )
    total_weight = inner[0] + inner[1] + inner[2] + inner[3]
    stress_east, stress_north = forcing[2], forcing[3]
    stress = jnp.sqrt(stress_east * stress_east + stress_north * stress_north)
    constant = 0.05 * wet
    decaying = 0.15 * wet * (stress / (1.0 + stress))
    surface = [0.5 * wet * forcing[0], 0.5 * wet * forcing[1]]
    for at, value in enumerate(inner + (wet, constant, decaying, surface[0], surface[1])):
        coefficients[at] = value
    for target, row in zip((zed, core), edge_rows()):
        inner_rows = [coefficients[at, pl.ds(row, 1), :] for at in range(9)]
        total_row = inner_rows[0] + inner_rows[1] + inner_rows[2] + inner_rows[3]
        decays = jnp.exp(sub.astype(F32) / -8.0)
        for cell in range(0, CELLS, ROWS):
            level = cell % LEVELS
            start = (cell + 1) * ROWS + row

            def rows(skip, start=start):
                return tracers[pl.ds(start + skip, ROWS, stride=ROWS), :]

            here = rows(0)
            slow = (decays * math.exp(-level / 8.0)) * inner_rows[6]
            fall = (inner_rows[5] + slow) * (rows(ROWS) - here)
            flow = (inner_rows[5] + slow * math.exp(1.0 / 8.0)) * (here - rows(-ROWS))
            if level == 0:
                flow = jnp.where(sub == 0, -inner_rows[7 + cell // LEVELS], flow)
            if level == LEVELS - ROWS:
                fall = jnp.where(sub == ROWS - 1, 0.0, fall)
            value = here - total_row * here + (fall - flow)
            value = value + inner_rows[0] * rows(-1) + inner_rows[1] * rows(1)
            value = value + inner_rows[2] * roll(here, 1, 1)
            value = value + inner_rows[3] * roll(here, LANES - 1, 1)
            target[cell : cell + ROWS, :] = value
            target[BEFORE + cell : BEFORE + cell + ROWS, :] = here
        target[WET:MESSAGE, :] = jnp.broadcast_to(inner_rows[4], (ROWS, LANES))


def column_kernel(tracers, coefficients, west, east):
    lane = iota(1)
    inner = [coefficients[at] for at in range(9)]
    wet, constant, decaying = inner[4], inner[5], inner[6]
    total_weight = inner[0] + inner[1] + inner[2] + inner[3]
    unroll = 20

    def step(group, carry):
        kept = list(carry)
        for inner_level in range(unroll):
            level = group * unroll + inner_level
            spots = [lane == lax.rem(level + skip, LANES) for skip in (0, 1, LANES - 1, LANES - 2)]
            for tracer in range(2):
                turned = roll(inside(tracers, tracer * LEVELS + level), level, 1)
                for place, spot in enumerate(spots):
                    at = 2 * place + tracer
                    kept[at] = jnp.where(spot, turned, kept[at])
        return tuple(kept)

    zero = jnp.zeros((ROWS, LANES), F32)
    kept = list(lax.fori_loop(0, LEVELS // unroll, step, (zero,) * 8))
    for tracer in range(2):
        for place, shift in ((1, LANES - 1), (2, 1), (3, 2)):
            kept[2 * place + tracer] = roll(kept[2 * place + tracer], shift, 1)
    decays = jnp.exp(lane.astype(F32) / -8.0)
    for target, end, at_end, at_next, side in ((west, 0, 0, 2, 3), (east, LANES - 1, 4, 6, 2)):
        cut = slice(end, end + 1)
        rate = constant[:, cut] + decays * decaying[:, cut]
        for tracer in range(2):
            column, beside = kept[at_end + tracer], kept[at_next + tracer]
            fall = rate * (roll(column, LANES - 1, 1) - column)
            fall = jnp.where(lane < LEVELS - 1, fall, 0.0)
            flow = jnp.where(lane == 0, -inner[7 + tracer][:, cut], roll(fall, 1, 1))
            total = column - total_weight[:, cut] * column + (fall - flow)
            total = total + inner[0][:, cut] * roll(column, 1, 0)
            total = total + inner[1][:, cut] * roll(column, ROWS - 1, 0)
            target[tracer] = total + inner[side][:, cut] * beside
            target[2 + tracer] = column
        target[2] = jnp.where(lane == MASK_LANE, wet[:, cut], kept[at_end])
        target[4] = zero


def corner_kernel(zed, core, _, __, west, east):
    lane = lax.broadcasted_iota(jnp.int32, (1, LANES), 1)
    padding = jnp.zeros((LANES - LEVELS, LANES), F32)
    for place, source in enumerate((zed, core)):
        for tracer in range(2):
            start = BEFORE + tracer * LEVELS
            turned = jnp.concatenate([source[start : start + LEVELS, :], padding], axis=0).T
            for target, end in ((west, 0), (east, LANES - 1)):
                row = turned[end : end + 1, :]
                if tracer == 0:
                    row = jnp.where(lane == MASK_LANE, source[WET : WET + 1, end : end + 1], row)
                at = 2 * place + tracer
                target[4, at : at + 1, :] = row


class Rim:
    def __init__(self, own, halo, coefficients):
        self.own, self.halo = own[0:2], halo[0:2]
        own_west, own_east, west, east = own[2], own[3], halo[2], halo[3]
        self.west, self.east = west, east
        sub, lane = iota(0), iota(1)
        self.lane = lane[0:1]
        wet = coefficients[4]
        rows = edge_rows()
        self.inner = [coefficients[at] for at in range(4)]
        wet_rows = [ref[WET : WET + 1, :] for ref in self.halo]
        wet_west = to_first(west[2], MASK_LANE)
        wet_east = to_last(east[2], MASK_LANE)
        self.rows = [
            DIFFUSION_RATE * coefficients[4, pl.ds(row, 1), :] * wet_row
            for row, wet_row in zip(rows, wet_rows)
        ]
        column_west = DIFFUSION_RATE * wet * wet_west
        column_east = DIFFUSION_RATE * wet * wet_east
        zero = jnp.zeros((ROWS, LANES), F32)
        self.border = (
            jnp.where(sub == rows[0], self.rows[0], zero),
            jnp.where(sub == rows[1], self.rows[1], zero),
            jnp.where(lane == 0, column_west, zero),
            jnp.where(lane == LANES - 1, column_east, zero),
        )
        self.inner_total = sum(self.inner)
        self.total = self.inner_total + sum(self.border)
        self.step_west = [west[2 + tracer] - own_west[2 + tracer] for tracer in range(2)]
        self.step_east = [east[2 + tracer] - own_east[2 + tracer] for tracer in range(2)]
        self.corner_weight = []
        for place, wet_row in enumerate(wet_rows):
            mask = slice(2 * place, 2 * place + 1), slice(MASK_LANE, MASK_LANE + 1)
            self.corner_weight.append(
                jnp.where(self.lane == 0, DIFFUSION_RATE * wet_row * west[(4,) + mask], 0.0)
                + jnp.where(self.lane == LANES - 1, DIFFUSION_RATE * wet_row * east[(4,) + mask], 0.0)
            )
        self.side_west, self.side_east = [], []
        for side, tiles, wet_side, column, steps in (
            (self.side_west, west, wet_west[:, 0:1], column_west[:, 0:1], self.step_west),
            (
                self.side_east,
                east,
                wet_east[:, LANES - 1 :],
                column_east[:, LANES - 1 :],
                self.step_east,
            ),
        ):
            for tracer in range(2):
                value = tiles[tracer] - column * steps[tracer]
                for place, row in enumerate(rows):
                    diagonal = tiles[4, 2 * place : 2 * place + 1, MASK_LANE : MASK_LANE + 1]
                    corner = tiles[4, 2 * place + tracer : 2 * place + tracer + 1, :]
                    value = value + jnp.where(
                        sub == row,
                        (DIFFUSION_RATE * wet_side * diagonal) * (corner - tiles[2 + tracer]),
                        0.0,
                    )
                side.append(value)

    def beyond(self, place, now, before, corner):
        halo = self.halo[place]
        old = halo[before, :]
        step = old - self.own[place][before, :]
        edge = halo[now, :] - self.rows[place] * step + self.corner_weight[place] * (corner - old)
        return step, edge

    def after(self, tracers, tracer, level, steps, here, vertical):
        at = pl.multiple_of((tracer * LEVELS + level) * ROWS, ROWS)
        value = here - self.inner_total * here + vertical
        value = value + self.inner[0] * tracers[pl.ds(at + ROWS - 1, ROWS), :]
        value = value + self.inner[1] * tracers[pl.ds(at + ROWS + 1, ROWS), :]
        value = value + self.inner[2] * roll(here, 1, 1)
        value = value + self.inner[3] * roll(here, LANES - 1, 1)
        value = value + self.border[0] * steps[0] + self.border[1] * steps[1]
        value = value + self.border[2] * to_first(self.step_west[tracer], level)
        return value + self.border[3] * to_last(self.step_east[tracer], level)

    def lateral(self, tracer, level, here, edges):
        value = here - self.total * here
        value = value + self.border[0] * edges[0] + self.border[1] * edges[1]
        value = value + self.border[2] * to_first(self.side_west[tracer], level)
        value = value + self.border[3] * to_last(self.side_east[tracer], level)
        value = value + self.inner[0] * roll(here, 1, 0)
        value = value + self.inner[1] * roll(here, ROWS - 1, 0)
        value = value + self.inner[2] * roll(here, 1, 1)
        return value + self.inner[3] * roll(here, LANES - 1, 1)


def reply_kernel(
    tracers, own_zed, own_core, own_west, own_east, zed, core, east, west, coefficients,
    weight, slots, replies,
):
    pairs = weight.shape[1]
    own, halo = (own_zed, own_core, own_west, own_east), (zed, core, west, east)
    rim = Rim(own, halo, coefficients)
    steps, edges = [], []
    for place in range(2):
        row = slice(2 * place, 2 * place + 1)
        corner = jnp.where(rim.lane == 0, west[4, row, 0:1], east[4, row, 0:1])
        step, edge = rim.beyond(place, slice(0, 1), slice(BEFORE, BEFORE + 1), corner)
        steps.append(step)
        edges.append(edge)
    below = slice(BEFORE + 1, BEFORE + 2)
    first, second, third = [inside(tracers, level) for level in range(3)]
    rate = coefficients[5] + coefficients[6]
    rate_below = coefficients[5] + coefficients[6] * math.exp(-1.0 / 8.0)
    flow = rate * (second - first)
    here = rim.after(tracers, 0, 0, steps, first, flow + coefficients[7])
    steps = [rim.halo[at][below, :] - rim.own[at][below, :] for at in range(2)]
    later = rim.after(tracers, 0, 1, steps, second, rate_below * (third - second) - flow)
    fall = rate * (later - here)
    surface = rim.lateral(0, 0, here, edges) + (fall + coefficients[7])
    left = jnp.concatenate(split3(surface) + (jnp.ones((ROWS, LANES), F32),), axis=0).astype(BF16)
    replies[...] = jnp.zeros_like(replies)
    for row in range(ROWS):
        right = jnp.concatenate([weight[row, pair] for pair in range(pairs)], axis=1)
        product = lax.dot_general(left, right, (((1,), (0,)), ((), ())), preferred_element_type=F32)
        numer = product[row : row + 1] + product[8 + row : 9 + row] + product[16 + row : 17 + row]
        denom = product[24:25]
        both = jnp.concatenate([numer, denom], axis=0)
        for pair in range(pairs):
            slot = slots[pair, row]
            replies[slot] = replies[slot] + both[:, pair * LANES : (pair + 1) * LANES]


def final_kernel(
    returned, index, counts, previous, surface,
):
    blocks = previous.shape[0]
    peers = counts.shape[1]
    block = lax.broadcasted_iota(jnp.int32, (blocks, peers), 0)
    numer, denom = 0.0, 0.0
    for place in range(2):
        chosen = (block == index[place : place + 1, :]) & (place < counts[...])
        chosen = chosen.astype(F32).astype(BF16)
        rows = [returned[pl.ds(2 * place + at, peers, stride=4), :] for at in range(2)]
        parts = jnp.concatenate(split3(rows[0]) + split3(rows[1]), axis=1).astype(BF16)
        product = lax.dot_general(
            chosen, parts, (((1,), (0,)), ((), ())), preferred_element_type=F32
        )
        cuts = [product[:, at * LANES : (at + 1) * LANES] for at in range(6)]
        numer = cuts[0] + cuts[1] + cuts[2] + numer
        denom = cuts[3] + cuts[4] + cuts[5] + denom
    surface[...] = (previous[...] + numer) / (1.0 + denom)


def second_kernel(
    tracers, own_zed, own_core, own_west, own_east, zed, core, east, west, coefficients, _,
    output, result, step_core, step_zed, edge_core, edge_zed, sent,
):
    own, halo = (own_zed, own_core, own_west, own_east), (zed, core, west, east)
    rim = Rim(own, halo, coefficients)
    ends = jnp.concatenate([west[4, 0:4, :], east[4, 0:4, :]], axis=0).T
    lane = lax.broadcasted_iota(jnp.int32, (LEVELS, LANES), 1)
    for place, (steps, edges) in enumerate(((step_zed, edge_zed), (step_core, edge_core))):
        for tracer in range(2):
            at = 2 * place + tracer
            corner = jnp.where(lane == 0, ends[0:LEVELS, at : at + 1], ends[0:LEVELS, at + 4 : at + 5])
            now = slice(tracer * LEVELS, (tracer + 1) * LEVELS)
            before = slice(BEFORE + tracer * LEVELS, BEFORE + (tracer + 1) * LEVELS)
            steps[now, :], edges[now, :] = rim.beyond(place, now, before, corner)
    constant, decaying = coefficients[5], coefficients[6]
    unroll, parts = 4, 4
    decay = [math.exp(-inner_level / 8.0) for inner_level in range(unroll + 1)]

    def pick(refs, tracer, level):
        return [ref[pl.ds(tracer * LEVELS + level, 1), :] for ref in refs]

    def after(tracer, level, here, flow, rate):
        below = inside(tracers, tracer * LEVELS + jnp.minimum(level + 1, LEVELS - 1))
        fall = rate * (below - here)
        steps = pick((step_zed, step_core), tracer, level)
        return rim.after(tracers, tracer, level, steps, here, fall - flow), below, fall

    def step(group, carry):
        now, flow, state, fell, depth = [list(value) for value in carry[:4]] + [carry[4]]
        for inner_level in range(unroll):
            level = group * unroll + inner_level
            later = jnp.minimum(level + 1, LEVELS - 1)
            rate = constant + depth * decay[inner_level]
            rate_below = constant + depth * decay[inner_level + 1]
            for tracer in range(2):
                here = now[tracer]
                below, state[tracer], fell[tracer] = after(
                    tracer, later, state[tracer], fell[tracer], rate_below
                )
                fall = jnp.where(level < LEVELS - 1, rate * (below - here), 0.0)
                edges = pick((edge_zed, edge_core), tracer, level)
                total = rim.lateral(tracer, level, here, edges) + (fall - flow[tracer])
                at = pl.multiple_of((tracer * LEVELS + level) * ROWS, ROWS)
                result[pl.ds(at, ROWS), :] = total
                now[tracer] = below
                flow[tracer] = fall
        return tuple(now), tuple(flow), tuple(state), tuple(fell), depth * decay[unroll]

    starts = [
        after(tracer, 0, inside(tracers, tracer * LEVELS), -coefficients[7 + tracer], constant + decaying)
        for tracer in range(2)
    ]
    now, state, fell = zip(*starts)
    carry = (now, (-coefficients[7], -coefficients[8]), state, fell, decaying)
    groups = LEVELS // unroll // parts
    copies = []
    for part in range(parts):
        carry = lax.fori_loop(part * groups, (part + 1) * groups, step, carry)
        count = groups * unroll * ROWS
        for tracer in range(2):
            at = pl.ds(tracer * LEVELS * ROWS + part * count, count)
            copies.append(
                pltpu.make_async_copy(result.at[at, :], output.at[at, :], sent.at[len(copies)])
            )
            copies[-1].start()
    for copy in copies:
        copy.wait()


def shards(
    atmos_profile_state,
    previous_surface_temp,
    outbound_block_index,
    outbound_slot_counts,
    pair_source_slot,
    overlay_weight,
    ocean_tracer_state,
    ocean_cell_mask,
):
    peers, levs = lax.axis_size("tile"), lax.axis_size("lev")
    slot_total = 2 * peers
    blocks = previous_surface_temp.shape[0] // LANES
    shape = jax.ShapeDtypeStruct
    index = outbound_block_index.T
    slots = pair_source_slot.T
    tracers = ocean_tracer_state.reshape(CELLS * ROWS, LANES)
    prior = previous_surface_temp.reshape(1, -1)
    square = previous_surface_temp.reshape(blocks, LANES)

    staged = (tracers, ocean_cell_mask, slots, index, outbound_slot_counts, square)
    packed, *staged = call(
        flux_kernel,
        (pltpu.VMEM((slot_total, 4, LANES), F32),)
        + (pltpu.VMEM(((CELLS + 2) * ROWS, LANES), F32),)
        + tuple(
            (pltpu.SMEM if value is slots else pltpu.VMEM)(value.shape, value.dtype)
            for value in staged[1:]
        ),
        [AN] * (3 + STAGED),
        [
            pltpu.VMEM((blocks, 4, LANES), F32),
            pltpu.VMEM(atmos_profile_state.shape, BF16),
            pltpu.VMEM(prior.shape, F32),
            pltpu.SMEM(index.shape, jnp.int32),
            pltpu.SemaphoreType.DMA((6,)),
            pltpu.SemaphoreType.DMA((STAGED,)),
        ],
        "flux",
        outs=(VM,) * 3 + (SM,) + (VM,) * (STAGED - 3),
    )(hbm(atmos_profile_state), hbm(prior), hbm(index), *[hbm(value) for value in staged])
    tracers, mask, slots, index, counts, square = staged
    weight = overlay_weight
    slots = pltpu.with_memory_space_constraint(slots, pltpu.SMEM)
    arrived = lax.all_to_all(packed, "tile", split_axis=0, concat_axis=0, tiled=True)

    row_message, column_message = shape((MESSAGE, LANES), F32), shape((5, ROWS, LANES), F32)
    zed, core, coefficients = call(
        first_kernel,
        (
            row_message,
            row_message,
            shape((9, ROWS, LANES), F32),
        ),
        [VM, SM] + [VM] * 3,
        [pltpu.VMEM((ROWS // 2, ROWS, 4 * LANES), F32), pltpu.VMEM((4, ROWS, LANES), F32)],
        "first",
    )(vm(arrived), slots, vm(weight), vm(tracers), vm(mask))
    across = [(i, i + 1) for i in range(1, peers - 1, 2)]
    across += [(target, source) for source, target in across]
    halo_core = vm(lax.ppermute(core, "tile", [(i, i ^ 1) for i in range(peers)]))
    halo_zed = vm(lax.ppermute(zed, "tile", across))
    west, east = call(
        column_kernel,
        (column_message, column_message),
        [VM] * 2,
        (),
        "columns",
    )(vm(tracers), vm(coefficients))
    west, east = call(
        corner_kernel,
        (column_message, column_message),
        [VM] * 4,
        (),
        "corner",
        {2: 0, 3: 1},
    )(halo_zed, halo_core, vm(west), vm(east))
    halo_west = vm(lax.ppermute(east, "lev", [(i, i + 1) for i in range(levs - 1)]))
    halo_east = vm(lax.ppermute(west, "lev", [(i + 1, i) for i in range(levs - 1)]))
    edges = [
        vm(value)
        for value in (
            tracers, zed, core, west, east, halo_zed, halo_core, halo_east, halo_west, coefficients,
        )
    ]
    replies = call(
        reply_kernel,
        shape((slot_total, 2, LANES), F32),
        [VM] * 11 + [SM],
        (),
        "reply",
    )(*edges, vm(weight), slots)
    returned = lax.all_to_all(replies, "tile", split_axis=0, concat_axis=0, tiled=True)
    output = call(
        second_kernel,
        shape((CELLS * ROWS, LANES), F32),
        [VM] * 10 + [AN],
        [pltpu.VMEM((CELLS * ROWS, LANES), F32)]
        + [pltpu.VMEM((CELLS, LANES), F32)] * 4
        + [pltpu.SemaphoreType.DMA((8,))],
        "second",
        outs=AN,
    )(*edges, replies)
    surface = call(
        final_kernel,
        shape((blocks, LANES), F32),
        [VM] * 4,
        (),
        "final",
    )(vm(returned.reshape(2 * slot_total, LANES)), vm(index), vm(counts), vm(square))
    return (output.reshape(ocean_tracer_state.shape), surface.reshape(-1))


def solution(mesh):
    placed = (
        P(None, None, ("sec", "tile", "lev")),
        P(("sec", "tile", "lev")),
        P(("sec", "tile", "lev"), None),
        P(("sec", "tile", "lev"), None),
        P(("sec", "tile", "lev"), None),
        P(("sec", "tile", "lev"), None, None, None),
        P(None, None, ("sec", "tile"), "lev"),
        P(("sec", "tile"), "lev"),
    )
    return jax.shard_map(
        shards,
        mesh=mesh,
        in_specs=placed,
        out_specs=(P(None, None, ("sec", "tile"), "lev"), P(("sec", "tile", "lev"))),
        check_vma=False,
    )
```
